32 devices in a mesh: dp: 16 (over z, x, core), seq: 2 (over y).
Axes of the slice: x: 2, y: 2, z: 4, core: 2. Of those that a mesh axis runs over, the one named last changes fastest.
Arguments:
- pixels_a: bfloat16 [16, 24, 24, 300], P('dp', 'seq'), may hold values from -6 to 6
- pixels_b: bfloat16 [64, 32, 32, 432], P('dp', 'seq'), may hold values from -6 to 6
- labels_a: int32 [16], P('dp'), may hold values from 0 to 999
- labels_b: int32 [64], P('dp'), may hold values from 0 to 999
- live_a: int32 [16], P('dp'), may hold values 0 or 1
- live_b: int32 [64], P('dp'), may hold values 0 or 1
- qkv_w: float32 [768, 2304], P(('dp', 'seq')), may hold values from -0.21875 to 0.21875
- out_w: float32 [768, 768], P(('dp', 'seq')), may hold values from -3 to 3
- mlp_w: float32 [2, 768, 3072], P(None, ('dp', 'seq')), may hold values from -0.21875 to 0.21875
- kern_w: float32 [3072, 768], P(('dp', 'seq')), may hold values from -0.5 to 0.5
- pos_w: float32 [49, 768], P(None, ('dp', 'seq')), may hold values from -3 to 3
- head_w: float32 [768, 1000], P(('dp', 'seq')), may hold values from -0.875 to 0.875
- gains: float32 [2, 768], P(None, ('dp', 'seq')), may hold values from 0.25 to 3.2
- qkv_m: float32 [768, 2304], P(('dp', 'seq')), may hold values from -4.7683716e-07 to 4.7683716e-07
- out_m: float32 [768, 768], P(('dp', 'seq')), may hold values from -1.4901161e-07 to 1.4901161e-07
- mlp_m: float32 [2, 768, 3072], P(None, ('dp', 'seq')), may hold values from -4.7683716e-07 to 4.7683716e-07
- kern_m: float32 [3072, 768], P(('dp', 'seq')), may hold values from -4.7683716e-07 to 4.7683716e-07
- pos_m: float32 [49, 768], P(None, ('dp', 'seq')), may hold values from -4.7683716e-07 to 4.7683716e-07
- head_m: float32 [768, 1000], P(('dp', 'seq')), may hold values from -4.7683716e-07 to 4.7683716e-07
- gains_m: float32 [2, 768], P(None, ('dp', 'seq')), may hold values from -2.3841858e-06 to 2.3841858e-06
- qkv_v: float32 [768, 2304], P(('dp', 'seq')), may hold values from 9.7614764e-17 to 3.9045905e-16
- out_v: float32 [768, 768], P(('dp', 'seq')), may hold values from 5.856886e-18 to 2.3427543e-17
- mlp_v: float32 [2, 768, 3072], P(None, ('dp', 'seq')), may hold values from 9.7614764e-17 to 3.9045905e-16
- kern_v: float32 [3072, 768], P(('dp', 'seq')), may hold values from 9.7614764e-17 to 3.9045905e-16
- pos_v: float32 [49, 768], P(None, ('dp', 'seq')), may hold values from 9.7614764e-17 to 3.9045905e-16
- head_v: float32 [768, 1000], P(('dp', 'seq')), may hold values from 9.7614764e-17 to 3.9045905e-16
- gains_v: float32 [2, 768], P(None, ('dp', 'seq')), may hold values from 2.440369e-15 to 9.761476e-15
Outputs:
- qkv_new: float32 [768, 2304], P(('dp', 'seq'))
- out_new: float32 [768, 768], P(('dp', 'seq'))
- mlp_new: float32 [2, 768, 3072], P(None, ('dp', 'seq'))
- kern_new: float32 [3072, 768], P(('dp', 'seq'))
- pos_new: float32 [49, 768], P(None, ('dp', 'seq'))
- head_new: float32 [768, 1000], P(('dp', 'seq'))
- gains_new: float32 [2, 768], P(None, ('dp', 'seq'))
- qkv_m_new: float32 [768, 2304], P(('dp', 'seq'))
- out_m_new: float32 [768, 768], P(('dp', 'seq'))
- mlp_m_new: float32 [2, 768, 3072], P(None, ('dp', 'seq'))
- kern_m_new: float32 [3072, 768], P(('dp', 'seq'))
- pos_m_new: float32 [49, 768], P(None, ('dp', 'seq'))
- head_m_new: float32 [768, 1000], P(('dp', 'seq'))
- gains_m_new: float32 [2, 768], P(None, ('dp', 'seq'))
- qkv_v_new: float32 [768, 2304], P(('dp', 'seq'))
- out_v_new: float32 [768, 768], P(('dp', 'seq'))
- mlp_v_new: float32 [2, 768, 3072], P(None, ('dp', 'seq'))
- kern_v_new: float32 [3072, 768], P(('dp', 'seq'))
- pos_v_new: float32 [49, 768], P(None, ('dp', 'seq'))
- head_v_new: float32 [768, 1000], P(('dp', 'seq'))
- gains_v_new: float32 [2, 768], P(None, ('dp', 'seq'))
- size_stats: float32 [2], replicated
- grad_norm: float32 [], replicated
The draws below stay inside these ranges and needn't reach their ends.
All inputs are finite; a program needn't handle non-finite values. No bound on the sum of `live_a` or of `live_b` on one device may be relied on, other than what follows from the above.
Results may differ from the reference program's by a relative error of at most 0.019.
Values may be sent and summed in bfloat16 or wider, within the bound.
No kernel may reach another device: no remote copies, remote signals or barrier semaphores. Data moves between devices by JAX's collectives and lax.ppermute only.
A program may use at most 576 MiB of HBM per device.

```python
import math
import jax
import jax.numpy as jnp
from jax import lax

D = 768
HEADS = 12
HEAD_DIM = 64
MLP = 3072
CLASSES = 1000
BASE = 32
PATCH_A = 10
PATCH_B = 12
GA = 24
GB = 32
IMAGES_A = 16
IMAGES_B = 64
PARAMS = 10244352


def draw_gains(key, part):
    place = jnp.arange(D, dtype=jnp.float32) / float(D - 1)
    ramp = 0.5 * 4.0 ** place
    noise = jax.random.uniform(key, (2, D), jnp.float32, 0.85, 1.15)
    return (ramp[None, :] * noise).astype(jnp.float32)


def place_ends(drawn, key, smallest, high):
    extent = drawn.shape
    spot = [jax.random.randint(jax.random.fold_in(key, axis), (), 0, extent[axis]) for axis in range(len(extent))]
    drawn = drawn.at[tuple(spot)].set(smallest)
    longest = extent.index(max(extent))
    spot[longest] = (spot[longest] + 1) % extent[longest]
    return drawn.at[tuple(spot)].set(high)


def block_scale(own_key, shape, cuts, smallest, largest):
    def one(axis_at, shards_of):
        steps = jax.random.uniform(jax.random.fold_in(jax.random.fold_in(own_key, 6), axis_at), (shards_of,), jnp.float32, smallest / len(cuts), largest / len(cuts))
        return jnp.repeat(jnp.exp(steps), shape[axis_at] // shards_of).reshape((-1,) + (1,) * (len(shape) - axis_at - 1))

    factor_of = one(*cuts[0])
    for cut in cuts[1:]:
        factor_of = factor_of * one(*cut)
    return factor_of


def gaussian(stream_key, extent, deviation, limit, split=(), kind=jnp.bfloat16):
    factor_of = block_scale(stream_key, extent, split, -0.22, 0.18) if split else 1.0
    entries = jax.random.normal(stream_key, extent, jnp.float32) * deviation * factor_of
    return jnp.minimum(jnp.maximum(entries, -limit), limit).astype(kind)


def setup_inputs(seed: int = 0) -> dict:
    seeds = jax.random.split(jax.random.key(seed), 28)
    return {
        "pixels_a": gaussian(seeds[0], (IMAGES_A, GA, GA, 3 * PATCH_A * PATCH_A), 1.0, 6.0, ((0, 16), (1, 2))),
        "pixels_b": gaussian(seeds[1], (IMAGES_B, GB, GB, 3 * PATCH_B * PATCH_B), 1.0, 6.0, ((0, 16), (1, 2))),
        "labels_a": place_ends(jax.random.randint(seeds[2], (IMAGES_A,), 0, CLASSES), jax.random.fold_in(seeds[2], 1), 0, CLASSES - 1).astype(jnp.int32),
        "labels_b": place_ends(jax.random.randint(seeds[3], (IMAGES_B,), 0, CLASSES), jax.random.fold_in(seeds[3], 1), 0, CLASSES - 1).astype(jnp.int32),
        "live_a": place_ends((jax.random.randint(seeds[4], (IMAGES_A,), 0, 4) < 3).astype(jnp.int32), jax.random.fold_in(seeds[4], 1), 0, 1),
        "live_b": place_ends((jax.random.randint(seeds[5], (IMAGES_B,), 0, 4) < 3).astype(jnp.int32), jax.random.fold_in(seeds[5], 1), 0, 1),
        "qkv_w": gaussian(seeds[6], (D, 3 * HEADS * HEAD_DIM), D ** -0.5, 0.21875, ((0, 32),), jnp.float32),
        "out_w": gaussian(seeds[7], (HEADS * HEAD_DIM, D), (HEADS * HEAD_DIM // 192) ** -0.5, 3.0, ((0, 32),), jnp.float32),
        "mlp_w": gaussian(seeds[8], (2, D, MLP), D ** -0.5, 0.21875, ((1, 32),), jnp.float32),
        "kern_w": gaussian(seeds[9], (3 * BASE * BASE, D), (4 * BASE) ** -0.5, 0.5, ((0, 32),), jnp.float32),
        "pos_w": gaussian(seeds[10], (49, D), 0.5, 3.0, ((1, 32),), jnp.float32),
        "head_w": gaussian(seeds[11], (D, CLASSES), (D // 16) ** -0.5, 0.875, ((0, 32),), jnp.float32),
        "gains": draw_gains(jax.random.fold_in(seeds[27], 71), 0),
        "qkv_m": gaussian(seeds[13], (D, 3 * HEADS * HEAD_DIM), (0.00011 / PARAMS ** 0.5), 4.76837158203125e-07, ((0, 32),), jnp.float32),
        "out_m": gaussian(seeds[14], (HEADS * HEAD_DIM, D), (0.00003 / PARAMS ** 0.5), 1.4901161193847656e-07, ((0, 32),), jnp.float32),
        "mlp_m": gaussian(seeds[15], (2, D, MLP), (0.00011 / PARAMS ** 0.5), 4.76837158203125e-07, ((1, 32),), jnp.float32),
        "kern_m": gaussian(seeds[16], (3 * BASE * BASE, D), (0.00011 / PARAMS ** 0.5), 4.76837158203125e-07, ((0, 32),), jnp.float32),
        "pos_m": gaussian(seeds[17], (49, D), (0.00011 / PARAMS ** 0.5), 4.76837158203125e-07, ((1, 32),), jnp.float32),
        "head_m": gaussian(seeds[18], (D, CLASSES), (0.00011 / PARAMS ** 0.5), 4.76837158203125e-07, ((0, 32),), jnp.float32),
        "gains_m": gaussian(seeds[19], (2, D), (0.00055 / PARAMS ** 0.5), 2.384185791015625e-06, ((1, 32),), jnp.float32),
        "qkv_v": jnp.clip(jnp.exp(math.log(3.9045905409686057e-16) - 1.3862944 * jax.random.uniform(seeds[20], (D, 3 * HEADS * HEAD_DIM), jnp.float32) ** block_scale(seeds[20], (D, 3 * HEADS * HEAD_DIM), ((0, 32),), -0.2, 0.2)), 9.761476352421514e-17, 3.9045905409686057e-16),
        "out_v": jnp.clip(jnp.exp(math.log(2.3427543311986083e-17) - 1.3862944 * jax.random.uniform(seeds[21], (HEADS * HEAD_DIM, D), jnp.float32) ** block_scale(seeds[21], (HEADS * HEAD_DIM, D), ((0, 32),), -0.2, 0.2)), 5.856885827996521e-18, 2.3427543311986083e-17),
        "mlp_v": jnp.clip(jnp.exp(math.log(3.9045905409686057e-16) - 1.3862944 * jax.random.uniform(seeds[22], (2, D, MLP), jnp.float32) ** block_scale(seeds[22], (2, D, MLP), ((1, 32),), -0.2, 0.2)), 9.761476352421514e-17, 3.9045905409686057e-16),
        "kern_v": jnp.clip(jnp.exp(math.log(3.9045905409686057e-16) - 1.3862944 * jax.random.uniform(seeds[23], (3 * BASE * BASE, D), jnp.float32) ** block_scale(seeds[23], (3 * BASE * BASE, D), ((0, 32),), -0.2, 0.2)), 9.761476352421514e-17, 3.9045905409686057e-16),
        "pos_v": jnp.clip(jnp.exp(math.log(3.9045905409686057e-16) - 1.3862944 * jax.random.uniform(seeds[24], (49, D), jnp.float32) ** block_scale(seeds[24], (49, D), ((1, 32),), -0.2, 0.2)), 9.761476352421514e-17, 3.9045905409686057e-16),
        "head_v": jnp.clip(jnp.exp(math.log(3.9045905409686057e-16) - 1.3862944 * jax.random.uniform(seeds[25], (D, CLASSES), jnp.float32) ** block_scale(seeds[25], (D, CLASSES), ((0, 32),), -0.2, 0.2)), 9.761476352421514e-17, 3.9045905409686057e-16),
        "gains_v": jnp.clip(jnp.exp(math.log(9.761476193602837e-15) - 1.3862944 * jax.random.uniform(seeds[26], (2, D), jnp.float32) ** block_scale(seeds[26], (2, D), ((1, 32),), -0.2, 0.2)), 2.440369048400709e-15, 9.761476193602837e-15),
    }


@jax.custom_vjp
def low(v):
    return lax.optimization_barrier(v.astype(jnp.bfloat16)).astype(jnp.float32)

@jax.custom_vjp
def low_back(v):
    return v

def low_keep(v):
    return (low(v), None)

def low_pass(kept, grad):
    return (grad,)

def back_keep(v):
    return (v, None)

def back_low(kept, grad):
    return (low(grad),)
low.defvjp(low_keep, low_pass)
low_back.defvjp(back_keep, back_low)
HIGH = lax.Precision.HIGHEST
RATES = (0.012, 0.2, 0.012, 0.03, 0.15, 0.06, 0.25)
CLIP = 0.001

def interp_matrix(n_out, n_in):
    places = jnp.arange(n_out, dtype=jnp.float32) * ((n_in - 1) / (n_out - 1))
    return jnp.maximum(0.0, 1.0 - jnp.abs(places[:, None] - jnp.arange(n_in, dtype=jnp.float32)[None, :]))

def pinv_table(patch):
    basis = interp_matrix(patch, BASE)
    gram = jnp.dot(basis, basis.T, precision=HIGH)
    factor = jnp.linalg.cholesky(gram)
    return jax.scipy.linalg.cho_solve((factor, True), basis)

def layer_norm(values, gain):
    centred = values - lax.optimization_barrier(jnp.mean(values, -1, keepdims=True))
    spread = lax.optimization_barrier(jnp.mean(centred * centred, -1, keepdims=True))
    return centred * lax.rsqrt(spread + 1e-06) * gain

def kernel_resize(kernel, patch):
    table = pinv_table(patch)
    shaped = kernel.reshape(3, BASE, BASE, -1)
    return jnp.einsum('ia,jb,cabd->cijd', table, table, shaped, precision=HIGH).reshape(3 * patch * patch, -1)

def grid_resize(position, row_table, grid):
    table = interp_matrix(grid, 7)
    return jnp.einsum('ia,jb,abd->ijd', row_table, table, position.reshape(7, 7, -1), precision=HIGH)

def adamw(weight, first, second, grad, rate):
    first = 0.9 * first + 0.1 * grad
    second = 0.999 * second + 0.001 * grad * grad
    step_dir = first / (1.0 - 0.9 ** 3) / (jnp.sqrt(second / (1.0 - 0.999 ** 3)) + 1e-08)
    return (weight - rate * (step_dir + 0.1 * weight), first, second)

def image_terms(pixel, label, weights, patch):
    qkv_w, out_w, mlp_w, kern, pos_w, head_w, gains = weights
    grid = pixel.shape[0]
    tokens = pixel.reshape(grid * grid, -1).astype(jnp.float32)
    embed = low_back(jnp.dot(tokens, low(kernel_resize(kern, patch)), precision=HIGH))
    x0 = embed + grid_resize(pos_w, interp_matrix(grid, 7), grid).reshape(grid * grid, -1)
    h1 = low(layer_norm(x0, gains[0]))
    qkv = low(low_back(jnp.dot(h1, qkv_w, precision=HIGH))).reshape(grid * grid, 3, HEADS, HEAD_DIM)
    scores = low_back(jnp.einsum('the,she->hts', qkv[:, 0], qkv[:, 1], precision=HIGH) * HEAD_DIM ** (-0.5))
    probs = low(jax.nn.softmax(scores, axis=-1))
    mixed = jnp.einsum('hts,she->the', probs, qkv[:, 2], precision=HIGH).reshape(grid * grid, -1)
    x1 = x0 + low_back(jnp.dot(low(low_back(mixed)), out_w, precision=HIGH))
    h2 = low(layer_norm(x1, gains[1]))
    inner = low_back(jnp.dot(h2, mlp_w[0], precision=HIGH))
    act = low(jax.nn.gelu(inner, approximate=False))
    x2 = x1 + low_back(jnp.dot(act, mlp_w[1].T, precision=HIGH))
    pooled = lax.optimization_barrier(jnp.mean(x2, axis=0))
    logits = low_back(jnp.dot(low(pooled), head_w, precision=HIGH))
    norm_log = jax.nn.logsumexp(logits)
    true_logit = jnp.sum(jnp.where(jnp.arange(logits.shape[0]) == label, logits, 0.0))
    return norm_log - true_logit

def run_size(pixels, labels, live, weights, patch):

    def one_image(carry, item):
        pixel, label, alive = item
        loss = image_terms(pixel, label, weights, patch)
        return (carry + alive.astype(jnp.float32) * loss, None)
    sums, _ = lax.scan(jax.checkpoint(one_image), jnp.zeros((), jnp.float32), (pixels, labels, live))
    return sums

def reference(pixels_a, pixels_b, labels_a, labels_b, live_a, live_b, qkv_w, out_w, mlp_w, kern_w, pos_w, head_w, gains, qkv_m, out_m, mlp_m, kern_m, pos_m, head_m, gains_m, qkv_v, out_v, mlp_v, kern_v, pos_v, head_v, gains_v):
    params = (qkv_w, out_w, mlp_w, kern_w, pos_w, head_w, gains)
    firsts = (qkv_m, out_m, mlp_m, kern_m, pos_m, head_m, gains_m)
    seconds = (qkv_v, out_v, mlp_v, kern_v, pos_v, head_v, gains_v)
    count_a = jnp.sum(live_a).astype(jnp.float32)
    count_b = jnp.sum(live_b).astype(jnp.float32)
    total = jnp.maximum(count_a + count_b, 1.0)

    def loss_fn(*weights):
        rounded = tuple((low(w) for w in weights))
        sums_a = run_size(pixels_a, labels_a, live_a, rounded, PATCH_A)
        sums_b = run_size(pixels_b, labels_b, live_b, rounded, PATCH_B)
        return ((sums_a + sums_b) / total, (sums_a, sums_b))
    loss, pullback, aux = jax.vjp(loss_fn, *params, has_aux=True)
    grads = pullback(jnp.ones_like(loss))
    grad_norm = jnp.sqrt(sum((jnp.sum(g * g) for g in grads)))
    factor = jnp.minimum(1.0, CLIP / (grad_norm + 1e-06))
    done = [adamw(params[i], firsts[i], seconds[i], grads[i] * factor, RATES[i]) for i in range(7)]
    size_stats = jnp.stack([aux[0] / jnp.maximum(count_a, 1.0), aux[1] / jnp.maximum(count_b, 1.0)])
    return (done[0][0], done[1][0], done[2][0], done[3][0], done[4][0], done[5][0], done[6][0], done[0][1], done[1][1], done[2][1], done[3][1], done[4][1], done[5][1], done[6][1], done[0][2], done[1][2], done[2][2], done[3][2], done[4][2], done[5][2], done[6][2], size_stats, grad_norm)
```

```python
from functools import partial

import jax
import jax.numpy as jnp
import ml_dtypes
import numpy as np
from jax import lax
from jax.experimental import pallas as pl
from jax.experimental.pallas import tpu as pltpu
from jax.sharding import PartitionSpec as P

HEADS = 12
HEAD_DIM = 64
BASE = 32
PATCH_A = 10
PATCH_B = 12


HIGH = lax.Precision.HIGHEST
RATES = (0.012, 0.2, 0.012, 0.03, 0.15, 0.06, 0.25)
CLIP = 0.001
ROWS_DIM = (((0,), (0,)), ((), ()))
COLS_DIM = (((1,), (1,)), ((), ()))


def from_behind(value, axis, steps):
    count = lax.axis_size(axis)
    pairs = [(source, (source + steps) % count) for source in range(count)]
    return lax.ppermute(value, axis, pairs)


def interp_matrix(n_out, n_in):
    places = jnp.arange(n_out, dtype=jnp.float32) * ((n_in - 1) / (n_out - 1))
    return jnp.maximum(
        0.0, 1.0 - jnp.abs(places[:, None] - jnp.arange(n_in, dtype=jnp.float32)[None, :])
    )


def pinv_table(patch):
    basis = interp_matrix(patch, BASE)
    gram = jnp.dot(basis, basis.T, precision=HIGH)
    factor = jnp.linalg.cholesky(gram)
    return jax.scipy.linalg.cho_solve((factor, True), basis)


def layer_norm(values, gain):
    centred = values - jnp.mean(values, -1, keepdims=True)
    spread = jnp.mean(centred * centred, -1, keepdims=True)
    return centred * lax.rsqrt(spread + 1e-06) * gain


def kernel_resize(kernel, patch):
    table = pinv_table(patch)
    shaped = kernel.reshape(3, BASE, BASE, -1)
    return jnp.einsum("ia,jb,cabd->cijd", table, table, shaped, precision=HIGH).reshape(
        3 * patch * patch, -1
    )


def grid_resize(position, row_table, grid):
    table = interp_matrix(grid, 7)
    return jnp.einsum(
        "ia,jb,abd->ijd", row_table, table, position.reshape(7, 7, -1), precision=HIGH
    )


def adamw(weight, first, second, grad, rate):
    first = 0.9 * first + 0.1 * grad
    second = 0.999 * second + 0.001 * grad * grad
    step_dir = first / (1.0 - 0.9**3) / (jnp.sqrt(second / (1.0 - 0.999**3)) + 1e-08)
    return (weight - rate * (step_dir + 0.1 * weight), first, second)


def attend(query, keys, values):
    scores = jnp.einsum(
        "ithe,ishe->ihts", query, keys, preferred_element_type=jnp.float32
    ) * HEAD_DIM ** (-0.5)
    norm_log = jax.nn.logsumexp(scores, -1, keepdims=True)
    probs = jnp.exp(scores - norm_log).astype(jnp.bfloat16)
    return (
        jnp.einsum("ihts,ishe->ithe", probs, values, preferred_element_type=jnp.float32),
        norm_log,
    )


def attend_back(query, keys, values, norm_log, d_out):
    scale = HEAD_DIM ** (-0.5)
    scores = jnp.einsum("ithe,ishe->ihts", query, keys, preferred_element_type=jnp.float32) * scale
    probs = jnp.exp(scores - norm_log)
    d_probs = jnp.einsum("ithe,ishe->ihts", d_out, values, preferred_element_type=jnp.float32)
    d_scores = (probs * (d_probs - jnp.sum(probs * d_probs, -1, keepdims=True))).astype(
        jnp.bfloat16
    )
    d_query = (
        jnp.einsum("ihts,ishe->ithe", d_scores, keys, preferred_element_type=jnp.float32) * scale
    )
    d_keys = (
        jnp.einsum("ihts,ithe->ishe", d_scores, query, preferred_element_type=jnp.float32) * scale
    )
    d_values = jnp.einsum(
        "ihts,ithe->ishe", probs.astype(jnp.bfloat16), d_out, preferred_element_type=jnp.float32
    )
    return (d_query, d_keys, d_values)


def grid_shape(size_sets, index):
    pixels = size_sets[index][0]
    return (pixels.shape[1], pixels.shape[2], -1)


AXES = ("dp", "seq")
NT = (((1,), (1,)), ((), ()))
NN = (((1,), (0,)), ((), ()))
BF = jnp.bfloat16
F32 = jnp.float32
VMEM_BYTES = 58 << 20


class Places:
    def __init__(self):
        dp, seq = lax.axis_size("dp"), lax.axis_size("seq")
        self.count = dp * seq
        deep = 4 if dp % 8 == 0 else 1
        self.z = (dp // deep * seq, deep)
        self.x = (2 * seq, dp // deep // 2)
        self.core = (seq, 2)
        self.y = (1, seq)
        self.flat = lax.axis_index("dp") * seq + lax.axis_index("seq")

    def digit(self, digit):
        return (self.flat // digit[0]) % digit[1]

    def send(self, value, digit, steps):
        stride, radix = digit
        pairs = []
        for source in range(self.count):
            place = (source // stride) % radix
            pairs.append((source, source + ((place + steps) % radix - place) * stride))
        return lax.ppermute(value, AXES, pairs)

    def gather(self, value, order):
        held = value[None]
        shifts = [{}]
        for turn, digit in enumerate(order):
            parts = [held] + [self.send(held, digit, step) for step in range(1, digit[1])]
            shifts = [{**shift, digit: step} for step in range(digit[1]) for shift in shifts]
            if turn < len(order) - 1:
                held = jnp.concatenate(parts, 0)
        owner = jnp.zeros((self.count,), jnp.int32)
        for digit in order:
            steps = np.array([shift[digit] for shift in shifts], np.int32)
            owner = owner + ((self.digit(digit) - steps) % digit[1]) * digit[0]
        return parts, owner

    def scatter_sum(self, value, order):
        rows = value.shape[0] // self.count
        kept = [self.z, self.x, self.core, self.y]
        held = value.reshape([digit[1] for digit in kept] + [rows, value.shape[1]])
        for digit in order:
            axis = kept.index(digit)
            place, radix = self.digit(digit), digit[1]
            total = lax.dynamic_index_in_dim(held, place, axis, False).astype(F32)
            for step in range(1, radix):
                away = lax.dynamic_index_in_dim(held, (place + step) % radix, axis, False)
                total = total + self.send(away.astype(BF), digit, step).astype(F32)
            held = total
            kept.pop(axis)
        return held

    def sum_all(self, value, digits):
        for digit in digits:
            stride, radix = digit
            parts = [value] + [self.send(value, digit, step) for step in range(1, radix)]
            if radix == 2:
                value = parts[0] + parts[1]
            elif radix == 4:
                value = (parts[0] + parts[2]) + (parts[1] + parts[3])
            else:
                order = (self.digit(digit) - jnp.arange(radix)) % radix
                value = jnp.sum(jnp.take(jnp.stack(parts), order, 0), 0)
        return value


def placed_kernel(owner_ref, *refs, cuts):
    out_ref, sems = refs[-2], refs[-1]
    copies = []
    at = 0
    for half, (first, width, pieces) in enumerate(cuts):
        block = 0
        for _ in range(pieces):
            piece = refs[at]
            at += 1
            for index in range(piece.shape[0]):
                copies.append(
                    pltpu.make_async_copy(
                        piece.at[index],
                        out_ref.at[owner_ref[half, block], :, pl.ds(first, width)],
                        sems.at[half, block],
                    )
                )
                block += 1
    for copy in copies:
        copy.start()
    for copy in copies:
        copy.wait()


def place_blocks(halves):
    cuts, arrays, owners, first = [], [], [], 0
    for pieces, owner in halves:
        cuts.append((first, pieces[0].shape[2], len(pieces)))
        first += pieces[0].shape[2]
        arrays += pieces
        owners.append(owner)
    count, rows = owners[0].shape[0], arrays[0].shape[1]
    size = count * rows * first * 2
    out = pl.pallas_call(
        partial(placed_kernel, cuts=tuple(cuts)),
        out_shape=jax.ShapeDtypeStruct((count, rows, first), BF),
        in_specs=[pl.BlockSpec(memory_space=pltpu.SMEM)]
        + [pl.BlockSpec(memory_space=pl.ANY)] * len(arrays),
        out_specs=pl.BlockSpec(memory_space=pltpu.VMEM),
        scratch_shapes=[pltpu.SemaphoreType.DMA((len(cuts), count))],
        compiler_params=pltpu.CompilerParams(vmem_limit_bytes=VMEM_BYTES),
        cost_estimate=pl.CostEstimate(flops=0, bytes_accessed=2 * size, transcendentals=0),
        name="place_blocks",
    )(jnp.stack(owners), *arrays)
    return out.reshape(count * rows, first)


def interp_table(n_out, n_in):
    places = np.arange(n_out) * ((n_in - 1) / (n_out - 1))
    return np.maximum(0.0, 1.0 - np.abs(places[:, None] - np.arange(n_in)[None, :]))


def resize_table(patch):
    basis = interp_table(patch, BASE)
    table = np.linalg.solve(basis @ basis.T, basis)
    return np.kron(table, table).astype(np.float32)


def place_table(grid):
    table = interp_table(grid, 7)
    full = np.kron(table, table).astype(np.float32)
    high = full.astype(ml_dtypes.bfloat16)
    low = (full - high.astype(np.float32)).astype(ml_dtypes.bfloat16)
    return np.concatenate([high, low], 1)


def dot(left, right, dims):
    return lax.dot_general(left, right, dims, preferred_element_type=F32)


def estimate(flops, nbytes):
    return pl.CostEstimate(flops=int(flops), bytes_accessed=int(nbytes), transcendentals=0)


def normed(values):
    centred = values - jnp.mean(values, -1, keepdims=True)
    scale = lax.rsqrt(jnp.mean(centred * centred, -1, keepdims=True) + 1e-06)
    return centred * scale, scale


def norm_back(d_out, gain, hat, scale):
    d_hat = d_out * gain
    return scale * (
        d_hat
        - jnp.mean(d_hat, -1, keepdims=True)
        - hat * jnp.mean(d_hat * hat, -1, keepdims=True)
    )


def embed_kernel(flat_ref, weight_ref, gain_ref, qkvw_ref, x0_ref, qkv_ref):
    x0 = dot(flat_ref[...], weight_ref[...], NN)
    x0_ref[...] = x0
    h1 = (normed(x0)[0] * gain_ref[...]).astype(BF)
    width = 768
    for first in range(0, qkvw_ref.shape[1], width):
        cols = slice(first, first + width)
        qkv_ref[:, cols] = dot(h1, qkvw_ref[:, cols], NN).astype(BF)


def embed(flat, weight, gain, w_qkv, block):
    rows, depth = flat.shape
    width, out = w_qkv.shape
    return pl.pallas_call(
        embed_kernel,
        out_shape=(
            jax.ShapeDtypeStruct((rows, width), F32),
            jax.ShapeDtypeStruct((rows, out), BF),
        ),
        grid=(rows // block,),
        in_specs=[
            pl.BlockSpec((block, depth), lambda i: (i, 0)),
            pl.BlockSpec((depth, width), lambda i: (0, 0)),
            pl.BlockSpec((1, width), lambda i: (0, 0)),
            pl.BlockSpec((width, out), lambda i: (0, 0)),
        ],
        out_specs=[
            pl.BlockSpec((block, width), lambda i: (i, 0)),
            pl.BlockSpec((block, out), lambda i: (i, 0)),
        ],
        compiler_params=pltpu.CompilerParams(vmem_limit_bytes=VMEM_BYTES),
        cost_estimate=estimate(2 * rows * width * (depth + out), rows * (width + out) * 4),
        name="embed",
    )(flat, weight, gain, w_qkv)


def head_split(first, values):
    zero = jnp.zeros((), values.dtype)
    return jnp.where(first, values, zero), jnp.where(first, zero, values)


def attend_kernel(q_ref, k_ref, v_ref, out_ref, log_ref):
    lane = lax.broadcasted_iota(jnp.int32, (1, 128), 1)
    first = lane < HEAD_DIM
    one = jnp.ones((), BF)
    values = v_ref[...]
    keys = head_split(first, k_ref[...])
    sided = (jnp.where(first, values, one).T, jnp.where(first, one, values).T)
    query = q_ref[...] * jnp.asarray(HEAD_DIM**-0.5, BF)
    outs = []
    for head in range(2):
        scores = dot(keys[head], query, NT)
        top = jnp.max(scores, 0, keepdims=True)
        probs = jnp.exp(scores - top).astype(BF)
        mixed = dot(sided[head], probs, NN)
        at = HEAD_DIM * (1 - head)
        total = mixed[at : at + 1]
        own = HEAD_DIM * head
        outs.append(mixed[own : own + HEAD_DIM] / total)
        log_ref[0, 0, head : head + 1, :] = top + jnp.log(total)
    out_ref[...] = jnp.concatenate(outs, 0).T.astype(BF)


def attend_pairs(query, keys, values, cols, images, n_query, n_key):
    pairs = HEADS // 2
    width = HEADS * HEAD_DIM
    return pl.pallas_call(
        attend_kernel,
        out_shape=(
            jax.ShapeDtypeStruct((images * n_query, width), BF),
            jax.ShapeDtypeStruct((images, pairs, 2, n_query), F32),
        ),
        grid=(images, pairs),
        in_specs=[
            pl.BlockSpec((n_query, 128), lambda i, h: (i, h + cols[0])),
            pl.BlockSpec((n_key, 128), lambda i, h: (i, h + cols[1])),
            pl.BlockSpec((n_key, 128), lambda i, h: (i, h + cols[2])),
        ],
        out_specs=[
            pl.BlockSpec((n_query, 128), lambda i, h: (i, h)),
            pl.BlockSpec((1, 1, 2, n_query), lambda i, h: (i, h, 0, 0)),
        ],
        compiler_params=pltpu.CompilerParams(vmem_limit_bytes=VMEM_BYTES),
        cost_estimate=estimate(
            images * HEADS * n_query * n_key * 1600, images * (n_query + n_key) * width * 4
        ),
        name="attend",
    )(query, keys, values)


def attend_back_kernel(q_ref, k_ref, v_ref, do_ref, o_ref, log_ref, dq_ref, dk_ref, dv_ref):
    lane = lax.broadcasted_iota(jnp.int32, (1, 128), 1)
    first = lane < HEAD_DIM
    scale = jnp.asarray(HEAD_DIM**-0.5, BF)
    keys_all = k_ref[...]
    keys = head_split(first, keys_all)
    values = head_split(first, v_ref[...])
    query = q_ref[...] * scale
    d_out = do_ref[...]
    queries = head_split(first, query)
    d_outs = head_split(first, d_out)
    keys_t = tuple(part.T for part in head_split(first, keys_all * scale))
    both = (d_out.astype(F32) * o_ref[...].astype(F32)).T
    d_query, d_keys, d_values = 0.0, 0.0, 0.0
    for head in range(2):
        row = jnp.sum(both[HEAD_DIM * head : HEAD_DIM * (head + 1)], 0, keepdims=True)
        scores = dot(keys[head], query, NT)
        probs = jnp.exp(scores - log_ref[0, 0, head : head + 1, :])
        d_probs = dot(values[head], d_out, NT)
        d_scores = (probs * (d_probs - row)).astype(BF)
        d_keys = d_keys + dot(d_scores, queries[head], NN)
        d_values = d_values + dot(probs.astype(BF), d_outs[head], NN)
        d_query = d_query + dot(keys_t[head], d_scores, NN)
    dq_ref[...] = d_query.T.astype(BF)
    dk_ref[...] = d_keys.astype(dk_ref.dtype)
    dv_ref[...] = d_values.astype(dv_ref.dtype)


def attend_back_pairs(query, keys, values, cols, d_out, out, log, images, n_query, n_key, pair_set):
    begin, end = pair_set
    width = (end - begin) * 128
    rows = pl.BlockSpec((n_query, 128), lambda i, h: (i, h + begin))
    over_q = pl.BlockSpec((n_query, 128), lambda i, h: (i, h))
    over_k = pl.BlockSpec((n_key, 128), lambda i, h: (i, h))
    return pl.pallas_call(
        attend_back_kernel,
        out_shape=(
            jax.ShapeDtypeStruct((images * n_query, width), BF),
            jax.ShapeDtypeStruct((images * n_key, width), BF),
            jax.ShapeDtypeStruct((images * n_key, width), BF),
        ),
        grid=(images, end - begin),
        in_specs=[
            pl.BlockSpec((n_query, 128), lambda i, h: (i, h + cols[0] + begin)),
            pl.BlockSpec((n_key, 128), lambda i, h: (i, h + cols[1] + begin)),
            pl.BlockSpec((n_key, 128), lambda i, h: (i, h + cols[2] + begin)),
            rows,
            rows,
            pl.BlockSpec((1, 1, 2, n_query), lambda i, h: (i, h + begin, 0, 0)),
        ],
        out_specs=[over_q, over_k, over_k],
        compiler_params=pltpu.CompilerParams(vmem_limit_bytes=VMEM_BYTES),
        cost_estimate=estimate(
            images * 2 * (end - begin) * n_query * n_key * 2900,
            images * (n_query + n_key) * width * 8,
        ),
        name="attend_back",
    )(query, keys, values, d_out, out, log)


def gelu_parts(inner):
    bell = jnp.exp(-0.5 * inner * inner)
    base = 1.0 + (0.3275911 * 0.7071067811865476) * jnp.abs(inner)
    turn = pl.reciprocal(base, approx=True)
    turn = turn * (2.0 - base * turn)
    poly = 0.5 * 1.061405429
    for term in (-1.453152027, 1.421413741, -0.284496736, 0.254829592):
        poly = poly * turn + 0.5 * term
    tail = poly * turn * bell
    upper = jnp.where(inner < 0.0, tail, 1.0 - tail)
    return upper, inner * bell * 0.3989422804014327


def mlp_kernel(x0_ref, mixed_ref, wout_ref, gain_ref, wup_ref, x1_ref, slope_ref, xsum_ref, asum_ref, *, per):
    x1 = x0_ref[...] + dot(mixed_ref[...], wout_ref[...], NN)
    x1_ref[...] = x1
    h2 = (normed(x1)[0] * gain_ref[...]).astype(BF)

    @pl.when(pl.program_id(0) % per == 0)
    def _():
        xsum_ref[...] = jnp.zeros_like(xsum_ref)
        asum_ref[...] = jnp.zeros_like(asum_ref)

    xsum_ref[0] += jnp.sum(x1, 0, keepdims=True)
    width = 512
    for first in range(0, wup_ref.shape[1], width):
        cols = slice(first, first + width)
        inner = dot(h2, wup_ref[:, cols], NN)
        upper, slope = gelu_parts(inner)
        slope_ref[:, cols] = (upper + slope).astype(BF)
        act = (inner * upper).astype(BF).astype(F32)
        asum_ref[0, :, cols] += jnp.sum(act, 0, keepdims=True)


def mlp(x0, mixed, w_up_out, gain, images, block):
    rows, width = x0.shape
    hidden = w_up_out.shape[1] - width
    per = rows // images // block
    return pl.pallas_call(
        partial(mlp_kernel, per=per),
        out_shape=(
            jax.ShapeDtypeStruct((rows, width), F32),
            jax.ShapeDtypeStruct((rows, hidden), BF),
            jax.ShapeDtypeStruct((images, 1, width), F32),
            jax.ShapeDtypeStruct((images, 1, hidden), F32),
        ),
        grid=(rows // block,),
        in_specs=[
            pl.BlockSpec((block, width), lambda i: (i, 0)),
            pl.BlockSpec((block, width), lambda i: (i, 0)),
            pl.BlockSpec((width, width), lambda i: (0, hidden // width)),
            pl.BlockSpec((1, width), lambda i: (0, 0)),
            pl.BlockSpec((width, hidden), lambda i: (0, 0)),
        ],
        out_specs=[
            pl.BlockSpec((block, width), lambda i: (i, 0)),
            pl.BlockSpec((block, hidden), lambda i: (i, 0)),
            pl.BlockSpec((1, 1, width), lambda i: (i // per, 0, 0)),
            pl.BlockSpec((1, 1, hidden), lambda i: (i // per, 0, 0)),
        ],
        compiler_params=pltpu.CompilerParams(vmem_limit_bytes=VMEM_BYTES),
        cost_estimate=estimate(4 * rows * width * (hidden + width), rows * hidden * 4),
        name="mlp",
    )(x0, mixed, w_up_out, gain, w_up_out)


def head_kernel(
    xsum_ref, asum_ref, down_ref, head_ref, label_ref, alive_ref, whole_ref, total_ref,
    loss_ref, dlogit_ref, pooled_ref, dx2_ref, dact_ref, *, classes
):
    asum = asum_ref[...]
    high = asum.astype(BF)
    low = (asum - high.astype(F32)).astype(BF)
    whole = whole_ref[...]
    down = down_ref[...]
    pooled = (xsum_ref[...] + (dot(high, down, NT) + dot(low, down, NT))) / whole
    pooled_low = pooled.astype(BF)
    pooled_ref[...] = pooled_low
    head = head_ref[...]
    place = lax.broadcasted_iota(jnp.int32, (1, head.shape[1]), 1)
    logits = jnp.where(place < classes, dot(pooled_low, head, NN), -1e30)
    top = jnp.max(logits, -1, keepdims=True)
    norm_log = top + jnp.log(jnp.sum(jnp.exp(logits - top), -1, keepdims=True))
    hot = place == label_ref[...]
    true_logit = jnp.sum(jnp.where(hot, logits, 0.0), -1, keepdims=True)
    loss_ref[...] = jnp.broadcast_to(norm_log - true_logit, loss_ref.shape)
    soft = jnp.exp(logits - norm_log) - hot.astype(F32)
    d_logits = (soft * alive_ref[...] / total_ref[...]).astype(BF)
    dlogit_ref[...] = d_logits
    d_x2 = dot(d_logits, head, NT) / whole
    dx2_ref[...] = d_x2
    dact_ref[...] = dot(d_x2.astype(BF), down, NN)


def head_step(xsum, asum, w_down_head, labels, alive, whole, total, classes):
    rows, width = xsum.shape
    hidden = asum.shape[1]
    padded = w_down_head.shape[1] - hidden
    full = pl.BlockSpec(memory_space=pltpu.VMEM)
    spec = lambda shape, place: pl.BlockSpec(shape, lambda i: place)
    return pl.pallas_call(
        partial(head_kernel, classes=classes),
        out_shape=(
            jax.ShapeDtypeStruct((rows, 128), F32),
            jax.ShapeDtypeStruct((rows, padded), BF),
            jax.ShapeDtypeStruct((rows, width), BF),
            jax.ShapeDtypeStruct((rows, width), F32),
            jax.ShapeDtypeStruct((rows, hidden), F32),
        ),
        grid=(1,),
        in_specs=[
            spec((rows, width), (0, 0)),
            spec((rows, hidden), (0, 0)),
            spec((width, hidden), (0, 0)),
            spec((width, padded), (0, hidden // padded)),
            spec((rows, 1), (0, 0)),
            spec((rows, 1), (0, 0)),
            spec((rows, 1), (0, 0)),
            spec((1, 1), (0, 0)),
        ],
        out_specs=[
            spec((rows, 128), (0, 0)),
            spec((rows, padded), (0, 0)),
            spec((rows, width), (0, 0)),
            spec((rows, width), (0, 0)),
            spec((rows, hidden), (0, 0)),
        ],
        compiler_params=pltpu.CompilerParams(vmem_limit_bytes=VMEM_BYTES),
        cost_estimate=estimate(1 << 32, 8 << 20),
        name="head",
    )(xsum, asum, w_down_head, w_down_head, labels, alive, whole, total)


def mlp_back_kernel(*refs, steps):
    parts = (refs[0:5], refs[5:10])
    wout_ref, gain_ref, wup_ref = refs[10:13]
    outs = (refs[13:15], refs[15:17])
    gup_ref, gout_ref, ggain_ref = refs[17:20]
    up_acc, out_acc = refs[20:22]
    step = pl.program_id(0)

    def body(inputs, outputs, begin):
        slope_ref, dact_ref, x1_ref, dx2_ref, mixed_ref = inputs
        dx1_ref, dmixed_ref = outputs
        gain = gain_ref[...]
        hat, scale = normed(x1_ref[...])
        h2_t = (hat * gain).astype(BF).T
        d_h2 = 0.0
        width = 768
        for first in range(0, slope_ref.shape[1], width):
            cols = slice(first, first + width)
            d_inner = (slope_ref[:, cols].astype(F32) * dact_ref[0, :, cols]).astype(BF)
            d_h2 = d_h2 + dot(d_inner, wup_ref[:, cols], NT)
            grad = dot(h2_t, d_inner, NN)
            up_acc[:, cols] = grad if begin else up_acc[:, cols] + grad
        gain_grad = jnp.sum(d_h2 * hat, 0, keepdims=True)
        ggain_ref[...] = gain_grad if begin else ggain_ref[...] + gain_grad
        d_x1 = dx2_ref[0] + norm_back(d_h2, gain, hat, scale)
        dx1_ref[...] = d_x1
        d_attn = d_x1.astype(BF)
        grad = dot(mixed_ref[...].T, d_attn, NN)
        out_acc[...] = grad if begin else out_acc[...] + grad
        dmixed_ref[...] = dot(d_attn, wout_ref[...], NT).astype(BF)

    @pl.when(step == 0)
    def _():
        body(parts[1], outs[1], True)

    @pl.when(step > 0)
    def _():
        body(parts[0], outs[0], False)

    @pl.when(step == steps)
    def _():
        gup_ref[...] = up_acc[...].astype(BF)
        gout_ref[...] = out_acc[...].astype(BF)


def mlp_back(part_b, part_a, w_up_out, gain, images, block):
    slope_b, dact_b, x1_b, dx2_b, mixed_b = part_b
    slope_a, dact_a, x1_a, dx2_a, mixed_a = part_a
    rows, width = x1_b.shape
    rows_a = x1_a.shape[0]
    hidden = slope_b.shape[1]
    steps = rows // block
    per = steps // images
    at = lambda i: jnp.maximum(i - 1, 0)
    moving = lambda cols: pl.BlockSpec((block, cols), lambda i: (at(i), 0))
    still = lambda shape: pl.BlockSpec(shape, lambda i: (0,) * len(shape))
    image = lambda cols: pl.BlockSpec((1, 1, cols), lambda i: (at(i) // per, 0, 0))
    return pl.pallas_call(
        partial(mlp_back_kernel, steps=steps),
        out_shape=(
            jax.ShapeDtypeStruct((rows, width), F32),
            jax.ShapeDtypeStruct((rows, width), BF),
            jax.ShapeDtypeStruct((rows_a, width), F32),
            jax.ShapeDtypeStruct((rows_a, width), BF),
            jax.ShapeDtypeStruct((width, hidden), BF),
            jax.ShapeDtypeStruct((width, width), BF),
            jax.ShapeDtypeStruct((1, width), F32),
        ),
        grid=(steps + 1,),
        in_specs=[
            moving(hidden), image(hidden), moving(width), image(width), moving(width),
            still((rows_a, hidden)), still((1, 1, hidden)), still((rows_a, width)),
            still((1, 1, width)), still((rows_a, width)),
            pl.BlockSpec((width, width), lambda i: (0, hidden // width)),
            still((1, width)),
            still((width, hidden)),
        ],
        out_specs=[
            moving(width), moving(width), still((rows_a, width)), still((rows_a, width)),
            still((width, hidden)), still((width, width)), still((1, width)),
        ],
        scratch_shapes=[pltpu.VMEM((width, hidden), F32), pltpu.VMEM((width, width), F32)],
        compiler_params=pltpu.CompilerParams(vmem_limit_bytes=VMEM_BYTES),
        cost_estimate=estimate(
            4 * (rows + rows_a) * width * (hidden + width), (rows + rows_a) * hidden * 4
        ),
        name="mlp_back",
    )(slope_b, dact_b, x1_b, dx2_b, mixed_b, slope_a, dact_a, x1_a, dx2_a, mixed_a,
      w_up_out, gain, w_up_out)


def qkv_grad_kernel(*refs, steps, groups):
    n_in = 1 + groups
    parts = (refs[0:n_in], refs[n_in : 2 * n_in])
    gain_ref = refs[2 * n_in]
    out_ref, acc = refs[2 * n_in + 1], refs[2 * n_in + 2]
    step = pl.program_id(0)

    def body(inputs, begin):
        h1_t = (normed(inputs[0][...])[0] * gain_ref[...]).astype(BF).T
        first = 0
        for ref in inputs[1:]:
            cols = slice(first, first + ref.shape[1])
            first += ref.shape[1]
            grad = dot(h1_t, ref[...], NN)
            acc[:, cols] = grad if begin else acc[:, cols] + grad

    @pl.when(step == 0)
    def _():
        body(parts[1], True)

    @pl.when(step > 0)
    def _():
        body(parts[0], False)

    @pl.when(step == steps)
    def _():
        out_ref[...] = acc[...].astype(BF)


def qkv_grad(x0_b, d_b, x0_a, d_a, gain, block):
    rows, width = x0_b.shape
    rows_a = x0_a.shape[0]
    steps = rows // block
    at = lambda i: jnp.maximum(i - 1, 0)
    moving = lambda cols: pl.BlockSpec((block, cols), lambda i: (at(i), 0))
    still = lambda shape: pl.BlockSpec(shape, lambda i: (0,) * len(shape))
    total = sum(piece.shape[1] for piece in d_b)
    return pl.pallas_call(
        partial(qkv_grad_kernel, steps=steps, groups=len(d_b)),
        out_shape=jax.ShapeDtypeStruct((width, total), BF),
        grid=(steps + 1,),
        in_specs=[moving(width)]
        + [moving(piece.shape[1]) for piece in d_b]
        + [still((rows_a, width))]
        + [still((rows_a, piece.shape[1])) for piece in d_a]
        + [still((1, width))],
        out_specs=still((width, total)),
        scratch_shapes=[pltpu.VMEM((width, total), F32)],
        compiler_params=pltpu.CompilerParams(vmem_limit_bytes=VMEM_BYTES),
        cost_estimate=estimate(2 * (rows + rows_a) * width * total, (rows + rows_a) * total * 4),
        name="qkv_grad",
    )(x0_b, *d_b, x0_a, *d_a, gain)


def embed_back_kernel(*refs, steps, groups, places):
    n_in = 3 + groups
    parts = (refs[0:n_in], refs[n_in : 2 * n_in])
    gain_ref, qkvw_ref = refs[2 * n_in : 2 * n_in + 2]
    outs = refs[2 * n_in + 2 : 2 * n_in + 4]
    ggain_ref = refs[2 * n_in + 4]
    step = pl.program_id(0)

    def body(inputs, out_ref, begin, first_of_sum):
        x0_ref, dx1_ref, flat_ref = inputs[:3]
        gain = gain_ref[...]
        hat, scale = normed(x0_ref[...])
        d_h1 = 0.0
        for ref, (first, width) in zip(inputs[3:], places):
            d_h1 = d_h1 + dot(ref[...], qkvw_ref[:, first : first + width], NT)
        gain_grad = jnp.sum(d_h1 * hat, 0, keepdims=True)
        ggain_ref[...] = gain_grad if first_of_sum else ggain_ref[...] + gain_grad
        d_x0 = (dx1_ref[...] + norm_back(d_h1, gain, hat, scale)).astype(BF)
        grad = dot(d_x0.T, flat_ref[...], NN)
        if begin is None:
            out_ref[...] = grad
        else:
            out_ref[...] = jnp.where(begin, 0.0, out_ref[...]) + grad

    @pl.when(step == 0)
    def _():
        outs[0][...] = jnp.zeros_like(outs[0])
        body(parts[1], outs[1], None, True)

    @pl.when(step > 0)
    def _():
        body(parts[0], outs[0], False, False)


def embed_back(x0_b, dx1_b, flat_b, d_b, x0_a, dx1_a, flat_a, d_a, gain, w_qkv, places, block):
    rows, width = x0_b.shape
    rows_a = x0_a.shape[0]
    steps = rows // block
    at = lambda i: jnp.maximum(i - 1, 0)
    moving = lambda array: pl.BlockSpec((block, array.shape[1]), lambda i: (at(i), 0))
    still = lambda shape: pl.BlockSpec(shape, lambda i: (0,) * len(shape))
    inputs_b = (x0_b, dx1_b, flat_b, *d_b)
    inputs_a = (x0_a, dx1_a, flat_a, *d_a)
    return pl.pallas_call(
        partial(embed_back_kernel, steps=steps, groups=len(d_b), places=tuple(places)),
        out_shape=(
            jax.ShapeDtypeStruct((width, flat_b.shape[1]), F32),
            jax.ShapeDtypeStruct((width, flat_a.shape[1]), F32),
            jax.ShapeDtypeStruct((1, width), F32),
        ),
        grid=(steps + 1,),
        in_specs=[moving(array) for array in inputs_b]
        + [still(array.shape) for array in inputs_a]
        + [still((1, width)), still(w_qkv.shape)],
        out_specs=[
            still((width, flat_b.shape[1])),
            still((width, flat_a.shape[1])),
            still((1, width)),
        ],
        compiler_params=pltpu.CompilerParams(vmem_limit_bytes=VMEM_BYTES),
        cost_estimate=estimate(
            2 * (rows + rows_a) * width * (w_qkv.shape[1] + 640), (rows + rows_a) * 10000
        ),
        name="embed_back",
    )(*inputs_b, *inputs_a, gain, w_qkv)


def after(value, *others):
    return lax.optimization_barrier((value, *others))[0]


def padded_cols(array, width):
    return jnp.pad(array, ((0, 0), (0, width - array.shape[1])))


def round_up(count, unit):
    return -(-count // unit) * unit


def fast_step(
    pixels_a, pixels_b, labels_a, labels_b, live_a, live_b, masters, firsts, seconds
):
    qkv_w, out_w, mlp_w, kern_w, pos_w, head_w, gains = masters
    places = Places()
    z, x, core, y = places.z, places.x, places.core, places.y
    seq = lax.axis_size("seq")
    row = lax.axis_index("seq")
    lead = (row == 0).astype(F32)
    width = HEADS * HEAD_DIM
    hidden = mlp_w.shape[2]
    classes = head_w.shape[1]
    classes_up = round_up(classes, 1024)
    rows_own = qkv_w.shape[0]

    images_a, rows_a, grid_a, depth_a = pixels_a.shape
    images_b, rows_b, grid_b, depth_b = pixels_b.shape
    own_b = images_b // seq
    parts_b, tabs_b = [], []
    table_b = jnp.asarray(place_table(grid_b))
    table_a = jnp.asarray(place_table(grid_a))
    span_b, span_a = rows_b * grid_b, rows_a * grid_a
    for step in range(seq):
        part = lax.dynamic_slice_in_dim(pixels_b, ((row + step) % seq) * own_b, own_b, 0)
        parts_b.append(places.send(part, y, step) if step else part)
        tabs_b.append(lax.dynamic_slice_in_dim(table_b, ((row - step) % seq) * span_b, span_b, 0))
    tab_a = lax.dynamic_slice_in_dim(table_a, row * span_a, span_a, 0)
    whole_a, whole_b = grid_a * grid_a, grid_b * grid_b

    tables = [resize_table(PATCH_B), resize_table(PATCH_A)]
    sizes = [3 * table.shape[0] for table in tables]
    kern_cols = lax.all_to_all(
        kern_w.astype(BF).T, AXES, split_axis=0, concat_axis=1, tiled=True
    )
    kern_cols = kern_cols.astype(F32).reshape(rows_own, 3, BASE * BASE)
    resized = [
        jnp.einsum("dck,pk->dcp", kern_cols, jnp.asarray(table), precision=HIGH).reshape(
            rows_own, -1
        )
        for table in tables
    ]
    small = jnp.concatenate(
        [piece.astype(BF) for piece in resized] + [pos_w.astype(BF).T, gains.astype(BF).T], 1
    )
    small_width = small.shape[1]
    small = padded_cols(small, round_up(small_width, 128))

    def gather_halves(value):
        cut = value.shape[1] // 2
        return [
            places.gather(value[:, :cut], (z, x, y, core)),
            places.gather(value[:, cut:], (z, y, x, core)),
        ]

    qkv_halves = gather_halves(qkv_w.astype(BF))
    w_small = place_blocks([places.gather(small, (z, x, y, core))])
    w_qkv = place_blocks(qkv_halves)
    up_out = jnp.concatenate([mlp_w[0].astype(BF), out_w.astype(BF)], 1)
    up_out = after(up_out, qkv_halves[0][0][0], qkv_halves[1][0][0])
    up_halves = gather_halves(up_out)
    down_head = jnp.concatenate(
        [mlp_w[1].astype(BF), padded_cols(head_w.astype(BF), classes_up)], 1
    )
    down_head = after(down_head, up_halves[0][0][0], up_halves[1][0][0])
    down_halves = gather_halves(down_head)

    count = jnp.stack([jnp.sum(live_a), jnp.sum(live_b)]).astype(F32).reshape(1, 2)
    count = places.sum_all(count, (z, x, core))
    total = jnp.maximum(jnp.sum(count), 1.0)

    small_t = w_small.T
    pos_rows = small_t[sum(sizes) : sum(sizes) + 49]
    gain_rows = small_t[sum(sizes) + 49 : sum(sizes) + 51].astype(F32)
    gain1, gain2 = gain_rows[0:1], gain_rows[1:2]

    def embedding(rows, tab, kernel):
        depth = round_up(rows.shape[1] + 98, 128)
        flat = padded_cols(jnp.concatenate([rows, tab], 1), depth)
        weight = jnp.concatenate([kernel, pos_rows, pos_rows], 0)
        return flat, jnp.pad(weight, ((0, depth - weight.shape[0]), (0, 0)))

    pix_b = jnp.concatenate(parts_b, 1).reshape(own_b * whole_b, depth_b)
    tab_b = jnp.broadcast_to(
        jnp.concatenate(tabs_b, 0)[None], (own_b, whole_b, 98)
    ).reshape(-1, 98)
    flat_b, weight_b = embedding(pix_b, tab_b, small_t[: sizes[0]])
    flat_a, weight_a = embedding(
        pixels_a.reshape(span_a, depth_a), tab_a, small_t[sizes[0] : sizes[0] + sizes[1]]
    )
    block = 256
    x0_a, qkv_a = embed(flat_a, weight_a, gain1, w_qkv, span_a)
    kv_a = [qkv_a[:, width:]]
    kv_a += [places.send(kv_a[0], y, step) for step in range(1, seq)]
    x0_b, qkv_b = embed(flat_b, weight_b, gain1, w_qkv, block)
    pairs = HEADS // 2
    cols_b = (0, pairs, 2 * pairs)
    cols_a = (0, 0, pairs)
    mixed_b, log_b = attend_pairs(qkv_b, qkv_b, qkv_b, cols_b, own_b, whole_b, whole_b)
    kv_a = jnp.concatenate(kv_a, 0)
    mixed_a, log_a = attend_pairs(qkv_a, kv_a, kv_a, cols_a, 1, span_a, seq * span_a)

    w_up_out = place_blocks(up_halves)
    x1_a, slope_a, xsum_a, asum_a = mlp(x0_a, mixed_a, w_up_out, gain2, 1, span_a)
    sums_a = places.sum_all(jnp.concatenate([xsum_a[0], asum_a[0]], 1), (y,))
    x1_b, slope_b, xsum_b, asum_b = mlp(x0_b, mixed_b, w_up_out, gain2, own_b, block)
    w_down_head = place_blocks(down_halves)

    rows_up = round_up(own_b + 1, 8)
    fill = rows_up - own_b - 1
    stack = lambda first, last: jnp.pad(
        jnp.concatenate([first, last], 0), ((0, fill), (0, 0))
    )
    xsum = stack(xsum_b[:, 0], sums_a[:, :width])
    asum = stack(asum_b[:, 0], sums_a[:, width:])
    mine = lambda array: lax.dynamic_slice_in_dim(array, row * own_b, own_b, 0)[:, None]
    labels = stack(mine(labels_b), labels_a[:, None])
    alive_b = mine(live_b).astype(F32)
    alive_a = live_a.astype(F32)[:, None]
    alive = stack(alive_b, alive_a)
    whole = np.ones((rows_up, 1), np.float32)
    whole[:own_b], whole[own_b] = whole_b, whole_a
    losses, d_logits, pooled, d_x2, d_act = head_step(
        xsum, asum, w_down_head, labels, alive, jnp.asarray(whole), total.reshape(1, 1), classes
    )
    loss_sums = jnp.stack(
        [lead * jnp.sum(alive_a * losses[own_b : own_b + 1, :1]),
         jnp.sum(alive_b * losses[:own_b, :1])]
    ).reshape(1, 2)
    loss_sums = places.sum_all(loss_sums, (z, x, core, y))

    once = jnp.concatenate(
        [jnp.ones((own_b, 1), F32), lead.reshape(1, 1), jnp.zeros((fill, 1), F32)], 0
    ).astype(BF)
    rows_out = jnp.concatenate(
        [asum.astype(BF), pooled, d_x2.astype(BF) * once, d_logits * once], 1
    )
    image_rows, _ = places.gather(rows_out, (z, x, y, core))
    image_rows = jnp.concatenate(image_rows, 0).reshape(places.count * rows_up, -1)

    part = lambda array, lo, hi: array[lo:hi][:, None]
    d_x1_b, d_mixed_b, d_x1_a, d_mixed_a, grad_up, grad_out, grad_gain2 = mlp_back(
        (slope_b, part(d_act, 0, own_b), x1_b, part(d_x2, 0, own_b), mixed_b),
        (slope_a, part(d_act, own_b, own_b + 1), x1_a, part(d_x2, own_b, own_b + 1), mixed_a),
        w_up_out, gain2, own_b, block,
    )
    cut = hidden // 2
    own_up = [
        places.scatter_sum(grad_up[:, :cut], (core, x, y, z)),
        places.scatter_sum(grad_up[:, cut:], (core, y, x, z)),
    ]
    own_out = places.scatter_sum(grad_out, (core, x, y, z))

    dq_a, dk_a, dv_a = attend_back_pairs(
        qkv_a, kv_a, kv_a, cols_a, d_mixed_a, mixed_a, log_a, 1, span_a, seq * span_a, (0, pairs)
    )
    dkv_a = jnp.concatenate([dk_a, dv_a], 1)
    dkv_own = dkv_a[:span_a].astype(F32)
    for step in range(1, seq):
        dkv_own = dkv_own + places.send(
            dkv_a[step * span_a : (step + 1) * span_a], y, seq - step
        ).astype(F32)
    dkv_own = dkv_own.astype(BF)

    group_sets = ((0, pairs // 2), (pairs // 2, pairs))
    d_parts_b, d_parts_a, spots, own_groups = [], [], [], []
    for begin, end in group_sets:
        got = attend_back_pairs(
            qkv_b, qkv_b, qkv_b, cols_b, d_mixed_b, mixed_b, log_b, own_b, whole_b, whole_b,
            (begin, end),
        )
        lo, hi = begin * 128, end * 128
        from_a = (dq_a[:, lo:hi], dkv_own[:, lo:hi], dkv_own[:, width + lo : width + hi])
        grad = qkv_grad(x0_b, got, x0_a, from_a, gain1, block)
        order = (core, x, y, z) if begin else (core, y, x, z)
        own_groups.append(places.scatter_sum(grad, order))
        d_parts_b += got
        d_parts_a += from_a
        spots += [(lo, hi - lo), (width + lo, hi - lo), (2 * width + lo, hi - lo)]
    grad_b, grad_a, grad_gain1 = embed_back(
        x0_b, d_x1_b, flat_b, d_parts_b, x0_a, d_x1_a, flat_a, d_parts_a, gain1, w_qkv, spots, block
    )
    span = hi - lo
    own_qkv = jnp.concatenate(
        [group[:, k * span : (k + 1) * span] for k in range(3) for group in own_groups], 1
    )
    twice = lambda array, at: array[:, at : at + 49] + array[:, at + 49 : at + 98]
    grad_small = jnp.concatenate(
        [
            grad_b[:, : sizes[0]],
            grad_a[:, : sizes[1]],
            twice(grad_b, sizes[0]) + twice(grad_a, sizes[1]),
            grad_gain1.T,
            grad_gain2.T,
        ],
        1,
    )
    grad_small = padded_cols(grad_small, round_up(small_width, 128)).astype(BF)
    own_small = places.scatter_sum(grad_small, (core, x, y, z))
    kern_t = jnp.zeros((rows_own, 3, BASE * BASE), F32)
    first = 0
    for table, size in zip(tables, sizes):
        piece = own_small[:, first : first + size].reshape(rows_own, 3, -1)
        kern_t = kern_t + jnp.einsum("dcp,pk->dck", piece, jnp.asarray(table), precision=HIGH)
        first += size
    kern_t = kern_t.reshape(rows_own, -1)
    own_pos = own_small[:, first : first + 49].T
    own_gain = own_small[:, first + 49 : first + 51].T
    own_kern = lax.all_to_all(kern_t, AXES, split_axis=1, concat_axis=0, tiled=True).T

    mine_at = places.flat * rows_own
    columns = lambda lo: lax.dynamic_slice_in_dim(
        image_rows[:, lo : lo + width], mine_at, rows_own, 1
    )
    own_down = lax.dot_general(
        columns(hidden + width), image_rows[:, :hidden], ROWS_DIM, preferred_element_type=F32
    )
    own_head = lax.dot_general(
        columns(hidden),
        image_rows[:, hidden + 2 * width : hidden + 2 * width + classes],
        ROWS_DIM,
        preferred_element_type=F32,
    )
    own_up = jnp.concatenate(own_up, 1)
    own_mlp = jnp.stack([own_up, own_down], 0)
    owned = (own_qkv, own_out, own_mlp, own_kern, own_pos, own_head, own_gain)
    square_sum = sum(
        jnp.sum(piece * piece)
        for piece in (own_qkv, own_out, own_up, own_down, kern_t, own_pos, own_head, own_gain)
    )
    grad_norm = jnp.sqrt(places.sum_all(square_sum.reshape(1, 1), (z, x, core, y)))[0, 0]
    factor = jnp.minimum(1.0, CLIP / (grad_norm + 1e-06))
    done = [adamw(masters[i], firsts[i], seconds[i], owned[i] * factor, RATES[i]) for i in range(7)]
    size_stats = (loss_sums / jnp.maximum(count, 1.0))[0]
    return (
        *(item[0] for item in done),
        *(item[1] for item in done),
        *(item[2] for item in done),
        size_stats,
        grad_norm,
    )


def fits_fast(pixels_a, pixels_b, qkv_w):
    dp, seq = lax.axis_size("dp"), lax.axis_size("seq")
    images_b, rows_b, grid_b, _ = pixels_b.shape
    span_a = pixels_a.shape[1] * pixels_a.shape[2]
    return (
        dp % 8 == 0
        and images_b % seq == 0
        and pixels_a.shape[0] == 1
        and grid_b * grid_b % 256 == 0
        and span_a % 32 == 0
    )


def on_device(
    pixels_a,
    pixels_b,
    labels_a,
    labels_b,
    live_a,
    live_b,
    qkv_w,
    out_w,
    mlp_w,
    kern_w,
    pos_w,
    head_w,
    gains,
    qkv_m,
    out_m,
    mlp_m,
    kern_m,
    pos_m,
    head_m,
    gains_m,
    qkv_v,
    out_v,
    mlp_v,
    kern_v,
    pos_v,
    head_v,
    gains_v,
):
    masters = (qkv_w, out_w, mlp_w, kern_w, pos_w, head_w, gains)
    firsts = (qkv_m, out_m, mlp_m, kern_m, pos_m, head_m, gains_m)
    seconds = (qkv_v, out_v, mlp_v, kern_v, pos_v, head_v, gains_v)
    if fits_fast(pixels_a, pixels_b, qkv_w):
        return fast_step(
            pixels_a, pixels_b, labels_a, labels_b, live_a, live_b, masters, firsts, seconds
        )
    bf16 = jnp.bfloat16
    w_qkv, w_out, w_mlp, w_kern, w_pos, w_head, w_gain = (
        lax.all_gather(qkv_w.astype(bf16), ("dp", "seq"), axis=0, tiled=True),
        lax.all_gather(out_w.astype(bf16), ("dp", "seq"), axis=0, tiled=True),
        lax.all_gather(mlp_w.astype(bf16), ("dp", "seq"), axis=1, tiled=True),
        lax.all_gather(kern_w.astype(bf16), ("dp", "seq"), axis=0, tiled=True),
        lax.all_gather(pos_w.astype(bf16), ("dp", "seq"), axis=1, tiled=True),
        lax.all_gather(head_w.astype(bf16), ("dp", "seq"), axis=0, tiled=True),
        lax.all_gather(gains.astype(bf16), ("dp", "seq"), axis=1, tiled=True),
    )
    seq_count = lax.axis_size("seq")
    seq_place = lax.axis_index("seq")
    gain_full = w_gain.astype(jnp.float32)
    kern_full = w_kern.astype(jnp.float32)
    pos_full = w_pos.astype(jnp.float32)
    size_sets = ((pixels_a, labels_a, live_a, PATCH_A), (pixels_b, labels_b, live_b, PATCH_B))
    embeds, flats, kern_backs, pos_backs, layouts = ([], [], [], [], [])
    start = 0
    for pixels, labels, live, patch in size_sets:
        images, rows, grid, depth = pixels.shape
        flat = pixels.reshape(images * rows * grid, depth)
        resized, kern_back = jax.vjp(partial(kernel_resize, patch=patch), kern_full)
        row_table = lax.dynamic_slice_in_dim(interp_matrix(grid, 7), seq_place * rows, rows, 0)
        place, pos_back = jax.vjp(partial(grid_resize, row_table=row_table, grid=grid), pos_full)
        embed = jnp.dot(flat, resized.astype(bf16), preferred_element_type=jnp.float32)
        embed = embed.reshape(images, rows * grid, -1) + place.reshape(1, rows * grid, -1)
        embeds.append(embed.reshape(images * rows * grid, -1))
        flats.append(flat)
        kern_backs.append(kern_back)
        pos_backs.append(pos_back)
        layouts.append((start, start + images * rows * grid, images, rows * grid, grid * grid))
        start = start + images * rows * grid
    x0 = jnp.concatenate(embeds, 0)
    h1_full, norm1_back = jax.vjp(layer_norm, x0, gain_full[0])
    h1 = h1_full.astype(bf16)
    qkv = jnp.dot(h1, w_qkv, preferred_element_type=jnp.float32).astype(bf16)
    width = qkv.shape[1] // 3
    local_kv = qkv[:, width:]
    blocks = [local_kv]
    moving = local_kv
    for turn in range(1, seq_count):
        moving = from_behind(moving, "seq", 1)
        blocks.append(moving)
    all_kv = jnp.stack(blocks, 0)
    mixed_parts, saved = ([], [])
    for first_row, last_row, images, length, whole in layouts:
        query = qkv[first_row:last_row, :width].reshape(images, length, HEADS, HEAD_DIM)
        remote = all_kv[:, first_row:last_row].reshape(
            seq_count, images, length, 2, HEADS, HEAD_DIM
        )
        remote = remote.transpose(1, 0, 2, 3, 4, 5).reshape(
            images, seq_count * length, 2, HEADS, HEAD_DIM
        )
        keys, values = (remote[:, :, 0], remote[:, :, 1])
        attended, norm_log = attend(query, keys, values)
        mixed_parts.append(attended.reshape(last_row - first_row, width))
        saved.append((query, keys, values, norm_log))
    mixed = jnp.concatenate(mixed_parts, 0).astype(bf16)
    x1 = x0 + jnp.dot(mixed, w_out, preferred_element_type=jnp.float32)
    h2_full, norm2_back = jax.vjp(layer_norm, x1, gain_full[1])
    h2 = h2_full.astype(bf16)
    inner = jnp.dot(h2, w_mlp[0], preferred_element_type=jnp.float32)
    act_full, gelu_back = jax.vjp(partial(jax.nn.gelu, approximate=False), inner)
    act = act_full.astype(bf16)
    x2 = x1 + lax.dot_general(act, w_mlp[1], COLS_DIM, preferred_element_type=jnp.float32)
    sum_a = x2[layouts[0][0] : layouts[0][1]].reshape(layouts[0][2], layouts[0][3], -1).sum(1)
    sum_b = x2[layouts[1][0] : layouts[1][1]].reshape(layouts[1][2], layouts[1][3], -1).sum(1)
    pooled_sums = lax.psum((sum_a, sum_b), "seq")
    stats, head_parts = ([], [])
    for index in range(2):
        labels, live = (size_sets[index][1], size_sets[index][2])
        pooled_low = (pooled_sums[index] / float(layouts[index][4])).astype(bf16)
        logits = jnp.dot(pooled_low, w_head, preferred_element_type=jnp.float32)
        norm_log = jax.nn.logsumexp(logits, -1)
        hot = (labels[:, None] == jnp.arange(logits.shape[1], dtype=jnp.int32)[None, :]).astype(
            jnp.float32
        )
        true_logit = jnp.sum(hot * logits, -1)
        alive = live.astype(jnp.float32)
        stats.append(jnp.stack([jnp.sum(alive * (norm_log - true_logit)), jnp.sum(alive)]))
        head_parts.append((pooled_low, jnp.exp(logits - norm_log[:, None]) - hot, alive))
    stats_a, stats_b = lax.psum((stats[0], stats[1]), "dp")
    total = jnp.maximum(stats_a[1] + stats_b[1], 1.0)
    grad_head = jnp.zeros(w_head.shape, jnp.float32)
    d_x2_parts = []
    for index in range(2):
        pooled_low, soft_minus, alive = head_parts[index]
        d_logits = (soft_minus * alive[:, None] / total).astype(bf16)
        grad_head = grad_head + lax.dot_general(
            pooled_low, d_logits, ROWS_DIM, preferred_element_type=jnp.float32
        )
        d_pooled = lax.dot_general(d_logits, w_head, COLS_DIM, preferred_element_type=jnp.float32)
        images, length, whole = (layouts[index][2], layouts[index][3], layouts[index][4])
        spread = jnp.broadcast_to(
            (d_pooled / float(whole))[:, None, :], (images, length, d_pooled.shape[1])
        )
        d_x2_parts.append(spread.reshape(images * length, -1))
    d_x2 = jnp.concatenate(d_x2_parts, 0)
    d_mix = d_x2.astype(bf16)
    grad_down = lax.dot_general(d_mix, act, ROWS_DIM, preferred_element_type=jnp.float32)
    d_act = jnp.dot(d_mix, w_mlp[1], preferred_element_type=jnp.float32)
    d_inner = gelu_back(d_act)[0].astype(bf16)
    grad_up = lax.dot_general(h2, d_inner, ROWS_DIM, preferred_element_type=jnp.float32)
    d_h2 = lax.dot_general(d_inner, w_mlp[0], COLS_DIM, preferred_element_type=jnp.float32)
    d_x1_norm, grad_gain2 = norm2_back(d_h2)
    d_x1 = d_x2 + d_x1_norm
    d_attn = d_x1.astype(bf16)
    grad_out = lax.dot_general(mixed, d_attn, ROWS_DIM, preferred_element_type=jnp.float32)
    d_mixed = lax.dot_general(d_attn, w_out, COLS_DIM, preferred_element_type=jnp.float32).astype(
        bf16
    )
    d_query_parts, d_kv_parts = ([], [])
    for index in range(2):
        first_row, last_row, images, length, whole = layouts[index]
        query, keys, values, norm_log = saved[index]
        d_out = d_mixed[first_row:last_row].reshape(images, length, HEADS, HEAD_DIM)
        d_query, d_keys, d_values = attend_back(query, keys, values, norm_log, d_out)
        d_query_parts.append(d_query.reshape(last_row - first_row, width))
        paired = jnp.stack([d_keys, d_values], 2).reshape(images, seq_count, length, 2 * width)
        d_kv_parts.append(
            paired.transpose(1, 0, 2, 3).reshape(seq_count, last_row - first_row, 2 * width)
        )
    d_all = jnp.concatenate(d_kv_parts, 1)
    mine_kv = d_all[1 % seq_count]
    for turn in range(1, seq_count):
        mine_kv = (
            from_behind(mine_kv.astype(jnp.bfloat16), "seq", 1).astype(mine_kv.dtype)
            + d_all[(turn + 1) % seq_count]
        )
    d_qkv = jnp.concatenate([jnp.concatenate(d_query_parts, 0), mine_kv], 1).astype(bf16)
    grad_qkv = lax.dot_general(h1, d_qkv, ROWS_DIM, preferred_element_type=jnp.float32)
    d_h1 = lax.dot_general(d_qkv, w_qkv, COLS_DIM, preferred_element_type=jnp.float32)
    d_x0_norm, grad_gain1 = norm1_back(d_h1)
    d_x0 = d_x1 + d_x0_norm
    grad_kern = jnp.zeros(kern_full.shape, jnp.float32)
    grad_pos = jnp.zeros(pos_full.shape, jnp.float32)
    for index in range(2):
        first_row, last_row, images, length, whole = layouts[index]
        d_rows = d_x0[first_row:last_row]
        d_kernel = lax.dot_general(
            flats[index], d_rows.astype(bf16), ROWS_DIM, preferred_element_type=jnp.float32
        )
        grad_kern = grad_kern + kern_backs[index](d_kernel)[0]
        d_place = d_rows.reshape(images, length, -1).sum(0)
        grad_pos = grad_pos + pos_backs[index](d_place.reshape(grid_shape(size_sets, index)))[0]
    grad_mlp = jnp.stack([grad_up, grad_down], 0)
    grad_gain = jnp.stack([grad_gain1, grad_gain2], 0)
    grad_head = grad_head / float(seq_count)
    owned = (
        lax.psum_scatter(grad_qkv, ("dp", "seq"), scatter_dimension=0, tiled=True),
        lax.psum_scatter(grad_out, ("dp", "seq"), scatter_dimension=0, tiled=True),
        lax.psum_scatter(grad_mlp, ("dp", "seq"), scatter_dimension=1, tiled=True),
        lax.psum_scatter(grad_kern, ("dp", "seq"), scatter_dimension=0, tiled=True),
        lax.psum_scatter(grad_pos, ("dp", "seq"), scatter_dimension=1, tiled=True),
        lax.psum_scatter(grad_head, ("dp", "seq"), scatter_dimension=0, tiled=True),
        lax.psum_scatter(grad_gain, ("dp", "seq"), scatter_dimension=1, tiled=True),
    )
    square_sum = sum((jnp.sum(piece * piece) for piece in owned))
    grad_norm = jnp.sqrt(lax.psum(square_sum, ("dp", "seq")))
    factor = jnp.minimum(1.0, CLIP / (grad_norm + 1e-06))
    done = [adamw(masters[i], firsts[i], seconds[i], owned[i] * factor, RATES[i]) for i in range(7)]
    size_stats = jnp.stack(
        [stats_a[0] / jnp.maximum(stats_a[1], 1.0), stats_b[0] / jnp.maximum(stats_b[1], 1.0)]
    )
    return (
        done[0][0],
        done[1][0],
        done[2][0],
        done[3][0],
        done[4][0],
        done[5][0],
        done[6][0],
        done[0][1],
        done[1][1],
        done[2][1],
        done[3][1],
        done[4][1],
        done[5][1],
        done[6][1],
        done[0][2],
        done[1][2],
        done[2][2],
        done[3][2],
        done[4][2],
        done[5][2],
        done[6][2],
        size_stats,
        grad_norm,
    )


def solution(mesh):
    placed = (
        P("dp", "seq", None, None),
        P("dp", "seq", None, None),
        P("dp"),
        P("dp"),
        P("dp"),
        P("dp"),
        P(("dp", "seq"), None),
        P(("dp", "seq"), None),
        P(None, ("dp", "seq"), None),
        P(("dp", "seq"), None),
        P(None, ("dp", "seq")),
        P(("dp", "seq"), None),
        P(None, ("dp", "seq")),
        P(("dp", "seq"), None),
        P(("dp", "seq"), None),
        P(None, ("dp", "seq"), None),
        P(("dp", "seq"), None),
        P(None, ("dp", "seq")),
        P(("dp", "seq"), None),
        P(None, ("dp", "seq")),
        P(("dp", "seq"), None),
        P(("dp", "seq"), None),
        P(None, ("dp", "seq"), None),
        P(("dp", "seq"), None),
        P(None, ("dp", "seq")),
        P(("dp", "seq"), None),
        P(None, ("dp", "seq")),
    )
    return jax.shard_map(
        on_device,
        mesh=mesh,
        in_specs=placed,
        out_specs=(
            P(("dp", "seq"), None),
            P(("dp", "seq"), None),
            P(None, ("dp", "seq"), None),
            P(("dp", "seq"), None),
            P(None, ("dp", "seq")),
            P(("dp", "seq"), None),
            P(None, ("dp", "seq")),
            P(("dp", "seq"), None),
            P(("dp", "seq"), None),
            P(None, ("dp", "seq"), None),
            P(("dp", "seq"), None),
            P(None, ("dp", "seq")),
            P(("dp", "seq"), None),
            P(None, ("dp", "seq")),
            P(("dp", "seq"), None),
            P(("dp", "seq"), None),
            P(None, ("dp", "seq"), None),
            P(("dp", "seq"), None),
            P(None, ("dp", "seq")),
            P(("dp", "seq"), None),
            P(None, ("dp", "seq")),
            P(),
            P(),
        ),
        check_vma=False,
    )
```

```python
import math
from functools import partial

import jax
import jax.numpy as jnp
import ml_dtypes
import numpy as np
from jax import lax
from jax.experimental import pallas as pl
from jax.experimental.pallas import tpu as pltpu
from jax.sharding import Mesh
from jax.sharding import PartitionSpec as P

HEADS = 12
HEAD_DIM = 64
BASE = 32
PATCH_A = 10
PATCH_B = 12


HIGH = lax.Precision.HIGHEST
RATES = (0.012, 0.2, 0.012, 0.03, 0.15, 0.06, 0.25)
CLIP = 0.001
ROWS_DIM = (((0,), (0,)), ((), ()))
COLS_DIM = (((1,), (1,)), ((), ()))


def from_behind(value, axis, steps):
    count = lax.axis_size(axis)
    pairs = [(source, (source + steps) % count) for source in range(count)]
    return lax.ppermute(value, axis, pairs)


def interp_matrix(n_out, n_in):
    places = jnp.arange(n_out, dtype=jnp.float32) * ((n_in - 1) / (n_out - 1))
    return jnp.maximum(
        0.0, 1.0 - jnp.abs(places[:, None] - jnp.arange(n_in, dtype=jnp.float32)[None, :])
    )


def pinv_table(patch):
    basis = interp_matrix(patch, BASE)
    gram = jnp.dot(basis, basis.T, precision=HIGH)
    factor = jnp.linalg.cholesky(gram)
    return jax.scipy.linalg.cho_solve((factor, True), basis)


def layer_norm(values, gain):
    centred = values - jnp.mean(values, -1, keepdims=True)
    spread = jnp.mean(centred * centred, -1, keepdims=True)
    return centred * lax.rsqrt(spread + 1e-06) * gain


def kernel_resize(kernel, patch):
    table = pinv_table(patch)
    shaped = kernel.reshape(3, BASE, BASE, -1)
    return jnp.einsum("ia,jb,cabd->cijd", table, table, shaped, precision=HIGH).reshape(
        3 * patch * patch, -1
    )


def grid_resize(position, row_table, grid):
    table = interp_matrix(grid, 7)
    return jnp.einsum(
        "ia,jb,abd->ijd", row_table, table, position.reshape(7, 7, -1), precision=HIGH
    )


def adamw(weight, first, second, grad, rate):
    first = 0.9 * first + 0.1 * grad
    second = 0.999 * second + 0.001 * grad * grad
    step_dir = first / (1.0 - 0.9**3) / (jnp.sqrt(second / (1.0 - 0.999**3)) + 1e-08)
    return (weight - rate * (step_dir + 0.1 * weight), first, second)


def attend(query, keys, values):
    scores = jnp.einsum(
        "ithe,ishe->ihts", query, keys, preferred_element_type=jnp.float32
    ) * HEAD_DIM ** (-0.5)
    norm_log = jax.nn.logsumexp(scores, -1, keepdims=True)
    probs = jnp.exp(scores - norm_log).astype(jnp.bfloat16)
    return (
        jnp.einsum("ihts,ishe->ithe", probs, values, preferred_element_type=jnp.float32),
        norm_log,
    )


def attend_back(query, keys, values, norm_log, d_out):
    scale = HEAD_DIM ** (-0.5)
    scores = jnp.einsum("ithe,ishe->ihts", query, keys, preferred_element_type=jnp.float32) * scale
    probs = jnp.exp(scores - norm_log)
    d_probs = jnp.einsum("ithe,ishe->ihts", d_out, values, preferred_element_type=jnp.float32)
    d_scores = (probs * (d_probs - jnp.sum(probs * d_probs, -1, keepdims=True))).astype(
        jnp.bfloat16
    )
    d_query = (
        jnp.einsum("ihts,ishe->ithe", d_scores, keys, preferred_element_type=jnp.float32) * scale
    )
    d_keys = (
        jnp.einsum("ihts,ithe->ishe", d_scores, query, preferred_element_type=jnp.float32) * scale
    )
    d_values = jnp.einsum(
        "ihts,ithe->ishe", probs.astype(jnp.bfloat16), d_out, preferred_element_type=jnp.float32
    )
    return (d_query, d_keys, d_values)


def grid_shape(size_sets, index):
    pixels = size_sets[index][0]
    return (pixels.shape[1], pixels.shape[2], -1)


AXES = ("z", "x", "core", "y")
CHIPS = ("z", "x", "y")
NT = (((1,), (1,)), ((), ()))
NN = (((1,), (0,)), ((), ()))
BF = jnp.bfloat16
F32 = jnp.float32
VMEM_BYTES = 58 << 20


def shift(value, axis, steps):
    count = lax.axis_size(axis)
    pairs = [(source, (source + steps) % count) for source in range(count)]
    return lax.ppermute(value, axis, pairs)


def chip_sizes():
    return tuple(lax.axis_size(axis) for axis in CHIPS)


def gather_rows(value, token=None):
    rows, cols = value.shape
    z, x, y = chip_sizes()
    chips = z * x * y
    copies = jnp.broadcast_to(value[None], (chips, rows, cols)).reshape(chips * rows, cols)
    mine = lax.all_to_all(copies, CHIPS, split_axis=0, concat_axis=0, tiled=True)
    mine = mine if token is None else after(mine, token)
    other = shift(mine, "core", 1)
    parts = [part.reshape(z, x, 1, y, rows, cols) for part in (mine, other)]
    first = lax.axis_index("core") == 0
    both = jnp.concatenate(
        [jnp.where(first, parts[0], parts[1]), jnp.where(first, parts[1], parts[0])], 2
    )
    return both.reshape(2 * chips * rows, cols)


def scatter_rows(away, own):
    z, x, y = chip_sizes()
    chips = z * x * y
    both = (own.astype(F32) + shift(away, "core", 1).astype(F32)).astype(BF)
    got = lax.all_to_all(both, CHIPS, split_axis=0, concat_axis=0, tiled=True)
    return jnp.sum(got.reshape(chips, own.shape[0] // chips, own.shape[1]).astype(F32), 0)


def store_by_core(core, acc, away_ref, own_ref, count):
    rows = acc.shape[0] // count // 2
    for pair in range(count):
        at = slice(pair * rows, (pair + 1) * rows)
        for side, ref in ((core, own_ref), (1 - core, away_ref)):
            first = pl.multiple_of((2 * pair + side) * rows, rows)
            ref[at, :] = acc[pl.ds(first, rows), :].astype(BF)


def interp_table(n_out, n_in):
    places = np.arange(n_out) * ((n_in - 1) / (n_out - 1))
    return np.maximum(0.0, 1.0 - np.abs(places[:, None] - np.arange(n_in)[None, :]))


def resize_table(patch):
    basis = interp_table(patch, BASE)
    table = np.linalg.solve(basis @ basis.T, basis)
    return np.kron(table, table).astype(np.float32)


def place_table(grid):
    table = interp_table(grid, 7)
    full = np.kron(table, table).astype(np.float32)
    high = full.astype(ml_dtypes.bfloat16)
    low = (full - high.astype(np.float32)).astype(ml_dtypes.bfloat16)
    return np.concatenate([high, low, np.zeros((grid * grid, 30), ml_dtypes.bfloat16)], 1)


def dot(left, right, dims):
    return lax.dot_general(left, right, dims, preferred_element_type=F32)


def estimate(flops, nbytes, share=32):
    return pl.CostEstimate(
        flops=int(flops) // share, bytes_accessed=int(nbytes) // share, transcendentals=0
    )


def normed(values):
    centred = values - jnp.mean(values, -1, keepdims=True)
    scale = lax.rsqrt(jnp.mean(centred * centred, -1, keepdims=True) + 1e-06)
    return centred * scale, scale


def norm_back(d_out, gain, hat, scale):
    d_hat = d_out * gain
    return scale * (
        d_hat
        - jnp.mean(d_hat, -1, keepdims=True)
        - hat * jnp.mean(d_hat * hat, -1, keepdims=True)
    )


def embed_kernel(*refs, pieces, at, depth, spot):
    pixel_refs, (tab_ref, weight_ref, gain_ref, *rest) = refs[:pieces], refs[pieces:]
    x0_ref, h1_ref = rest
    base = dot(tab_ref[...], weight_ref[:, spot : spot + tab_ref.shape[1]], NT)

    def body(pixel_ref):
        x0 = base + dot(pixel_ref[...], weight_ref[:, at : at + depth], NT)
        x0_ref[...] = x0
        h1_ref[...] = (normed(x0)[0] * gain_ref[...]).astype(BF)

    for piece, pixel_ref in enumerate(pixel_refs):
        pl.when(pl.program_id(1) == piece)(partial(body, pixel_ref))


def embed(pieces, tab, weight, at, spot, gain, images):
    count, depth = len(pieces), pieces[0].shape[1]
    block = tab.shape[0] // count
    rows, width = images * tab.shape[0], weight.shape[0]
    still = lambda array: pl.BlockSpec(array.shape, lambda i, j: (0, 0))
    moving = lambda cols: pl.BlockSpec((block, cols), lambda i, j: (i * count + j, 0))
    outs = [(width, F32), (width, BF)]
    return pl.pallas_call(
        partial(embed_kernel, pieces=count, at=at, depth=depth, spot=spot),
        out_shape=tuple(jax.ShapeDtypeStruct((rows, cols), kind) for cols, kind in outs),
        grid=(images, count),
        in_specs=[pl.BlockSpec((block, depth), lambda i, j: (i, 0))] * count
        + [pl.BlockSpec((block, tab.shape[1]), lambda i, j: (j, 0)), still(weight), still(gain)],
        out_specs=[moving(cols) for cols, _ in outs],
        compiler_params=pltpu.CompilerParams(vmem_limit_bytes=VMEM_BYTES),
        cost_estimate=estimate(2 * rows * width * width, rows * width * 8, 1),
        name="embed",
    )(*pieces, tab, weight, gain)


def head_split(first, values):
    zero = jnp.zeros((), values.dtype)
    return jnp.where(first, values, zero), jnp.where(first, zero, values)


def attend_pair(rows_ref, n_query, out_ref, log_ref, between=None):
    lane = lax.broadcasted_iota(jnp.int32, (1, 128), 1)
    first = lane < HEAD_DIM
    one = jnp.ones((), BF)
    values = rows_ref[:, 256:]
    keys = head_split(first, rows_ref[:, 128:256])
    sided = (jnp.where(first, values, one).T, jnp.where(first, one, values).T)
    query = rows_ref[:n_query, :128] * jnp.asarray(HEAD_DIM**-0.5, BF)
    scores = [dot(keys[head], query, NT) for head in range(2)]
    if between is not None:
        between()
    tops, probs, mixed = [], [], []
    for head in range(2):
        tops.append(jnp.max(scores[head], 0, keepdims=True))
        probs.append(jnp.exp(scores[head] - tops[head]).astype(BF))
        mixed.append(dot(sided[head], probs[head], NN))
    outs = []
    for head in range(2):
        at = HEAD_DIM * (1 - head)
        total = mixed[head][at : at + 1]
        own = HEAD_DIM * head
        outs.append(mixed[head][own : own + HEAD_DIM] / total)
        log_ref[0, 0, head : head + 1, :] = tops[head] + jnp.log(total)
    out_ref[...] = jnp.concatenate(outs, 0).T.astype(BF)


def attend_kernel(h1_ref, weight_ref, qkv_ref, out_ref, log_ref, held, *, items, n_query):
    step = pl.program_id(0)

    def project():
        rows = dot(h1_ref[...], weight_ref[...], NN).astype(BF)
        qkv_ref[...] = rows
        held[step % 2] = rows

    def attend(between=None):
        attend_pair(held.at[(step + 1) % 2], n_query, out_ref, log_ref, between)

    @pl.when(step == 0)
    def _():
        project()

    @pl.when((step > 0) & (step < items))
    def _():
        attend(project)

    @pl.when(step == items)
    def _():
        attend()


def attend_pairs(h1, weight, images, n_query):
    rows, width = h1.shape
    count = rows // images
    pairs = weight.shape[1] // 384
    items = images * pairs
    now = lambda s: jnp.minimum(s, items - 1)
    last = lambda s: jnp.maximum(s - 1, 0)
    return pl.pallas_call(
        partial(attend_kernel, items=items, n_query=n_query),
        out_shape=(
            jax.ShapeDtypeStruct((rows, pairs * 384), BF),
            jax.ShapeDtypeStruct((images * n_query, pairs * 128), BF),
            jax.ShapeDtypeStruct((images, pairs, 2, n_query), F32),
        ),
        grid=(items + 1,),
        in_specs=[
            pl.BlockSpec((count, width), lambda s: (now(s) // pairs, 0)),
            pl.BlockSpec((width, 384), lambda s: (0, now(s) % pairs)),
        ],
        out_specs=[
            pl.BlockSpec((count, 384), lambda s: (now(s) // pairs, now(s) % pairs)),
            pl.BlockSpec((n_query, 128), lambda s: (last(s) // pairs, last(s) % pairs)),
            pl.BlockSpec(
                (1, 1, 2, n_query), lambda s: (last(s) // pairs, last(s) % pairs, 0, 0)
            ),
        ],
        scratch_shapes=[pltpu.VMEM((2, count, 384), BF)],
        compiler_params=pltpu.CompilerParams(vmem_limit_bytes=VMEM_BYTES),
        cost_estimate=estimate(
            2 * items * count * (n_query * 1200 + width * 384), rows * width * 8, 1
        ),
        name="attend",
    )(h1, weight)


def attend_back_pair(q_ref, kv_ref, do_ref, o_ref, log_ref):
    lane = lax.broadcasted_iota(jnp.int32, (1, 128), 1)
    first = lane < HEAD_DIM
    scale = jnp.asarray(HEAD_DIM**-0.5, BF)
    keys_all = kv_ref[:, 128:256]
    keys = head_split(first, keys_all)
    values = head_split(first, kv_ref[:, 256:])
    query = q_ref[:, :128] * scale
    d_out = do_ref[...]
    queries = head_split(first, query)
    d_outs = head_split(first, d_out)
    keys_t = tuple(part.T for part in head_split(first, keys_all * scale))
    both = (d_out.astype(F32) * o_ref[...].astype(F32)).T
    d_query, d_keys, d_values = 0.0, 0.0, 0.0
    for head in range(2):
        row = jnp.sum(both[HEAD_DIM * head : HEAD_DIM * (head + 1)], 0, keepdims=True)
        scores = dot(keys[head], query, NT)
        probs = jnp.exp(scores - log_ref[0, 0, head : head + 1, :])
        d_probs = dot(values[head], d_out, NT)
        d_scores = (probs * (d_probs - row)).astype(BF)
        d_keys = d_keys + dot(d_scores, queries[head], NN)
        d_values = d_values + dot(probs.astype(BF), d_outs[head], NN)
        d_query = d_query + dot(keys_t[head], d_scores, NN)
    return d_query.astype(BF), d_keys.astype(BF), d_values.astype(BF)


def attend_back_kernel(q_ref, kv_ref, do_ref, o_ref, log_ref, d_ref):
    parts = attend_back_pair(q_ref, kv_ref, do_ref, o_ref, log_ref)
    rows = parts[0].shape[1]
    d_ref[:rows, :128] = parts[0].T
    d_ref[rows:, :128] = jnp.zeros((d_ref.shape[0] - rows, 128), BF)
    for index, part in enumerate(parts[1:], 1):
        d_ref[:, 128 * index : 128 * (index + 1)] = part


def attend_back_apart(query, keys, d_out, out, log, pairs, n_query, n_key):
    over_q = lambda cols: pl.BlockSpec((n_query, cols), lambda h: (0, h))
    over_k = lambda cols: pl.BlockSpec((n_key, cols), lambda h: (0, h))
    return pl.pallas_call(
        attend_back_kernel,
        out_shape=jax.ShapeDtypeStruct((n_key, pairs * 384), BF),
        grid=(pairs,),
        in_specs=[
            over_q(384),
            over_k(384),
            over_q(128),
            over_q(128),
            pl.BlockSpec((1, 1, 2, n_query), lambda h: (0, h, 0, 0)),
        ],
        out_specs=over_k(384),
        compiler_params=pltpu.CompilerParams(vmem_limit_bytes=VMEM_BYTES),
        cost_estimate=estimate(2 * pairs * n_query * n_key * 2400, (n_query + n_key) * pairs * 1024),
        name="attend_back_apart",
    )(query, keys, d_out, out, log)


def attend_back_grad_kernel(
    core_ref, qkv_ref, do_ref, o_ref, log_ref, h1_ref, h1_a_ref, d_a_ref,
    d_ref, away_ref, own_ref, acc, turned, *, images, blocks
):
    image = pl.program_id(1)

    @pl.when(image == 0)
    def _():
        acc[...] = dot(d_a_ref[...].T, h1_a_ref[...], NN)

    d_query, d_keys, d_values = attend_back_pair(qkv_ref, qkv_ref, do_ref, o_ref, log_ref)
    d_ref[:, :128] = d_query.T
    d_ref[:, 128:256] = d_keys
    d_ref[:, 256:] = d_values
    d_turned = jnp.concatenate([d_query, d_keys.T, d_values.T], 0)
    acc[...] += dot(d_turned, h1_ref[...], NN)

    @pl.when(image == images - 1)
    def _():
        turned[...] = acc[...].T
        store_by_core(core_ref[0], turned, away_ref, own_ref, blocks)


def attend_back_grad(qkv, d_out, out, log, h1, h1_a, d_a, core, pairs, images, count, blocks):
    width = h1.shape[1]
    rows_a = h1_a.shape[0]
    over = lambda cols: pl.BlockSpec((count, cols), lambda h, i: (i, h))
    grad = pl.BlockSpec((width // 2, 384), lambda h, i: (0, h))
    return pl.pallas_call(
        partial(attend_back_grad_kernel, images=images, blocks=blocks),
        out_shape=(
            jax.ShapeDtypeStruct((images * count, pairs * 384), BF),
            jax.ShapeDtypeStruct((width // 2, pairs * 384), BF),
            jax.ShapeDtypeStruct((width // 2, pairs * 384), BF),
        ),
        grid=(pairs, images),
        in_specs=[
            pl.BlockSpec(memory_space=pltpu.SMEM),
            over(384),
            over(128),
            over(128),
            pl.BlockSpec((1, 1, 2, count), lambda h, i: (i, h, 0, 0)),
            pl.BlockSpec((count, width), lambda h, i: (i, 0)),
            pl.BlockSpec((rows_a, width), lambda h, i: (0, 0)),
            pl.BlockSpec((rows_a, 384), lambda h, i: (0, h)),
        ],
        out_specs=[over(384), grad, grad],
        scratch_shapes=[
            pltpu.VMEM((384, width), F32),
            pltpu.VMEM((width, 384), F32),
        ],
        compiler_params=pltpu.CompilerParams(vmem_limit_bytes=VMEM_BYTES),
        cost_estimate=estimate(
            images * 2 * pairs * count * count * 2800, images * count * pairs * 2048
        ),
        name="attend_back",
    )(core, qkv, d_out, out, log, h1, h1_a, d_a)


def gelu_parts(inner):
    scaled = inner * (0.5**0.5)
    upper = 0.5 * lax.erf(scaled) + 0.5
    bell = jnp.exp2(scaled * scaled * -math.log2(math.e) - 0.5 * math.log2(2.0 * math.pi))
    return upper, inner * bell


def mlp_kernel(
    x0_ref, mixed0_ref, mixed1_ref, wout_ref, gain_ref, wup_ref,
    x1_ref, slope_ref, xsum_ref, asum_ref, *, per
):
    mixed = jnp.concatenate([mixed0_ref[...], mixed1_ref[...]], 1)
    x1 = x0_ref[...] + dot(mixed, wout_ref[...], NN)
    x1_ref[...] = x1
    h2 = (normed(x1)[0] * gain_ref[...]).astype(BF)

    @pl.when(pl.program_id(0) % per == 0)
    def _():
        xsum_ref[...] = jnp.zeros_like(xsum_ref)
        asum_ref[...] = jnp.zeros_like(asum_ref)

    xsum_ref[0] += jnp.sum(x1, 0, keepdims=True)
    width = 512
    for first in range(0, wup_ref.shape[1], width):
        cols = slice(first, first + width)
        inner = dot(h2, wup_ref[:, cols], NN)
        upper, slope = gelu_parts(inner)
        slope_ref[:, cols] = (upper + slope).astype(BF)
        asum_ref[0, :, cols] += jnp.sum(inner * upper, 0, keepdims=True)


def mlp(x0, mixed, w_up_out, gain, images, block):
    rows, width = x0.shape
    hidden = w_up_out.shape[1] - width
    per = rows // images // block
    return pl.pallas_call(
        partial(mlp_kernel, per=per),
        out_shape=(
            jax.ShapeDtypeStruct((rows, width), F32),
            jax.ShapeDtypeStruct((rows, hidden), BF),
            jax.ShapeDtypeStruct((images, 1, width), F32),
            jax.ShapeDtypeStruct((images, 1, hidden), F32),
        ),
        grid=(rows // block,),
        in_specs=[
            pl.BlockSpec((block, width), lambda i: (i, 0)),
            pl.BlockSpec((block, width // 2), lambda i: (i, 0)),
            pl.BlockSpec((block, width // 2), lambda i: (i, 0)),
            pl.BlockSpec((width, width), lambda i: (0, hidden // width)),
            pl.BlockSpec((1, width), lambda i: (0, 0)),
            pl.BlockSpec((width, hidden), lambda i: (0, 0)),
        ],
        out_specs=[
            pl.BlockSpec((block, width), lambda i: (i, 0)),
            pl.BlockSpec((block, hidden), lambda i: (i, 0)),
            pl.BlockSpec((1, 1, width), lambda i: (i // per, 0, 0)),
            pl.BlockSpec((1, 1, hidden), lambda i: (i // per, 0, 0)),
        ],
        compiler_params=pltpu.CompilerParams(vmem_limit_bytes=VMEM_BYTES),
        cost_estimate=estimate(4 * rows * width * (hidden + width), rows * hidden * 4),
        name="mlp",
    )(x0, *mixed, w_up_out, gain, w_up_out)


def head_kernel(
    xsum_ref, asum_ref, sums_a_ref, down_ref, head_ref, label_ref, alive_ref, once_ref, whole_ref,
    total_ref, loss_ref, rows_ref, dx2_ref, dact_ref, *, classes, own
):
    width, hidden = down_ref.shape
    fill = loss_ref.shape[0] - own - 1

    def stacked(ref, cols):
        rows = [ref[image] for image in range(own)] + [sums_a_ref[:, cols]]
        return jnp.concatenate(rows + [jnp.zeros((fill, rows[0].shape[1]), F32)], 0)

    xsum = stacked(xsum_ref, slice(0, width))
    asum = stacked(asum_ref, slice(width, width + hidden))
    high = asum.astype(BF)
    low = (asum - high.astype(F32)).astype(BF)
    whole = whole_ref[...]
    down = down_ref[...]
    pooled = (xsum + (dot(high, down, NT) + dot(low, down, NT))) / whole
    pooled_low = pooled.astype(BF)
    head = head_ref[...]
    place = lax.broadcasted_iota(jnp.int32, (1, head.shape[1]), 1)
    logits = jnp.where(place < classes, dot(pooled_low, head, NN), -1e30)
    top = jnp.max(logits, -1, keepdims=True)
    norm_log = top + jnp.log(jnp.sum(jnp.exp(logits - top), -1, keepdims=True))
    hot = place == label_ref[...]
    true_logit = jnp.sum(jnp.where(hot, logits, 0.0), -1, keepdims=True)
    loss_ref[...] = jnp.broadcast_to(norm_log - true_logit, loss_ref.shape)
    soft = jnp.exp(logits - norm_log) - hot.astype(F32)
    d_logits = (soft * alive_ref[...] / total_ref[...]).astype(BF)
    d_x2 = dot(d_logits, head, NT) / whole
    d_mix = d_x2.astype(BF)
    d_act = dot(d_mix, down, NN)
    for image in range(own + 1):
        dx2_ref[image] = d_x2[image : image + 1]
        dact_ref[image] = d_act[image : image + 1]
    once = once_ref[...]
    rows_ref[:, :hidden] = high
    rows_ref[:, hidden : hidden + width] = pooled_low
    rows_ref[:, hidden + width : hidden + 2 * width] = (d_mix * once).astype(BF)
    rows_ref[:, hidden + 2 * width :] = (d_logits * once).astype(BF)


def head_step(xsum, asum, sums_a, w_down_head, labels, alive, once, whole, total, classes):
    own, _, width = xsum.shape
    hidden = asum.shape[2]
    rows = labels.shape[0]
    padded = w_down_head.shape[1] - hidden
    spec = lambda shape, *place: pl.BlockSpec(shape, lambda i: place or (0,) * len(shape))
    shapes = (
        ((rows, 128), F32),
        ((rows, hidden + 2 * width + padded), BF),
        ((own + 1, 1, width), F32),
        ((own + 1, 1, hidden), F32),
    )
    return pl.pallas_call(
        partial(head_kernel, classes=classes, own=own),
        out_shape=tuple(jax.ShapeDtypeStruct(*shape) for shape in shapes),
        grid=(1,),
        in_specs=[
            spec(xsum.shape),
            spec(asum.shape),
            spec(sums_a.shape),
            spec((width, hidden), 0, 0),
            spec((width, padded), 0, hidden // padded),
            spec((rows, 1)),
            spec((rows, 1)),
            spec((rows, 1)),
            spec((rows, 1)),
            spec((1, 1)),
        ],
        out_specs=[spec(shape[0]) for shape in shapes],
        compiler_params=pltpu.CompilerParams(vmem_limit_bytes=VMEM_BYTES),
        cost_estimate=estimate(1 << 32, 8 << 20),
        name="head",
    )(xsum, asum, sums_a, w_down_head, w_down_head, labels, alive, once, whole, total)


def mlp_back_kernel(*refs, steps):
    parts = (refs[0:6], refs[6:12])
    wout_ref, gain_ref, wup_ref = refs[12:15]
    outs = (refs[15:18], refs[18:21])
    grad_ref, ggain_ref = refs[21:23]
    up_acc, out_acc = refs[23:25]
    step = pl.program_id(0)

    def body(inputs, outputs, begin):
        slope_ref, dact_ref, x1_ref, dx2_ref, *mixed_refs = inputs
        dx1_ref, *dmixed_refs = outputs
        gain = gain_ref[...]
        hat, scale = normed(x1_ref[...])
        h2_t = (hat * gain).astype(BF).T
        d_h2 = 0.0
        width = 768
        for first in range(0, slope_ref.shape[1], width):
            cols = slice(first, first + width)
            d_inner = (slope_ref[:, cols].astype(F32) * dact_ref[0, :, cols]).astype(BF)
            d_h2 = d_h2 + dot(d_inner, wup_ref[:, cols], NT)
            grad = dot(h2_t, d_inner, NN)
            up_acc[:, cols] = grad if begin else up_acc[:, cols] + grad
        gain_grad = jnp.sum(d_h2 * hat, 0, keepdims=True)
        ggain_ref[...] = gain_grad if begin else ggain_ref[...] + gain_grad
        d_x1 = dx2_ref[0] + norm_back(d_h2, gain, hat, scale)
        dx1_ref[...] = d_x1
        d_attn = d_x1.astype(BF)
        mixed = jnp.concatenate([mixed_ref[...] for mixed_ref in mixed_refs], 1)
        grad = dot(mixed.T, d_attn, NN)
        out_acc[...] = grad if begin else out_acc[...] + grad
        d_mixed = dot(d_attn, wout_ref[...], NT).astype(BF)
        half = mixed_refs[0].shape[1]
        for index, dmixed_ref in enumerate(dmixed_refs):
            dmixed_ref[...] = d_mixed[:, index * half : (index + 1) * half]

    @pl.when(step == 0)
    def _():
        body(parts[1], outs[1], True)

    @pl.when(step > 0)
    def _():
        body(parts[0], outs[0], False)

    @pl.when(step == steps)
    def _():
        hidden = up_acc.shape[1]
        grad_ref[:, :hidden] = up_acc[...].astype(BF)
        grad_ref[:, hidden:] = out_acc[...].astype(BF)


def mlp_back(part_b, part_a, w_up_out, gain, images, block):
    rows, width = part_b[2].shape
    rows_a = part_a[2].shape[0]
    hidden = part_b[0].shape[1]
    steps = rows // block
    per = steps // images
    at = lambda i: jnp.maximum(i - 1, 0)
    moving = lambda cols: pl.BlockSpec((block, cols), lambda i: (at(i), 0))
    still = lambda shape: pl.BlockSpec(shape, lambda i: (0,) * len(shape))
    image = lambda cols: pl.BlockSpec((1, 1, cols), lambda i: (at(i) // per, 0, 0))
    last = lambda cols: pl.BlockSpec((1, 1, cols), lambda i: (images, 0, 0))
    half = width // 2
    outs = []
    for count in (rows, rows_a):
        outs += [
            jax.ShapeDtypeStruct((count, width), F32),
            jax.ShapeDtypeStruct((count, half), BF),
            jax.ShapeDtypeStruct((count, half), BF),
        ]
    return pl.pallas_call(
        partial(mlp_back_kernel, steps=steps),
        out_shape=(
            *outs,
            jax.ShapeDtypeStruct((width, hidden + width), BF),
            jax.ShapeDtypeStruct((1, width), F32),
        ),
        grid=(steps + 1,),
        in_specs=[
            moving(hidden), image(hidden), moving(width), image(width), moving(half), moving(half),
            still((rows_a, hidden)), last(hidden), still((rows_a, width)),
            last(width), still((rows_a, half)), still((rows_a, half)),
            pl.BlockSpec((width, width), lambda i: (0, hidden // width)),
            still((1, width)),
            still((width, hidden)),
        ],
        out_specs=[
            moving(width), moving(half), moving(half),
            still((rows_a, width)), still((rows_a, half)), still((rows_a, half)),
            still((width, hidden + width)), still((1, width)),
        ],
        scratch_shapes=[pltpu.VMEM((width, hidden), F32), pltpu.VMEM((width, width), F32)],
        compiler_params=pltpu.CompilerParams(vmem_limit_bytes=VMEM_BYTES),
        cost_estimate=estimate(
            4 * (rows + rows_a) * width * (hidden + width), (rows + rows_a) * hidden * 4
        ),
        name="mlp_back",
    )(*part_b, *part_a, w_up_out, gain, w_up_out)


def embed_back_kernel(core_ref, *refs, steps, groups, pieces, blocks, parts_b):
    n_b, n_a = 3 + pieces + groups, 4 + groups
    inputs_b, inputs_a = refs[:n_b], refs[n_b : n_b + n_a]
    gain_ref, gain_grad_ref, *rest = refs[n_b + n_a :]
    weight_refs = rest[:groups]
    away_ref, own_ref, acc_b, acc_a, acc_tab, gain_acc = rest[groups:]
    step = pl.program_id(0)

    def body(inputs, acc, parts, pixel_ref):
        x0_ref, dx1_ref, tab_ref = inputs[:3]
        gain = gain_ref[...]
        count = x0_ref.shape[0] // parts
        turned = []
        for part in range(parts):
            rows = slice(part * count, (part + 1) * count)
            hat, scale = normed(x0_ref[rows])
            d_h1 = 0.0
            for ref, weight_ref in zip(inputs[-groups:], weight_refs):
                d_h1 = d_h1 + dot(ref[rows], weight_ref[...], NT)
            gain_acc[0:1] += jnp.sum(d_h1 * hat, 0, keepdims=True)
            d_x0 = dx1_ref[rows] + norm_back(d_h1, gain, hat, scale)
            turned.append(d_x0.astype(BF).T)
        turned = jnp.concatenate(turned, 1)
        acc_tab[...] += dot(turned, tab_ref[...], NN)
        acc[:, : pixel_ref.shape[1]] += dot(turned, pixel_ref[...], NN)

    @pl.when(step == 0)
    def _():
        for acc in (acc_b, acc_a, acc_tab, gain_acc):
            acc[...] = jnp.zeros_like(acc)
        gain_acc[1:2] = gain_grad_ref[...]
        body(inputs_a, acc_a, 1, inputs_a[3])

    for piece in range(pieces):

        @pl.when((step > 0) & ((step - 1) % pieces == piece))
        def _(piece=piece):
            body(inputs_b, acc_b, parts_b, inputs_b[3 + piece])

    @pl.when(step == steps)
    def _():
        place = lax.broadcasted_iota(jnp.int32, (8, 128), 1)
        row = lax.broadcasted_iota(jnp.int32, (8, 128), 0)
        spots = jnp.where((place == 126 + row) & (row < 2), 1.0, 0.0).astype(BF)
        acc_tab[...] += lax.dot_general(
            gain_acc[...].astype(BF), spots, ROWS_DIM, preferred_element_type=F32
        )
        at = 0
        for acc in (acc_b, acc_a, acc_tab):
            cols = slice(at, at + acc.shape[1])
            at += acc.shape[1]
            store_by_core(core_ref[0], acc, away_ref.at[:, cols], own_ref.at[:, cols], blocks)


def embed_back(
    x0_b, dx1_b, tab_b, pixels_b, d_b, x0_a, dx1_a, tab_a, pixels_a, d_a, gain, gain_grad, w_qkv,
    core, blocks, images, depths
):
    rows, width = x0_b.shape
    pieces = len(pixels_b)
    steps = images * pieces
    block = rows // steps
    at = lambda i: jnp.maximum(i - 1, 0)
    moving = lambda array: pl.BlockSpec((block, array.shape[1]), lambda i: (at(i), 0))
    still = lambda shape: pl.BlockSpec(shape, lambda i: (0,) * len(shape))
    inputs_a = (x0_a, dx1_a, tab_a, pixels_a, *d_a)
    grad = (width // 2, sum(depths) + 128)
    return pl.pallas_call(
        partial(
            embed_back_kernel, steps=steps, groups=len(d_b), pieces=pieces, blocks=blocks,
            parts_b=max(1, block // 256),
        ),
        out_shape=(jax.ShapeDtypeStruct(grad, BF), jax.ShapeDtypeStruct(grad, BF)),
        grid=(steps + 1,),
        in_specs=[pl.BlockSpec(memory_space=pltpu.SMEM)]
        + [moving(x0_b), moving(dx1_b)]
        + [pl.BlockSpec((block, 128), lambda i: (at(i) % pieces, 0))]
        + [
            pl.BlockSpec((block, array.shape[1]), lambda i: (at(i) // pieces, 0))
            for array in pixels_b
        ]
        + [moving(array) for array in d_b]
        + [still(array.shape) for array in inputs_a]
        + [still((1, width)), still((1, width))]
        + [still(weight.shape) for weight in w_qkv],
        out_specs=[still(grad), still(grad)],
        scratch_shapes=[pltpu.VMEM((width, depth), F32) for depth in (*depths, 128)]
        + [pltpu.VMEM((8, width), F32)],
        compiler_params=pltpu.CompilerParams(vmem_limit_bytes=VMEM_BYTES),
        cost_estimate=estimate(2 * rows * width * (3 * width + 640), rows * 10000),
        name="embed_back",
    )(core, x0_b, dx1_b, tab_b, *pixels_b, *d_b, *inputs_a, gain, gain_grad, *w_qkv)


def after(value, *others):
    return lax.optimization_barrier((value, *others))[0]


def padded_cols(array, width):
    return jnp.pad(array, ((0, 0), (0, width - array.shape[1])))


def round_up(count, unit):
    return -(-count // unit) * unit


def fast_step(
    pixels_a, pixels_b, labels_a, labels_b, live_a, live_b, masters, firsts, seconds
):
    qkv_w, out_w, mlp_w, kern_w, pos_w, head_w, gains = masters
    seq = lax.axis_size("y")
    row = lax.axis_index("y")
    count_all = seq * lax.axis_size("z") * lax.axis_size("x") * 2
    flat_index = lax.axis_index(AXES)
    lead = (row == 0).astype(F32)
    width = HEADS * HEAD_DIM
    hidden = mlp_w.shape[2]
    classes = head_w.shape[1]
    classes_up = round_up(classes, 1024)
    rows_own = qkv_w.shape[0]
    rows_kern = kern_w.shape[0]
    groups = 2
    span = width // groups
    pairs = span // 128

    images_a, rows_a, grid_a, depth_a = pixels_a.shape
    images_b, rows_b, grid_b, depth_b = pixels_b.shape
    own_b = images_b // seq
    parts_b, tabs_b, slices = [], [], []
    table_b = jnp.asarray(place_table(grid_b))
    table_a = jnp.asarray(place_table(grid_a))
    span_b, span_a = rows_b * grid_b, rows_a * grid_a
    for step in range(seq):
        part = lax.dynamic_slice_in_dim(
            pixels_b, ((row + step) % seq) * own_b, own_b, 0
        )
        part = part.reshape(own_b * rows_b * grid_b, depth_b)
        slices.append(part)
        parts_b.append(shift(part, "y", step) if step else part)
        tabs_b.append(lax.dynamic_slice_in_dim(table_b, ((row - step) % seq) * span_b, span_b, 0))
    tab_a = lax.dynamic_slice_in_dim(table_a, row * span_a, span_a, 0)
    whole_a, whole_b = grid_a * grid_a, grid_b * grid_b

    alive_a = live_a.astype(F32)[:, None]
    counts = jnp.stack([lead * jnp.sum(alive_a), lead * jnp.sum(live_b.astype(F32))]).astype(BF)
    lanes = round_up(rows_kern + 2, 128)
    sent = jnp.concatenate(
        [
            kern_w.astype(BF).T,
            jnp.broadcast_to(counts[None], (width, 2)),
            jnp.zeros((width, lanes - rows_kern - 2), BF),
        ],
        1,
    )
    sent = after(sent, *slices)
    got = lax.all_to_all(sent, AXES, split_axis=0, concat_axis=0, tiled=True)
    got, tab_a, tab_b, *parts_b = lax.optimization_barrier(
        (got, tab_a, jnp.concatenate(tabs_b, 0), *parts_b)
    )
    got = got.reshape(count_all, rows_own, lanes)
    counts = got[:, 0, rows_kern : rows_kern + 2]
    got = got.astype(F32)
    kern_cols = got[:, :, :rows_kern].transpose(1, 0, 2).reshape(rows_own, 3, BASE * BASE)

    def group_cols(array, group):
        shaped = array.reshape(rows_own, 3, groups, pairs, 128)[:, :, group]
        return shaped.transpose(0, 2, 1, 3).reshape(rows_own, 3 * span)

    qkv_low = qkv_w.astype(BF)
    w_groups = [lax.all_gather(group_cols(qkv_low, 0), AXES, axis=0, tiled=True)]

    tables = [resize_table(PATCH_B), resize_table(PATCH_A)]
    sizes = [3 * table.shape[0] for table in tables]
    resized = [
        jnp.einsum("dck,pk->dcp", kern_cols, jnp.asarray(table), precision=HIGH).reshape(
            rows_own, -1
        )
        for table in tables
    ]
    depths = [round_up(size, 128) for size in sizes]
    spot = sum(depths)
    pos_t = pos_w.astype(BF).T
    edge = jnp.zeros((rows_own, 28), BF)
    small = jnp.concatenate(
        [padded_cols(piece.astype(BF), depth) for piece, depth in zip(resized, depths)]
        + [pos_t, pos_t, edge, gains.astype(BF).T],
        1,
    )
    w_small = gather_rows(small)
    second = group_cols(qkv_low, 1)
    w_up_out = lax.all_gather(
        after(jnp.concatenate([mlp_w[0].astype(BF), out_w.astype(BF)], 1), got),
        AXES, axis=0, tiled=True,
    )
    w_down_head = lax.all_gather(
        after(
            jnp.concatenate([mlp_w[1].astype(BF), padded_cols(head_w.astype(BF), classes_up)], 1),
            w_small,
        ),
        AXES, axis=0, tiled=True,
    )

    gain_rows = w_small[:, spot + 126 :].T.astype(F32)
    gain1, gain2 = gain_rows[0:1], gain_rows[1:2]
    flat_a = pixels_a.reshape(span_a, depth_a)
    block = min(512, whole_b)
    x0_a, h1_a = embed([flat_a], tab_a, w_small, depths[0], spot, gain1, 1)
    h1_all = jnp.concatenate([h1_a] + [shift(h1_a, "y", step) for step in range(1, seq)], 0)
    x0_b, h1_b = embed(
        [after(parts_b[0], h1_a), *parts_b[1:]], tab_b, w_small, 0, spot, gain1, own_b
    )
    h1_b, h1_all = lax.optimization_barrier((h1_b, h1_all))
    outs_a, outs_b = [], []
    ready = h1_b
    for group in range(groups):
        if group:
            w_groups.append(gather_rows(after(second, h1_a), ready))
        outs_b.append(attend_pairs(after(h1_b, ready), w_groups[group], own_b, whole_b))
        ready = outs_b[-1][0]
    for group in range(groups):
        outs_a.append(attend_pairs(after(h1_all, ready), w_groups[group], 1, span_a))
    qkvs_a, qkvs_b = [out[0] for out in outs_a], [out[0] for out in outs_b]
    mixed_a, mixed_b = [out[1] for out in outs_a], [out[1] for out in outs_b]

    x1_a, slope_a, xsum_a, asum_a = mlp(x0_a, mixed_a, w_up_out, gain2, 1, span_a)
    sums_a = jnp.concatenate([xsum_a[0], asum_a[0]], 1)
    sums_a = sum([shift(sums_a, "y", step) for step in range(1, seq)], sums_a)
    x1_b, slope_b, xsum_b, asum_b = mlp(after(x0_b, x1_a), mixed_b, w_up_out, gain2, own_b, block)

    counts, labels_a, labels_b, live_b, alive_a = lax.optimization_barrier(
        (counts, labels_a, labels_b, live_b, alive_a, h1_b)
    )[:5]
    count = jnp.sum(counts.astype(F32), 0, keepdims=True)
    total = jnp.maximum(jnp.sum(count), 1.0)
    rows_up = round_up(own_b + 1, 8)
    fill = rows_up - own_b - 1
    stack = lambda first, last: jnp.pad(
        jnp.concatenate([first, last], 0), ((0, fill), (0, 0))
    )
    mine = lambda array: lax.dynamic_slice_in_dim(array, row * own_b, own_b, 0)[:, None]
    labels = stack(mine(labels_b), labels_a[:, None])
    alive_b = mine(live_b).astype(F32)
    alive = stack(alive_b, alive_a)
    once = stack(jnp.ones((own_b, 1), F32), lead.reshape(1, 1))
    whole = np.ones((rows_up, 1), np.float32)
    whole[:own_b], whole[own_b] = whole_b, whole_a
    losses, rows_out, d_x2, d_act = head_step(
        xsum_b, asum_b, sums_a, w_down_head, labels, alive, once, jnp.asarray(whole),
        total.reshape(1, 1), classes,
    )
    loss_sums = jnp.stack(
        [lead * jnp.sum(alive_a * losses[own_b : own_b + 1, :1]),
         jnp.sum(alive_b * losses[:own_b, :1])]
    )

    image_rows = lax.all_gather(rows_out[: round_up(own_b + 1, 4)], AXES, axis=0, tiled=True)

    d_x1_b, d0_b, d1_b, d_x1_a, d0_a, d1_a, grad_up_out, grad_gain2 = mlp_back(
        (slope_b, d_act, x1_b, d_x2, *mixed_b),
        (slope_a, d_act, x1_a, d_x2, *mixed_a),
        w_up_out, gain2, own_b, block,
    )
    d_mixed_a, d_mixed_b = (d0_a, d1_a), (d0_b, d1_b)

    d_alls, d_groups_a = [], []
    for group in range(groups):
        d_all = attend_back_apart(
            qkvs_a[group], qkvs_a[group], d_mixed_a[group], mixed_a[group],
            outs_a[group][2], pairs, span_a, seq * span_a,
        )
        own = d_all[:span_a].astype(F32)
        for step in range(1, seq):
            own = own + shift(
                d_all[step * span_a : (step + 1) * span_a], "y", seq - step
            ).astype(F32)
        d_alls.append(d_all)
        d_groups_a.append(own.astype(BF))
    own_up_out = lax.psum_scatter(
        after(grad_up_out, image_rows, *d_alls), AXES, scatter_dimension=0, tiled=True
    ).astype(F32)
    core = lax.axis_index("core").reshape(1).astype(jnp.int32)
    blocks = lax.axis_size("z") * lax.axis_size("x")
    d_groups_b, own_groups = [], []
    ready = d_alls[-1]
    for group in range(groups):
        got, away, own = attend_back_grad(
            qkvs_b[group],
            after(d_mixed_b[group], ready),
            mixed_b[group], outs_b[group][2],
            h1_b, h1_all, d_alls[group], core, pairs, own_b, whole_b, blocks,
        )
        if group:
            away, own, own_groups[-1] = lax.optimization_barrier((away, own, own_groups[-1]))
        else:
            away, own, *d_groups_a = lax.optimization_barrier((away, own, *d_groups_a))
        d_groups_b.append(got)
        own_groups.append(scatter_rows(away, own))
        ready = got
    away, own = embed_back(
        x0_b, after(d_x1_b, ready), tab_b, parts_b, d_groups_b,
        x0_a, d_x1_a, tab_a, flat_a, d_groups_a,
        gain1, grad_gain2, w_groups, core, blocks, own_b, depths,
    )
    away, own, own_up_out, *own_groups = lax.optimization_barrier(
        (away, own, own_up_out, *own_groups)
    )
    own_qkv = jnp.stack(own_groups, 1).reshape(rows_own, groups * pairs, 3, 128)
    own_qkv = own_qkv.transpose(0, 2, 1, 3).reshape(rows_own, 3 * width)
    own_small = scatter_rows(away, own)
    kern_t = jnp.zeros((rows_own, 3, BASE * BASE), F32)
    for table, size, at in zip(tables, sizes, (0, depths[0])):
        piece = own_small[:, at : at + size].reshape(rows_own, 3, -1)
        kern_t = kern_t + jnp.einsum("dcp,pk->dck", piece, jnp.asarray(table), precision=HIGH)
    own_pos = own_small[:, spot : spot + 49] + own_small[:, spot + 49 : spot + 98]
    kern_t = kern_t.reshape(rows_own, count_all, rows_kern)
    own_pos = own_pos.T
    own_gain = own_small[:, -2:].T

    columns = lambda lo: lax.dynamic_slice_in_dim(
        image_rows[:, lo : lo + width], flat_index * rows_own, rows_own, 1
    )
    own_down = lax.dot_general(
        columns(hidden + width), image_rows[:, :hidden], ROWS_DIM, preferred_element_type=F32
    )
    own_head = lax.dot_general(
        columns(hidden),
        image_rows[:, hidden + 2 * width : hidden + 2 * width + classes],
        ROWS_DIM,
        preferred_element_type=F32,
    )
    own_up, own_out = own_up_out[:, :hidden], own_up_out[:, hidden:]
    square_sum = sum(
        jnp.sum(piece * piece)
        for piece in (own_up_out, own_down, own_head, own_qkv, kern_t, own_pos, own_gain)
    )

    sums = jnp.concatenate([square_sum.reshape(1), loss_sums])
    sent = jnp.concatenate(
        [
            kern_t.transpose(1, 0, 2),
            jnp.broadcast_to(sums[None, None], (count_all, rows_own, 3)),
            jnp.zeros((count_all, rows_own, lanes - rows_kern - 3), F32),
        ],
        2,
    )
    got = lax.all_to_all(sent, AXES, split_axis=0, concat_axis=0, tiled=True)
    own_kern = got[:, :, :rows_kern].reshape(count_all * rows_own, rows_kern).T
    sums = jnp.sum(got[:, 0, rows_kern : rows_kern + 3], 0)
    grad_norm = jnp.sqrt(sums[0])
    factor = jnp.minimum(1.0, CLIP / (grad_norm + 1e-06))
    own_mlp = jnp.stack([own_up, own_down], 0)
    owned = (own_qkv, own_out, own_mlp, own_kern, own_pos, own_head, own_gain)
    done = [adamw(masters[i], firsts[i], seconds[i], owned[i] * factor, RATES[i]) for i in range(7)]
    size_stats = sums[1:] / jnp.maximum(count[0], 1.0)
    return (
        *(item[0] for item in done),
        *(item[1] for item in done),
        *(item[2] for item in done),
        size_stats,
        grad_norm,
    )


def fits_fast(mesh, pixels_a, pixels_b):
    dp, seq = mesh.shape["dp"], mesh.shape["seq"]
    images_b, rows_b, grid_b, _ = pixels_b.shape
    rows_a, grid_a = pixels_a.shape[1:3]
    return (
        dp % 8 == 0
        and rows_b % seq == 0
        and rows_a % seq == 0
        and images_b % (dp * seq) == 0
        and images_b // dp <= 256
        and pixels_a.shape[0] == dp
        and grid_b * grid_b % 256 == 0
        and rows_a // seq * grid_a % 32 == 0
    )


def fast_on_device(*args):
    return fast_step(*args[:6], args[6:13], args[13:20], args[20:27])


def on_device(
    pixels_a,
    pixels_b,
    labels_a,
    labels_b,
    live_a,
    live_b,
    qkv_w,
    out_w,
    mlp_w,
    kern_w,
    pos_w,
    head_w,
    gains,
    qkv_m,
    out_m,
    mlp_m,
    kern_m,
    pos_m,
    head_m,
    gains_m,
    qkv_v,
    out_v,
    mlp_v,
    kern_v,
    pos_v,
    head_v,
    gains_v,
):
    masters = (qkv_w, out_w, mlp_w, kern_w, pos_w, head_w, gains)
    firsts = (qkv_m, out_m, mlp_m, kern_m, pos_m, head_m, gains_m)
    seconds = (qkv_v, out_v, mlp_v, kern_v, pos_v, head_v, gains_v)
    bf16 = jnp.bfloat16
    w_qkv, w_out, w_mlp, w_kern, w_pos, w_head, w_gain = (
        lax.all_gather(qkv_w.astype(bf16), ("dp", "seq"), axis=0, tiled=True),
        lax.all_gather(out_w.astype(bf16), ("dp", "seq"), axis=0, tiled=True),
        lax.all_gather(mlp_w.astype(bf16), ("dp", "seq"), axis=1, tiled=True),
        lax.all_gather(kern_w.astype(bf16), ("dp", "seq"), axis=0, tiled=True),
        lax.all_gather(pos_w.astype(bf16), ("dp", "seq"), axis=1, tiled=True),
        lax.all_gather(head_w.astype(bf16), ("dp", "seq"), axis=0, tiled=True),
        lax.all_gather(gains.astype(bf16), ("dp", "seq"), axis=1, tiled=True),
    )
    seq_count = lax.axis_size("seq")
    seq_place = lax.axis_index("seq")
    gain_full = w_gain.astype(jnp.float32)
    kern_full = w_kern.astype(jnp.float32)
    pos_full = w_pos.astype(jnp.float32)
    size_sets = ((pixels_a, labels_a, live_a, PATCH_A), (pixels_b, labels_b, live_b, PATCH_B))
    embeds, flats, kern_backs, pos_backs, layouts = ([], [], [], [], [])
    start = 0
    for pixels, labels, live, patch in size_sets:
        images, rows, grid, depth = pixels.shape
        flat = pixels.reshape(images * rows * grid, depth)
        resized, kern_back = jax.vjp(partial(kernel_resize, patch=patch), kern_full)
        row_table = lax.dynamic_slice_in_dim(interp_matrix(grid, 7), seq_place * rows, rows, 0)
        place, pos_back = jax.vjp(partial(grid_resize, row_table=row_table, grid=grid), pos_full)
        embed = jnp.dot(flat, resized.astype(bf16), preferred_element_type=jnp.float32)
        embed = embed.reshape(images, rows * grid, -1) + place.reshape(1, rows * grid, -1)
        embeds.append(embed.reshape(images * rows * grid, -1))
        flats.append(flat)
        kern_backs.append(kern_back)
        pos_backs.append(pos_back)
        layouts.append((start, start + images * rows * grid, images, rows * grid, grid * grid))
        start = start + images * rows * grid
    x0 = jnp.concatenate(embeds, 0)
    h1_full, norm1_back = jax.vjp(layer_norm, x0, gain_full[0])
    h1 = h1_full.astype(bf16)
    qkv = jnp.dot(h1, w_qkv, preferred_element_type=jnp.float32).astype(bf16)
    width = qkv.shape[1] // 3
    local_kv = qkv[:, width:]
    blocks = [local_kv]
    moving = local_kv
    for turn in range(1, seq_count):
        moving = from_behind(moving, "seq", 1)
        blocks.append(moving)
    all_kv = jnp.stack(blocks, 0)
    mixed_parts, saved = ([], [])
    for first_row, last_row, images, length, whole in layouts:
        query = qkv[first_row:last_row, :width].reshape(images, length, HEADS, HEAD_DIM)
        remote = all_kv[:, first_row:last_row].reshape(
            seq_count, images, length, 2, HEADS, HEAD_DIM
        )
        remote = remote.transpose(1, 0, 2, 3, 4, 5).reshape(
            images, seq_count * length, 2, HEADS, HEAD_DIM
        )
        keys, values = (remote[:, :, 0], remote[:, :, 1])
        attended, norm_log = attend(query, keys, values)
        mixed_parts.append(attended.reshape(last_row - first_row, width))
        saved.append((query, keys, values, norm_log))
    mixed = jnp.concatenate(mixed_parts, 0).astype(bf16)
    x1 = x0 + jnp.dot(mixed, w_out, preferred_element_type=jnp.float32)
    h2_full, norm2_back = jax.vjp(layer_norm, x1, gain_full[1])
    h2 = h2_full.astype(bf16)
    inner = jnp.dot(h2, w_mlp[0], preferred_element_type=jnp.float32)
    act_full, gelu_back = jax.vjp(partial(jax.nn.gelu, approximate=False), inner)
    act = act_full.astype(bf16)
    x2 = x1 + lax.dot_general(act, w_mlp[1], COLS_DIM, preferred_element_type=jnp.float32)
    sum_a = x2[layouts[0][0] : layouts[0][1]].reshape(layouts[0][2], layouts[0][3], -1).sum(1)
    sum_b = x2[layouts[1][0] : layouts[1][1]].reshape(layouts[1][2], layouts[1][3], -1).sum(1)
    pooled_sums = lax.psum((sum_a, sum_b), "seq")
    stats, head_parts = ([], [])
    for index in range(2):
        labels, live = (size_sets[index][1], size_sets[index][2])
        pooled_low = (pooled_sums[index] / float(layouts[index][4])).astype(bf16)
        logits = jnp.dot(pooled_low, w_head, preferred_element_type=jnp.float32)
        norm_log = jax.nn.logsumexp(logits, -1)
        hot = (labels[:, None] == jnp.arange(logits.shape[1], dtype=jnp.int32)[None, :]).astype(
            jnp.float32
        )
        true_logit = jnp.sum(hot * logits, -1)
        alive = live.astype(jnp.float32)
        stats.append(jnp.stack([jnp.sum(alive * (norm_log - true_logit)), jnp.sum(alive)]))
        head_parts.append((pooled_low, jnp.exp(logits - norm_log[:, None]) - hot, alive))
    stats_a, stats_b = lax.psum((stats[0], stats[1]), "dp")
    total = jnp.maximum(stats_a[1] + stats_b[1], 1.0)
    grad_head = jnp.zeros(w_head.shape, jnp.float32)
    d_x2_parts = []
    for index in range(2):
        pooled_low, soft_minus, alive = head_parts[index]
        d_logits = (soft_minus * alive[:, None] / total).astype(bf16)
        grad_head = grad_head + lax.dot_general(
            pooled_low, d_logits, ROWS_DIM, preferred_element_type=jnp.float32
        )
        d_pooled = lax.dot_general(d_logits, w_head, COLS_DIM, preferred_element_type=jnp.float32)
        images, length, whole = (layouts[index][2], layouts[index][3], layouts[index][4])
        spread = jnp.broadcast_to(
            (d_pooled / float(whole))[:, None, :], (images, length, d_pooled.shape[1])
        )
        d_x2_parts.append(spread.reshape(images * length, -1))
    d_x2 = jnp.concatenate(d_x2_parts, 0)
    d_mix = d_x2.astype(bf16)
    grad_down = lax.dot_general(d_mix, act, ROWS_DIM, preferred_element_type=jnp.float32)
    d_act = jnp.dot(d_mix, w_mlp[1], preferred_element_type=jnp.float32)
    d_inner = gelu_back(d_act)[0].astype(bf16)
    grad_up = lax.dot_general(h2, d_inner, ROWS_DIM, preferred_element_type=jnp.float32)
    d_h2 = lax.dot_general(d_inner, w_mlp[0], COLS_DIM, preferred_element_type=jnp.float32)
    d_x1_norm, grad_gain2 = norm2_back(d_h2)
    d_x1 = d_x2 + d_x1_norm
    d_attn = d_x1.astype(bf16)
    grad_out = lax.dot_general(mixed, d_attn, ROWS_DIM, preferred_element_type=jnp.float32)
    d_mixed = lax.dot_general(d_attn, w_out, COLS_DIM, preferred_element_type=jnp.float32).astype(
        bf16
    )
    d_query_parts, d_kv_parts = ([], [])
    for index in range(2):
        first_row, last_row, images, length, whole = layouts[index]
        query, keys, values, norm_log = saved[index]
        d_out = d_mixed[first_row:last_row].reshape(images, length, HEADS, HEAD_DIM)
        d_query, d_keys, d_values = attend_back(query, keys, values, norm_log, d_out)
        d_query_parts.append(d_query.reshape(last_row - first_row, width))
        paired = jnp.stack([d_keys, d_values], 2).reshape(images, seq_count, length, 2 * width)
        d_kv_parts.append(
            paired.transpose(1, 0, 2, 3).reshape(seq_count, last_row - first_row, 2 * width)
        )
    d_all = jnp.concatenate(d_kv_parts, 1)
    mine_kv = d_all[1 % seq_count]
    for turn in range(1, seq_count):
        mine_kv = (
            from_behind(mine_kv.astype(jnp.bfloat16), "seq", 1).astype(mine_kv.dtype)
            + d_all[(turn + 1) % seq_count]
        )
    d_qkv = jnp.concatenate([jnp.concatenate(d_query_parts, 0), mine_kv], 1).astype(bf16)
    grad_qkv = lax.dot_general(h1, d_qkv, ROWS_DIM, preferred_element_type=jnp.float32)
    d_h1 = lax.dot_general(d_qkv, w_qkv, COLS_DIM, preferred_element_type=jnp.float32)
    d_x0_norm, grad_gain1 = norm1_back(d_h1)
    d_x0 = d_x1 + d_x0_norm
    grad_kern = jnp.zeros(kern_full.shape, jnp.float32)
    grad_pos = jnp.zeros(pos_full.shape, jnp.float32)
    for index in range(2):
        first_row, last_row, images, length, whole = layouts[index]
        d_rows = d_x0[first_row:last_row]
        d_kernel = lax.dot_general(
            flats[index], d_rows.astype(bf16), ROWS_DIM, preferred_element_type=jnp.float32
        )
        grad_kern = grad_kern + kern_backs[index](d_kernel)[0]
        d_place = d_rows.reshape(images, length, -1).sum(0)
        grad_pos = grad_pos + pos_backs[index](d_place.reshape(grid_shape(size_sets, index)))[0]
    grad_mlp = jnp.stack([grad_up, grad_down], 0)
    grad_gain = jnp.stack([grad_gain1, grad_gain2], 0)
    grad_head = grad_head / float(seq_count)
    owned = (
        lax.psum_scatter(grad_qkv, ("dp", "seq"), scatter_dimension=0, tiled=True),
        lax.psum_scatter(grad_out, ("dp", "seq"), scatter_dimension=0, tiled=True),
        lax.psum_scatter(grad_mlp, ("dp", "seq"), scatter_dimension=1, tiled=True),
        lax.psum_scatter(grad_kern, ("dp", "seq"), scatter_dimension=0, tiled=True),
        lax.psum_scatter(grad_pos, ("dp", "seq"), scatter_dimension=1, tiled=True),
        lax.psum_scatter(grad_head, ("dp", "seq"), scatter_dimension=0, tiled=True),
        lax.psum_scatter(grad_gain, ("dp", "seq"), scatter_dimension=1, tiled=True),
    )
    square_sum = sum((jnp.sum(piece * piece) for piece in owned))
    grad_norm = jnp.sqrt(lax.psum(square_sum, ("dp", "seq")))
    factor = jnp.minimum(1.0, CLIP / (grad_norm + 1e-06))
    done = [adamw(masters[i], firsts[i], seconds[i], owned[i] * factor, RATES[i]) for i in range(7)]
    size_stats = jnp.stack(
        [stats_a[0] / jnp.maximum(stats_a[1], 1.0), stats_b[0] / jnp.maximum(stats_b[1], 1.0)]
    )
    return (
        done[0][0],
        done[1][0],
        done[2][0],
        done[3][0],
        done[4][0],
        done[5][0],
        done[6][0],
        done[0][1],
        done[1][1],
        done[2][1],
        done[3][1],
        done[4][1],
        done[5][1],
        done[6][1],
        done[0][2],
        done[1][2],
        done[2][2],
        done[3][2],
        done[4][2],
        done[5][2],
        done[6][2],
        size_stats,
        grad_norm,
    )


def specs(row, col):
    both = (*row, *col)
    owned = (
        P(both, None), P(both, None), P(None, both, None), P(both, None), P(None, both),
        P(both, None), P(None, both),
    )
    images = P(row, col, None, None)
    return (images, images, P(row), P(row), P(row), P(row), *owned * 3), (*owned * 3, P(), P())


def solution(mesh):
    dp, seq = mesh.shape["dp"], mesh.shape["seq"]

    def run(*args):
        if fits_fast(mesh, args[0], args[1]):
            split = Mesh(mesh.devices.reshape(4, dp // 8, 2, seq), AXES)
            placed, given = specs(AXES[:3], AXES[3:])
            step = jax.shard_map(
                fast_on_device, mesh=split, in_specs=placed, out_specs=given, check_vma=False
            )
        else:
            placed, given = specs(("dp",), ("seq",))
            step = jax.shard_map(
                on_device, mesh=mesh, in_specs=placed, out_specs=given, check_vma=False
            )
        return step(*args)

    return run
```

```python
import math
from functools import partial

import jax
import jax.numpy as jnp
import ml_dtypes
import numpy as np
from jax import lax
from jax.experimental import pallas as pl
from jax.experimental.pallas import tpu as pltpu
from jax.sharding import Mesh
from jax.sharding import PartitionSpec as P

HEADS = 12
HEAD_DIM = 64
BASE = 32
PATCH_A = 10
PATCH_B = 12


HIGH = lax.Precision.HIGHEST
RATES = (0.012, 0.2, 0.012, 0.03, 0.15, 0.06, 0.25)
CLIP = 0.001
ROWS_DIM = (((0,), (0,)), ((), ()))
COLS_DIM = (((1,), (1,)), ((), ()))


def from_behind(value, axis, steps):
    count = lax.axis_size(axis)
    pairs = [(source, (source + steps) % count) for source in range(count)]
    return lax.ppermute(value, axis, pairs)


def interp_matrix(n_out, n_in):
    places = jnp.arange(n_out, dtype=jnp.float32) * ((n_in - 1) / (n_out - 1))
    return jnp.maximum(
        0.0, 1.0 - jnp.abs(places[:, None] - jnp.arange(n_in, dtype=jnp.float32)[None, :])
    )


def pinv_table(patch):
    basis = interp_matrix(patch, BASE)
    gram = jnp.dot(basis, basis.T, precision=HIGH)
    factor = jnp.linalg.cholesky(gram)
    return jax.scipy.linalg.cho_solve((factor, True), basis)


def layer_norm(values, gain):
    centred = values - jnp.mean(values, -1, keepdims=True)
    spread = jnp.mean(centred * centred, -1, keepdims=True)
    return centred * lax.rsqrt(spread + 1e-06) * gain


def kernel_resize(kernel, patch):
    table = pinv_table(patch)
    shaped = kernel.reshape(3, BASE, BASE, -1)
    return jnp.einsum("ia,jb,cabd->cijd", table, table, shaped, precision=HIGH).reshape(
        3 * patch * patch, -1
    )


def grid_resize(position, row_table, grid):
    table = interp_matrix(grid, 7)
    return jnp.einsum(
        "ia,jb,abd->ijd", row_table, table, position.reshape(7, 7, -1), precision=HIGH
    )


def adamw(weight, first, second, grad, rate):
    first = 0.9 * first + 0.1 * grad
    second = 0.999 * second + 0.001 * grad * grad
    step_dir = first / (1.0 - 0.9**3) / (jnp.sqrt(second / (1.0 - 0.999**3)) + 1e-08)
    return (weight - rate * (step_dir + 0.1 * weight), first, second)


def attend(query, keys, values):
    scores = jnp.einsum(
        "ithe,ishe->ihts", query, keys, preferred_element_type=jnp.float32
    ) * HEAD_DIM ** (-0.5)
    norm_log = jax.nn.logsumexp(scores, -1, keepdims=True)
    probs = jnp.exp(scores - norm_log).astype(jnp.bfloat16)
    return (
        jnp.einsum("ihts,ishe->ithe", probs, values, preferred_element_type=jnp.float32),
        norm_log,
    )


def attend_back(query, keys, values, norm_log, d_out):
    scale = HEAD_DIM ** (-0.5)
    scores = jnp.einsum("ithe,ishe->ihts", query, keys, preferred_element_type=jnp.float32) * scale
    probs = jnp.exp(scores - norm_log)
    d_probs = jnp.einsum("ithe,ishe->ihts", d_out, values, preferred_element_type=jnp.float32)
    d_scores = (probs * (d_probs - jnp.sum(probs * d_probs, -1, keepdims=True))).astype(
        jnp.bfloat16
    )
    d_query = (
        jnp.einsum("ihts,ishe->ithe", d_scores, keys, preferred_element_type=jnp.float32) * scale
    )
    d_keys = (
        jnp.einsum("ihts,ithe->ishe", d_scores, query, preferred_element_type=jnp.float32) * scale
    )
    d_values = jnp.einsum(
        "ihts,ithe->ishe", probs.astype(jnp.bfloat16), d_out, preferred_element_type=jnp.float32
    )
    return (d_query, d_keys, d_values)


def grid_shape(size_sets, index):
    pixels = size_sets[index][0]
    return (pixels.shape[1], pixels.shape[2], -1)


AXES = ("z", "x", "core", "y")
CHIPS = ("z", "x", "y")
NT = (((1,), (1,)), ((), ()))
NN = (((1,), (0,)), ((), ()))
BF = jnp.bfloat16
F32 = jnp.float32
VMEM_BYTES = 58 << 20
QUERY_SCALE = HEAD_DIM**-0.5 * math.log2(math.e)


def shift(value, axis, steps):
    count = lax.axis_size(axis)
    pairs = [(source, (source + steps) % count) for source in range(count)]
    return lax.ppermute(value, axis, pairs)


def chip_sizes():
    return tuple(lax.axis_size(axis) for axis in CHIPS)


def gather_rows(value):
    rows, cols = value.shape
    z, x, y = chip_sizes()
    chips = z * x * y
    copies = jnp.broadcast_to(value[None], (chips, rows, cols)).reshape(chips * rows, cols)
    mine = lax.all_to_all(copies, CHIPS, split_axis=0, concat_axis=0, tiled=True)
    other = shift(mine, "core", 1)
    parts = [part.reshape(z, x, 1, y, rows, cols) for part in (mine, other)]
    first = lax.axis_index("core") == 0
    both = jnp.concatenate(
        [jnp.where(first, parts[0], parts[1]), jnp.where(first, parts[1], parts[0])], 2
    )
    return both.reshape(2 * chips * rows, cols)


def scatter_rows(away, own):
    both = (own.astype(F32) + shift(away, "core", 1).astype(F32)).astype(BF)
    return lax.all_to_all(both, CHIPS, split_axis=0, concat_axis=0, tiled=True)


def block_sum(got, rows):
    return jnp.sum(got.reshape(-1, rows, got.shape[1]).astype(F32), 0)


def store_by_core(core, acc, away_ref, own_ref, count):
    rows = acc.shape[0] // count // 2
    for pair in range(count):
        at = slice(pair * rows, (pair + 1) * rows)
        for side, ref in ((core, own_ref), (1 - core, away_ref)):
            first = pl.multiple_of((2 * pair + side) * rows, rows)
            ref[at, :] = acc[pl.ds(first, rows), :].astype(BF)


def interp_table(n_out, n_in):
    places = np.arange(n_out) * ((n_in - 1) / (n_out - 1))
    return np.maximum(0.0, 1.0 - np.abs(places[:, None] - np.arange(n_in)[None, :]))


def resize_table(patch):
    basis = interp_table(patch, BASE)
    table = np.linalg.solve(basis @ basis.T, basis)
    return np.kron(table, table).astype(np.float32)


def place_table(grid):
    table = interp_table(grid, 7)
    full = np.kron(table, table).astype(np.float32)
    high = full.astype(ml_dtypes.bfloat16)
    low = (full - high.astype(np.float32)).astype(ml_dtypes.bfloat16)
    return np.concatenate([high, low, np.zeros((grid * grid, 30), ml_dtypes.bfloat16)], 1)


def dot(left, right, dims):
    return lax.dot_general(left, right, dims, preferred_element_type=F32)


def estimate(flops, nbytes, share=32):
    return pl.CostEstimate(
        flops=int(flops) // share, bytes_accessed=int(nbytes) // share, transcendentals=0
    )


def normed(values):
    centred = values - jnp.mean(values, -1, keepdims=True)
    scale = lax.rsqrt(jnp.mean(centred * centred, -1, keepdims=True) + 1e-06)
    return centred * scale, scale


def norm_back(d_out, gain, hat, scale):
    d_hat = d_out * gain
    return scale * (
        d_hat
        - jnp.mean(d_hat, -1, keepdims=True)
        - hat * jnp.mean(d_hat * hat, -1, keepdims=True)
    )


def embed_kernel(*refs, pieces, at, depth, spot):
    pixel_refs, (tab_ref, weight_ref, gain_ref, *rest) = refs[:pieces], refs[pieces:]
    x0_ref, h1_ref = rest
    base = dot(tab_ref[...], weight_ref[:, spot : spot + tab_ref.shape[1]], NT)

    def body(pixel_ref):
        x0 = base + dot(pixel_ref[...], weight_ref[:, at : at + depth], NT)
        x0_ref[...] = x0
        h1_ref[...] = (normed(x0)[0] * gain_ref[...]).astype(BF)

    for piece, pixel_ref in enumerate(pixel_refs):
        pl.when(pl.program_id(1) == piece)(partial(body, pixel_ref))


def embed(pieces, tab, weight, at, spot, gain, images):
    count, depth = len(pieces), pieces[0].shape[1]
    block = tab.shape[0] // count
    rows, width = images * tab.shape[0], weight.shape[0]
    still = lambda array: pl.BlockSpec(array.shape, lambda i, j: (0, 0))
    moving = lambda cols: pl.BlockSpec((block, cols), lambda i, j: (i * count + j, 0))
    outs = [(width, F32), (width, BF)]
    return pl.pallas_call(
        partial(embed_kernel, pieces=count, at=at, depth=depth, spot=spot),
        out_shape=tuple(jax.ShapeDtypeStruct((rows, cols), kind) for cols, kind in outs),
        grid=(images, count),
        in_specs=[pl.BlockSpec((block, depth), lambda i, j: (i, 0))] * count
        + [pl.BlockSpec((block, tab.shape[1]), lambda i, j: (j, 0)), still(weight), still(gain)],
        out_specs=[moving(cols) for cols, _ in outs],
        compiler_params=pltpu.CompilerParams(vmem_limit_bytes=VMEM_BYTES),
        cost_estimate=estimate(2 * rows * width * width, rows * width * 8, 1),
        name="embed",
    )(*pieces, tab, weight, gain)


def head_split(first, values):
    zero = jnp.zeros((), values.dtype)
    return jnp.where(first, values, zero), jnp.where(first, zero, values)


def attend_pair(rows_ref, n_query, out_ref, log_ref, between=None):
    lane = lax.broadcasted_iota(jnp.int32, (1, 128), 1)
    first = lane < HEAD_DIM
    one = jnp.ones((), BF)
    values = rows_ref[:, 256:]
    keys = head_split(first, rows_ref[:, 128:256])
    sided = (jnp.where(first, values, one).T, jnp.where(first, one, values).T)
    query = rows_ref[:n_query, :128]
    scores = [dot(keys[head], query, NT) for head in range(2)]
    if between is not None:
        between()
    tops, probs, mixed = [], [], []
    for head in range(2):
        tops.append(jnp.max(scores[head], 0, keepdims=True))
        probs.append(jnp.exp2(scores[head] - tops[head]).astype(BF))
        mixed.append(dot(sided[head], probs[head], NN))
    outs = []
    for head in range(2):
        at = HEAD_DIM * (1 - head)
        total = mixed[head][at : at + 1]
        own = HEAD_DIM * head
        outs.append(mixed[head][own : own + HEAD_DIM] / total)
        log_ref[0, 0, head : head + 1, :] = tops[head] + jnp.log2(total)
    out_ref[...] = jnp.concatenate(outs, 0).T.astype(BF)


def attend_kernel(h1_ref, weight_ref, qkv_ref, out_ref, log_ref, held, *, items, n_query):
    step = pl.program_id(0)

    def project():
        lane = lax.broadcasted_iota(jnp.int32, (1, 384), 1)
        scale = jnp.where(lane < 128, QUERY_SCALE, 1.0)
        rows = (dot(h1_ref[...], weight_ref[...], NN) * scale).astype(BF)
        qkv_ref[...] = rows
        held[step % 2] = rows

    def attend(between=None):
        attend_pair(held.at[(step + 1) % 2], n_query, out_ref, log_ref, between)

    @pl.when(step == 0)
    def _():
        project()

    @pl.when((step > 0) & (step < items))
    def _():
        attend(project)

    @pl.when(step == items)
    def _():
        attend()


def attend_pairs(h1, weight, first, pairs, images, n_query):
    rows, width = h1.shape
    count = rows // images
    items = images * pairs
    now = lambda s: jnp.minimum(s, items - 1)
    last = lambda s: jnp.maximum(s - 1, 0)
    return pl.pallas_call(
        partial(attend_kernel, items=items, n_query=n_query),
        out_shape=(
            jax.ShapeDtypeStruct((rows, pairs * 384), BF),
            jax.ShapeDtypeStruct((images * n_query, pairs * 128), BF),
            jax.ShapeDtypeStruct((images, pairs, 2, n_query), F32),
        ),
        grid=(items + 1,),
        in_specs=[
            pl.BlockSpec((count, width), lambda s: (now(s) // pairs, 0)),
            pl.BlockSpec((width, 384), lambda s: (0, first + now(s) % pairs)),
        ],
        out_specs=[
            pl.BlockSpec((count, 384), lambda s: (now(s) // pairs, now(s) % pairs)),
            pl.BlockSpec((n_query, 128), lambda s: (last(s) // pairs, last(s) % pairs)),
            pl.BlockSpec(
                (1, 1, 2, n_query), lambda s: (last(s) // pairs, last(s) % pairs, 0, 0)
            ),
        ],
        scratch_shapes=[pltpu.VMEM((2, count, 384), BF)],
        compiler_params=pltpu.CompilerParams(vmem_limit_bytes=VMEM_BYTES),
        cost_estimate=estimate(
            2 * items * count * (n_query * 1200 + width * 384), rows * width * 8, 1
        ),
        name="attend",
    )(h1, weight)


def attend_back_pair(q_ref, kv_ref, do_ref, o_ref, log_ref):
    lane = lax.broadcasted_iota(jnp.int32, (1, 128), 1)
    first = lane < HEAD_DIM
    scale = jnp.asarray(HEAD_DIM**-0.5, BF)
    keys_all = kv_ref[:, 128:256]
    keys = head_split(first, keys_all)
    values = head_split(first, kv_ref[:, 256:])
    query = q_ref[:, :128]
    d_out = do_ref[...]
    queries = head_split(first, query)
    d_outs = head_split(first, d_out)
    keys_t = tuple(part.T for part in head_split(first, keys_all * scale))
    both = (d_out.astype(F32) * o_ref[...].astype(F32)).T
    d_query, d_keys, d_values = 0.0, 0.0, 0.0
    for head in range(2):
        row = jnp.sum(both[HEAD_DIM * head : HEAD_DIM * (head + 1)], 0, keepdims=True)
        scores = dot(keys[head], query, NT)
        probs = jnp.exp2(scores - log_ref[0, 0, head : head + 1, :])
        d_probs = dot(values[head], d_out, NT)
        d_scores = (probs * (d_probs - row)).astype(BF)
        d_keys = d_keys + dot(d_scores, queries[head], NN)
        d_values = d_values + dot(probs.astype(BF), d_outs[head], NN)
        d_query = d_query + dot(keys_t[head], d_scores, NN)
    return d_query.astype(BF), (d_keys * math.log(2.0)).astype(BF), d_values.astype(BF)


def attend_back_kernel(q_ref, kv_ref, do_ref, o_ref, log_ref, d_ref):
    parts = attend_back_pair(q_ref, kv_ref, do_ref, o_ref, log_ref)
    rows = parts[0].shape[1]
    d_ref[:rows, :128] = parts[0].T
    d_ref[rows:, :128] = jnp.zeros((d_ref.shape[0] - rows, 128), BF)
    for index, part in enumerate(parts[1:], 1):
        d_ref[:, 128 * index : 128 * (index + 1)] = part


def attend_back_apart(query, keys, d_out, out, log, pairs, n_query, n_key):
    over_q = lambda cols: pl.BlockSpec((n_query, cols), lambda h: (0, h))
    over_k = lambda cols: pl.BlockSpec((n_key, cols), lambda h: (0, h))
    return pl.pallas_call(
        attend_back_kernel,
        out_shape=jax.ShapeDtypeStruct((n_key, pairs * 384), BF),
        grid=(pairs,),
        in_specs=[
            over_q(384),
            over_k(384),
            over_q(128),
            over_q(128),
            pl.BlockSpec((1, 1, 2, n_query), lambda h: (0, h, 0, 0)),
        ],
        out_specs=over_k(384),
        compiler_params=pltpu.CompilerParams(vmem_limit_bytes=VMEM_BYTES),
        cost_estimate=estimate(2 * pairs * n_query * n_key * 2400, (n_query + n_key) * pairs * 1024),
        name="attend_back_apart",
    )(query, keys, d_out, out, log)


def attend_back_grad_kernel(
    core_ref, qkv_ref, do_ref, o_ref, log_ref, h1_ref, h1_a_ref, d_a_ref,
    d_ref, away_ref, own_ref, acc, turned, *, images, blocks
):
    image = pl.program_id(1)

    @pl.when(image == 0)
    def _():
        acc[...] = dot(d_a_ref[...].T, h1_a_ref[...], NN)

    d_query, d_keys, d_values = attend_back_pair(qkv_ref, qkv_ref, do_ref, o_ref, log_ref)
    d_ref[:, :128] = d_query.T
    d_ref[:, 128:256] = d_keys
    d_ref[:, 256:] = d_values
    d_turned = jnp.concatenate([d_query, d_keys.T, d_values.T], 0)
    acc[...] += dot(d_turned, h1_ref[...], NN)

    @pl.when(image == images - 1)
    def _():
        turned[...] = acc[...].T
        store_by_core(core_ref[0], turned, away_ref, own_ref, blocks)


def attend_back_grad(qkv, d_out, out, log, h1, h1_a, d_a, core, pairs, images, count, blocks):
    width = h1.shape[1]
    rows_a = h1_a.shape[0]
    over = lambda cols: pl.BlockSpec((count, cols), lambda h, i: (i, h))
    grad = pl.BlockSpec((width // 2, 384), lambda h, i: (0, h))
    return pl.pallas_call(
        partial(attend_back_grad_kernel, images=images, blocks=blocks),
        out_shape=(
            jax.ShapeDtypeStruct((images * count, pairs * 384), BF),
            jax.ShapeDtypeStruct((width // 2, pairs * 384), BF),
            jax.ShapeDtypeStruct((width // 2, pairs * 384), BF),
        ),
        grid=(pairs, images),
        in_specs=[
            pl.BlockSpec(memory_space=pltpu.SMEM),
            over(384),
            over(128),
            over(128),
            pl.BlockSpec((1, 1, 2, count), lambda h, i: (i, h, 0, 0)),
            pl.BlockSpec((count, width), lambda h, i: (i, 0)),
            pl.BlockSpec((rows_a, width), lambda h, i: (0, 0)),
            pl.BlockSpec((rows_a, 384), lambda h, i: (0, h)),
        ],
        out_specs=[over(384), grad, grad],
        scratch_shapes=[
            pltpu.VMEM((384, width), F32),
            pltpu.VMEM((width, 384), F32),
        ],
        compiler_params=pltpu.CompilerParams(vmem_limit_bytes=VMEM_BYTES),
        cost_estimate=estimate(
            images * 2 * pairs * count * count * 2800, images * count * pairs * 2048
        ),
        name="attend_back",
    )(core, qkv, d_out, out, log, h1, h1_a, d_a)


def gelu_parts(inner):
    scaled = inner * (0.5**0.5)
    upper = 0.5 * lax.erf(scaled) + 0.5
    bell = jnp.exp2(scaled * scaled * -math.log2(math.e) - 0.5 * math.log2(2.0 * math.pi))
    return upper, inner * bell


def mlp_kernel(
    x0_ref, mixed0_ref, mixed1_ref, wout_ref, gain_ref, wup_ref,
    x1_ref, slope_ref, xsum_ref, asum_ref, *, per
):
    mixed = jnp.concatenate([mixed0_ref[...], mixed1_ref[...]], 1)
    x1 = x0_ref[...] + dot(mixed, wout_ref[...], NN)
    x1_ref[...] = x1
    h2 = (normed(x1)[0] * gain_ref[...]).astype(BF)

    @pl.when(pl.program_id(0) % per == 0)
    def _():
        xsum_ref[...] = jnp.zeros_like(xsum_ref)
        asum_ref[...] = jnp.zeros_like(asum_ref)

    xsum_ref[0] += jnp.sum(x1, 0, keepdims=True)
    width = 512
    for first in range(0, wup_ref.shape[1], width):
        cols = slice(first, first + width)
        inner = dot(h2, wup_ref[:, cols], NN)
        upper, slope = gelu_parts(inner)
        slope_ref[:, cols] = (upper + slope).astype(BF)
        asum_ref[0, :, cols] += jnp.sum(inner * upper, 0, keepdims=True)


def mlp(x0, mixed, w_all, hidden, gain, images, block):
    rows, width = x0.shape
    per = rows // images // block
    return pl.pallas_call(
        partial(mlp_kernel, per=per),
        out_shape=(
            jax.ShapeDtypeStruct((rows, width), F32),
            jax.ShapeDtypeStruct((rows, hidden), BF),
            jax.ShapeDtypeStruct((images, 1, width), F32),
            jax.ShapeDtypeStruct((images, 1, hidden), F32),
        ),
        grid=(rows // block,),
        in_specs=[
            pl.BlockSpec((block, width), lambda i: (i, 0)),
            pl.BlockSpec((block, width // 2), lambda i: (i, 0)),
            pl.BlockSpec((block, width // 2), lambda i: (i, 0)),
            pl.BlockSpec((width, width), lambda i: (0, 3)),
            pl.BlockSpec((1, width), lambda i: (0, 0)),
            pl.BlockSpec((width, hidden), lambda i: (0, 4 * width // hidden)),
        ],
        out_specs=[
            pl.BlockSpec((block, width), lambda i: (i, 0)),
            pl.BlockSpec((block, hidden), lambda i: (i, 0)),
            pl.BlockSpec((1, 1, width), lambda i: (i // per, 0, 0)),
            pl.BlockSpec((1, 1, hidden), lambda i: (i // per, 0, 0)),
        ],
        compiler_params=pltpu.CompilerParams(vmem_limit_bytes=VMEM_BYTES),
        cost_estimate=estimate(4 * rows * width * (hidden + width), rows * hidden * 4),
        name="mlp",
    )(x0, *mixed, w_all, gain, w_all)


def head_kernel(
    xsum_ref, asum_ref, sums_a_ref, down_ref, head_ref, label_ref, alive_ref, once_ref, whole_ref,
    total_ref, loss_ref, rows_ref, dx2_ref, dact_ref, *, classes, own
):
    width, hidden = down_ref.shape
    fill = loss_ref.shape[0] - own - 1

    def stacked(ref, cols):
        rows = [ref[image] for image in range(own)] + [sums_a_ref[:, cols]]
        return jnp.concatenate(rows + [jnp.zeros((fill, rows[0].shape[1]), F32)], 0)

    xsum = stacked(xsum_ref, slice(0, width))
    asum = stacked(asum_ref, slice(width, width + hidden))
    high = asum.astype(BF)
    low = (asum - high.astype(F32)).astype(BF)
    whole = whole_ref[...]
    down = down_ref[...]
    both = dot(jnp.concatenate([high, low], 0), down, NT)
    pooled = (xsum + (both[: both.shape[0] // 2] + both[both.shape[0] // 2 :])) / whole
    pooled_low = pooled.astype(BF)
    head = head_ref[...]
    place = lax.broadcasted_iota(jnp.int32, (1, head.shape[1]), 1)
    logits = jnp.where(place < classes, dot(pooled_low, head, NN), -1e30)
    top = jnp.max(logits, -1, keepdims=True)
    norm_log = top + jnp.log(jnp.sum(jnp.exp(logits - top), -1, keepdims=True))
    hot = place == label_ref[...]
    true_logit = jnp.sum(jnp.where(hot, logits, 0.0), -1, keepdims=True)
    loss_ref[...] = jnp.broadcast_to(norm_log - true_logit, loss_ref.shape)
    soft = jnp.exp(logits - norm_log) - hot.astype(F32)
    d_logits = (soft * alive_ref[...] / total_ref[...]).astype(BF)
    d_x2 = dot(d_logits, head, NT) / whole
    d_mix = d_x2.astype(BF)
    d_act = dot(d_mix, down, NN)
    for image in range(own + 1):
        dx2_ref[image] = d_x2[image : image + 1]
        dact_ref[image] = d_act[image : image + 1]
    once = once_ref[...]
    rows_ref[:, :hidden] = high
    rows_ref[:, hidden : hidden + width] = pooled_low
    rows_ref[:, hidden + width : hidden + 2 * width] = (d_mix * once).astype(BF)
    rows_ref[:, hidden + 2 * width :] = (d_logits * once).astype(BF)


def head_step(xsum, asum, sums_a, w_down_head, labels, alive, once, whole, total, classes):
    own, _, width = xsum.shape
    hidden = asum.shape[2]
    rows = labels.shape[0]
    padded = w_down_head.shape[1] - hidden
    spec = lambda shape, *place: pl.BlockSpec(shape, lambda i: place or (0,) * len(shape))
    shapes = (
        ((rows, 128), F32),
        ((rows, hidden + 2 * width + padded), BF),
        ((own + 1, 1, width), F32),
        ((own + 1, 1, hidden), F32),
    )
    return pl.pallas_call(
        partial(head_kernel, classes=classes, own=own),
        out_shape=tuple(jax.ShapeDtypeStruct(*shape) for shape in shapes),
        grid=(1,),
        in_specs=[
            spec(xsum.shape),
            spec(asum.shape),
            spec(sums_a.shape),
            spec((width, hidden), 0, 0),
            spec((width, padded), 0, hidden // padded),
            spec((rows, 1)),
            spec((rows, 1)),
            spec((rows, 1)),
            spec((rows, 1)),
            spec((1, 1)),
        ],
        out_specs=[spec(shape[0]) for shape in shapes],
        compiler_params=pltpu.CompilerParams(vmem_limit_bytes=VMEM_BYTES),
        cost_estimate=estimate(1 << 32, 8 << 20),
        name="head",
    )(xsum, asum, sums_a, w_down_head, w_down_head, labels, alive, once, whole, total)


def mlp_back_kernel(*refs, steps):
    parts = (refs[0:6], refs[6:12])
    wout_ref, gain_ref, wup_ref = refs[12:15]
    outs = (refs[15:18], refs[18:21])
    grad_ref, ggain_ref = refs[21:23]
    up_acc, out_acc = refs[23:25]
    step = pl.program_id(0)

    def body(inputs, outputs, begin):
        slope_ref, dact_ref, x1_ref, dx2_ref, *mixed_refs = inputs
        dx1_ref, *dmixed_refs = outputs
        gain = gain_ref[...]
        hat, scale = normed(x1_ref[...])
        h2_t = (hat * gain).astype(BF).T
        width = 768
        cuts = [slice(first, first + width) for first in range(0, slope_ref.shape[1], width)]
        d_inner = [
            (slope_ref[:, cols].astype(F32) * dact_ref[0, :, cols]).astype(BF) for cols in cuts
        ]
        d_h2 = sum(dot(part, wup_ref[:, cols], NT) for part, cols in zip(d_inner, cuts))
        gain_grad = jnp.sum(d_h2 * hat, 0, keepdims=True)
        ggain_ref[...] = gain_grad if begin else ggain_ref[...] + gain_grad
        rows = x1_ref.shape[0] // len(cuts)
        for index, (part, cols) in enumerate(zip(d_inner, cuts)):
            share = slice(index * rows, (index + 1) * rows)
            grad = dot(h2_t, part, NN)
            up_acc[:, cols] = grad if begin else up_acc[:, cols] + grad
            dx1_ref[share] = dx2_ref[0] + norm_back(d_h2[share], gain, hat[share], scale[share])
        d_attn = dx1_ref[...].astype(BF)
        mixed = jnp.concatenate([mixed_ref[...] for mixed_ref in mixed_refs], 1)
        grad = dot(mixed.T, d_attn, NN)
        out_acc[...] = grad if begin else out_acc[...] + grad
        d_mixed = dot(d_attn, wout_ref[...], NT).astype(BF)
        half = mixed_refs[0].shape[1]
        for index, dmixed_ref in enumerate(dmixed_refs):
            dmixed_ref[...] = d_mixed[:, index * half : (index + 1) * half]

    @pl.when(step == 0)
    def _():
        body(parts[1], outs[1], True)

    @pl.when(step > 0)
    def _():
        body(parts[0], outs[0], False)

    @pl.when(step == steps)
    def _():
        hidden = up_acc.shape[1]
        grad_ref[:, :hidden] = up_acc[...].astype(BF)
        grad_ref[:, hidden:] = out_acc[...].astype(BF)


def mlp_back(part_b, part_a, w_all, gain, images, block):
    rows, width = part_b[2].shape
    rows_a = part_a[2].shape[0]
    hidden = part_b[0].shape[1]
    steps = rows // block
    per = steps // images
    at = lambda i: jnp.maximum(i - 1, 0)
    moving = lambda cols: pl.BlockSpec((block, cols), lambda i: (at(i), 0))
    still = lambda shape: pl.BlockSpec(shape, lambda i: (0,) * len(shape))
    image = lambda cols: pl.BlockSpec((1, 1, cols), lambda i: (at(i) // per, 0, 0))
    last = lambda cols: pl.BlockSpec((1, 1, cols), lambda i: (images, 0, 0))
    half = width // 2
    outs = []
    for count in (rows, rows_a):
        outs += [
            jax.ShapeDtypeStruct((count, width), F32),
            jax.ShapeDtypeStruct((count, half), BF),
            jax.ShapeDtypeStruct((count, half), BF),
        ]
    return pl.pallas_call(
        partial(mlp_back_kernel, steps=steps),
        out_shape=(
            *outs,
            jax.ShapeDtypeStruct((width, hidden + width), BF),
            jax.ShapeDtypeStruct((1, width), F32),
        ),
        grid=(steps + 1,),
        in_specs=[
            moving(hidden), image(hidden), moving(width), image(width), moving(half), moving(half),
            still((rows_a, hidden)), last(hidden), still((rows_a, width)),
            last(width), still((rows_a, half)), still((rows_a, half)),
            pl.BlockSpec((width, width), lambda i: (0, 3)),
            still((1, width)),
            pl.BlockSpec((width, hidden), lambda i: (0, 4 * width // hidden)),
        ],
        out_specs=[
            moving(width), moving(half), moving(half),
            still((rows_a, width)), still((rows_a, half)), still((rows_a, half)),
            still((width, hidden + width)), still((1, width)),
        ],
        scratch_shapes=[pltpu.VMEM((width, hidden), F32), pltpu.VMEM((width, width), F32)],
        compiler_params=pltpu.CompilerParams(vmem_limit_bytes=VMEM_BYTES),
        cost_estimate=estimate(
            4 * (rows + rows_a) * width * (hidden + width), (rows + rows_a) * hidden * 4
        ),
        name="mlp_back",
    )(*part_b, *part_a, w_all, gain, w_all)


def embed_back_kernel(core_ref, *refs, steps, groups, pieces, blocks, parts_b, parts_a):
    n_b, n_a = 3 + pieces + groups, 4 + groups * parts_a
    inputs_b, inputs_a = refs[:n_b], refs[n_b : n_b + n_a]
    gain_ref, gain_grad_ref, *rest = refs[n_b + n_a :]
    weight_refs = rest[:groups]
    away_ref, own_ref, acc_b, acc_a, acc_tab, gain_acc = rest[groups:]
    step = pl.program_id(0)

    def body(inputs, acc, parts, pixel_ref, terms):
        x0_ref, dx1_ref, tab_ref = inputs[:3]
        gain = gain_ref[...]
        count = x0_ref.shape[0] // parts
        turned = []
        for part in range(parts):
            rows = slice(part * count, (part + 1) * count)
            hat, scale = normed(x0_ref[rows])
            d_h1 = 0.0
            for group, weight_ref in enumerate(weight_refs):
                term_refs = inputs[len(inputs) - (groups - group) * terms :][:terms]
                d_qkv = term_refs[0][rows]
                if terms > 1:
                    d_qkv = sum(ref[rows].astype(F32) for ref in term_refs).astype(BF)
                d_h1 = d_h1 + dot(d_qkv, weight_ref[...], NT)
            gain_acc[0:1] += jnp.sum(d_h1 * hat, 0, keepdims=True)
            d_x0 = dx1_ref[rows] + norm_back(d_h1, gain, hat, scale)
            turned.append(d_x0.astype(BF).T)
        turned = jnp.concatenate(turned, 1)
        acc_tab[...] += dot(turned, tab_ref[...], NN)
        acc[:, : pixel_ref.shape[1]] += dot(turned, pixel_ref[...], NN)

    @pl.when(step == 0)
    def _():
        for acc in (acc_b, acc_a, acc_tab, gain_acc):
            acc[...] = jnp.zeros_like(acc)
        gain_acc[1:2] = gain_grad_ref[...]
        body(inputs_a, acc_a, 1, inputs_a[3], parts_a)

    for piece in range(pieces):

        @pl.when((step > 0) & ((step - 1) % pieces == piece))
        def _(piece=piece):
            body(inputs_b, acc_b, parts_b, inputs_b[3 + piece], 1)

    @pl.when(step == steps)
    def _():
        place = lax.broadcasted_iota(jnp.int32, (8, 128), 1)
        row = lax.broadcasted_iota(jnp.int32, (8, 128), 0)
        spots = jnp.where((place == 126 + row) & (row < 2), 1.0, 0.0).astype(BF)
        acc_tab[...] += lax.dot_general(
            gain_acc[...].astype(BF), spots, ROWS_DIM, preferred_element_type=F32
        )
        at = 0
        for acc in (acc_b, acc_a, acc_tab):
            cols = slice(at, at + acc.shape[1])
            at += acc.shape[1]
            store_by_core(core_ref[0], acc, away_ref.at[:, cols], own_ref.at[:, cols], blocks)


def embed_back(
    x0_b, dx1_b, tab_b, pixels_b, d_b, x0_a, dx1_a, tab_a, pixels_a, d_a, gain, gain_grad, w_all,
    core, blocks, images, depths
):
    rows, width = x0_b.shape
    pieces = len(pixels_b)
    steps = images * pieces
    block = rows // steps
    at = lambda i: jnp.maximum(i - 1, 0)
    moving = lambda array: pl.BlockSpec((block, array.shape[1]), lambda i: (at(i), 0))
    still = lambda shape: pl.BlockSpec(shape, lambda i: (0,) * len(shape))
    inputs_a = (x0_a, dx1_a, tab_a, pixels_a, *sum(d_a, ()))
    rows_a = x0_a.shape[0]
    grad = (width // 2, sum(depths) + 128)
    return pl.pallas_call(
        partial(
            embed_back_kernel, steps=steps, groups=len(d_b), pieces=pieces, blocks=blocks,
            parts_b=max(1, block // 256), parts_a=len(d_a[0]),
        ),
        out_shape=(jax.ShapeDtypeStruct(grad, BF), jax.ShapeDtypeStruct(grad, BF)),
        grid=(steps + 1,),
        in_specs=[pl.BlockSpec(memory_space=pltpu.SMEM)]
        + [moving(x0_b), moving(dx1_b)]
        + [pl.BlockSpec((block, 128), lambda i: (at(i) % pieces, 0))]
        + [
            pl.BlockSpec((block, array.shape[1]), lambda i: (at(i) // pieces, 0))
            for array in pixels_b
        ]
        + [moving(array) for array in d_b]
        + [still((rows_a, array.shape[1])) for array in inputs_a]
        + [still((1, width)), still((1, width))]
        + [
            pl.BlockSpec((width, array.shape[1]), partial(lambda group, i: (0, group), group))
            for group, array in enumerate(d_b)
        ],
        out_specs=[still(grad), still(grad)],
        scratch_shapes=[pltpu.VMEM((width, depth), F32) for depth in (*depths, 128)]
        + [pltpu.VMEM((8, width), F32)],
        compiler_params=pltpu.CompilerParams(vmem_limit_bytes=VMEM_BYTES),
        cost_estimate=estimate(2 * rows * width * (3 * width + 640), rows * 10000),
        name="embed_back",
    )(core, x0_b, dx1_b, tab_b, *pixels_b, *d_b, *inputs_a, gain, gain_grad, *[w_all] * len(d_b))


def resize_back_kernel(got_ref, table_b_ref, table_a_ref, sums_ref, sent_ref, small_ref, *, rows, at):
    owners, _, lanes = sent_ref.shape
    total = jnp.zeros(small_ref.shape, F32)
    for block in range(got_ref.shape[0] // rows):
        total = total + got_ref[block * rows : (block + 1) * rows].astype(F32)
    small_ref[...] = total
    parts, square = [], 0.0
    for channel in range(3):
        part = 0.0
        for table_ref, first in ((table_b_ref, 0), (table_a_ref, at)):
            size = table_ref.shape[0]
            part = part + lax.dot_general(
                total[:, first + channel * size : first + (channel + 1) * size],
                table_ref[...],
                NN,
                precision=HIGH,
                preferred_element_type=F32,
            )
        square = square + jnp.sum(part * part)
        parts.append(part)
    width = BASE * BASE * 3 // owners
    kern = jnp.concatenate(parts + [jnp.zeros((rows, lanes), F32)], 1)
    lane = lax.broadcasted_iota(jnp.int32, (1, lanes), 1)
    last = total[:, total.shape[1] - lanes :]
    pos = jnp.where(lane < 49, last + pltpu.roll(last, lanes - 49, 1), 0.0)
    last = jnp.where(lane < 126, pos, last)
    small_ref[:, total.shape[1] - lanes :] = last
    square = square + jnp.sum(last * last) + jnp.sum(jnp.where(lane == 0, sums_ref[...], 0.0))
    beside = jnp.where(lane == width, square, 0.0)
    for index in (1, 2):
        beside = beside + jnp.where(lane == width + index, pltpu.roll(sums_ref[...], width, 1), 0.0)
    for owner in range(owners):
        sent_ref[owner] = jnp.where(
            lane < width, kern[:, owner * width : owner * width + lanes], beside
        )


def resize_back(got, tables, sums, rows, at, owners, lanes):
    cols = got.shape[1]
    return pl.pallas_call(
        partial(resize_back_kernel, rows=rows, at=at),
        out_shape=(
            jax.ShapeDtypeStruct((owners, rows, lanes), F32),
            jax.ShapeDtypeStruct((rows, cols), F32),
        ),
        in_specs=[pl.BlockSpec(memory_space=pltpu.VMEM)] * 4,
        out_specs=[pl.BlockSpec(memory_space=pltpu.VMEM)] * 2,
        compiler_params=pltpu.CompilerParams(vmem_limit_bytes=VMEM_BYTES),
        cost_estimate=estimate(1 << 28, 4 << 20),
        name="resize_back",
    )(got, *tables, sums)


def update_kernel(got_ref, small_ref, qkv_ref, out_ref, up_ref, down_ref, head_ref, count_ref, *refs, width):
    masters, firsts, seconds = refs[0:7], refs[7:14], refs[14:21]
    new, new_firsts, new_seconds = refs[21:28], refs[28:35], refs[35:42]
    norm_ref, stat_ref = refs[42:]
    owners, rows, lanes = got_ref.shape
    sums = got_ref[0, 0:1, :]
    for owner in range(1, owners):
        sums = sums + got_ref[owner, 0:1, :]
    lane = lax.broadcasted_iota(jnp.int32, (1, lanes), 1)
    norm = jnp.sqrt(jnp.sum(jnp.where(lane == width, sums, 0.0), 1, keepdims=True))
    factor = jnp.minimum(1.0, CLIP / (norm + 1e-06))
    sums = pltpu.roll(sums, lanes - width, 1)
    ratio = sums / jnp.maximum(count_ref[...], 1.0)
    norm_ref[...] = norm
    stat_ref[...] = ratio[:, 1:3]
    kern = jnp.concatenate([got_ref[owner] for owner in range(owners)], 0).T[:width]
    small = small_ref[:, small_ref.shape[1] - lanes :]
    grads = (
        (Ellipsis, qkv_ref[...]),
        (Ellipsis, out_ref[...]),
        (0, up_ref[...]),
        (1, down_ref[...]),
        (Ellipsis, kern),
        (Ellipsis, small[:, :49]),
        (Ellipsis, head_ref[...]),
        (Ellipsis, small[:, 126:128].T),
    )
    for index, (at, grad) in zip((0, 1, 2, 2, 3, 4, 5, 6), grads):
        new[index][at], new_firsts[index][at], new_seconds[index][at] = adamw(
            masters[index][at], firsts[index][at], seconds[index][at], grad * factor, RATES[index]
        )


def update(got, small, grads, count, masters, firsts, seconds, width):
    full = pl.BlockSpec(memory_space=pltpu.VMEM)
    shapes = [jax.ShapeDtypeStruct(array.shape, F32) for array in masters]
    inputs = (got, small, *grads, count, *masters, *firsts, *seconds)
    return pl.pallas_call(
        partial(update_kernel, width=width),
        out_shape=(
            *shapes * 3, jax.ShapeDtypeStruct((1, 1), F32), jax.ShapeDtypeStruct((1, 2), F32)
        ),
        in_specs=[full] * len(inputs),
        out_specs=[full] * 23,
        compiler_params=pltpu.CompilerParams(vmem_limit_bytes=VMEM_BYTES),
        cost_estimate=estimate(1 << 28, 16 << 20),
        name="update",
    )(*inputs)


def after(value, *others):
    return lax.optimization_barrier((value, *others))[0]


def padded_cols(array, width):
    return jnp.pad(array, ((0, 0), (0, width - array.shape[1])))


def round_up(count, unit):
    return -(-count // unit) * unit


def fast_step(
    pixels_a, pixels_b, labels_a, labels_b, live_a, live_b, masters, firsts, seconds
):
    qkv_w, out_w, mlp_w, kern_w, pos_w, head_w, gains = masters
    seq = lax.axis_size("y")
    row = lax.axis_index("y")
    count_all = seq * lax.axis_size("z") * lax.axis_size("x") * 2
    flat_index = lax.axis_index(AXES)
    lead = (row == 0).astype(F32)
    width = HEADS * HEAD_DIM
    hidden = mlp_w.shape[2]
    classes = head_w.shape[1]
    classes_up = round_up(classes, 1024)
    rows_own = qkv_w.shape[0]
    rows_kern = kern_w.shape[0]
    groups = 2
    span = width // groups
    pairs = span // 128

    images_a, rows_a, grid_a, depth_a = pixels_a.shape
    images_b, rows_b, grid_b, depth_b = pixels_b.shape
    own_b = images_b // seq
    parts_b, tabs_b, slices = [], [], []
    table_b = jnp.asarray(place_table(grid_b))
    table_a = jnp.asarray(place_table(grid_a))
    span_b, span_a = rows_b * grid_b, rows_a * grid_a
    for step in range(seq):
        part = lax.dynamic_slice_in_dim(
            pixels_b, ((row + step) % seq) * own_b, own_b, 0
        )
        part = part.reshape(own_b * rows_b * grid_b, depth_b)
        slices.append(part)
        parts_b.append(shift(part, "y", step) if step else part)
        tabs_b.append(lax.dynamic_slice_in_dim(table_b, ((row - step) % seq) * span_b, span_b, 0))
    tab_a = lax.dynamic_slice_in_dim(table_a, row * span_a, span_a, 0)
    whole_a, whole_b = grid_a * grid_a, grid_b * grid_b

    alive_a = live_a.astype(F32)[:, None]
    counts = jnp.stack([lead * jnp.sum(alive_a), lead * jnp.sum(live_b.astype(F32))]).astype(BF)
    lanes = round_up(rows_kern + 2, 128)
    sent = jnp.concatenate(
        [
            kern_w.astype(BF).T,
            jnp.broadcast_to(counts[None], (width, 2)),
            jnp.zeros((width, lanes - rows_kern - 2), BF),
        ],
        1,
    )
    sent = after(sent, *slices)
    got = lax.all_to_all(sent, AXES, split_axis=0, concat_axis=0, tiled=True)
    got, tab_a, tab_b, *parts_b = lax.optimization_barrier(
        (got, tab_a, jnp.concatenate(tabs_b, 0), *parts_b)
    )
    got = got.reshape(count_all, rows_own, lanes)
    counts = got[:, 0, rows_kern : rows_kern + 2]
    got = got.astype(F32)
    kern_cols = got[:, :, :rows_kern].transpose(1, 0, 2).reshape(rows_own, 3, BASE * BASE)

    def group_cols(array, group):
        shaped = array.reshape(rows_own, 3, groups, pairs, 128)[:, :, group]
        return shaped.transpose(0, 2, 1, 3).reshape(rows_own, 3 * span)

    qkv_low = qkv_w.astype(BF)
    w_all = lax.all_gather(
        jnp.concatenate(
            [group_cols(qkv_low, group) for group in range(groups)]
            + [out_w.astype(BF), mlp_w[0].astype(BF)],
            1,
        ),
        AXES, axis=0, tiled=True,
    )

    tables = [resize_table(PATCH_B), resize_table(PATCH_A)]
    sizes = [3 * table.shape[0] for table in tables]
    resized = [
        jnp.einsum("dck,pk->dcp", kern_cols, jnp.asarray(table), precision=HIGH).reshape(
            rows_own, -1
        )
        for table in tables
    ]
    depths = [round_up(size, 128) for size in sizes]
    spot = sum(depths)
    pos_t = pos_w.astype(BF).T
    edge = jnp.zeros((rows_own, 28), BF)
    small = jnp.concatenate(
        [padded_cols(piece.astype(BF), depth) for piece, depth in zip(resized, depths)]
        + [pos_t, pos_t, edge, gains.astype(BF).T],
        1,
    )
    w_small = gather_rows(small)
    w_down_head = lax.all_gather(
        after(
            jnp.concatenate([mlp_w[1].astype(BF), padded_cols(head_w.astype(BF), classes_up)], 1),
            w_small,
        ),
        AXES, axis=0, tiled=True,
    )

    gain_rows = w_small[:, spot + 126 :].T.astype(F32)
    gain1, gain2 = gain_rows[0:1], gain_rows[1:2]
    flat_a = pixels_a.reshape(span_a, depth_a)
    block = min(512, whole_b)
    x0_a, h1_a = embed([flat_a], tab_a, w_small, depths[0], spot, gain1, 1)
    h1_all = jnp.concatenate([h1_a] + [shift(h1_a, "y", step) for step in range(1, seq)], 0)
    x0_b, h1_b = embed(
        [after(parts_b[0], h1_a), *parts_b[1:]], tab_b, w_small, 0, spot, gain1, own_b
    )
    h1_b, h1_all = lax.optimization_barrier((h1_b, h1_all))
    outs_a, outs_b = [], []
    ready = h1_b
    for group in range(groups):
        outs_b.append(
            attend_pairs(after(h1_b, ready), w_all, group * pairs, pairs, own_b, whole_b)
        )
        ready = outs_b[-1][0]
    for group in range(groups):
        outs_a.append(attend_pairs(after(h1_all, ready), w_all, group * pairs, pairs, 1, span_a))
    qkvs_a, qkvs_b = [out[0] for out in outs_a], [out[0] for out in outs_b]
    mixed_a, mixed_b = [out[1] for out in outs_a], [out[1] for out in outs_b]

    x1_a, slope_a, xsum_a, asum_a = mlp(x0_a, mixed_a, w_all, hidden, gain2, 1, span_a)
    sums_a = jnp.concatenate([xsum_a[0], asum_a[0]], 1)
    sums_a = sum([shift(sums_a, "y", step) for step in range(1, seq)], sums_a)
    x1_b, slope_b, xsum_b, asum_b = mlp(after(x0_b, x1_a), mixed_b, w_all, hidden, gain2, own_b, block)

    counts, labels_a, labels_b, live_b, alive_a = lax.optimization_barrier(
        (counts, labels_a, labels_b, live_b, alive_a, h1_b)
    )[:5]
    count = jnp.sum(counts.astype(F32), 0, keepdims=True)
    total = jnp.maximum(jnp.sum(count), 1.0)
    rows_up = round_up(own_b + 1, 8)
    fill = rows_up - own_b - 1
    stack = lambda first, last: jnp.pad(
        jnp.concatenate([first, last], 0), ((0, fill), (0, 0))
    )
    mine = lambda array: lax.dynamic_slice_in_dim(array, row * own_b, own_b, 0)[:, None]
    labels = stack(mine(labels_b), labels_a[:, None])
    alive_b = mine(live_b).astype(F32)
    alive = stack(alive_b, alive_a)
    once = stack(jnp.ones((own_b, 1), F32), lead.reshape(1, 1))
    whole = np.ones((rows_up, 1), np.float32)
    whole[:own_b], whole[own_b] = whole_b, whole_a
    losses, rows_out, d_x2, d_act = head_step(
        xsum_b, asum_b, sums_a, w_down_head, labels, alive, once, jnp.asarray(whole),
        total.reshape(1, 1), classes,
    )
    loss_sums = jnp.stack(
        [lead * jnp.sum(alive_a * losses[own_b : own_b + 1, :1]),
         jnp.sum(alive_b * losses[:own_b, :1])]
    )

    image_rows = lax.all_gather(rows_out, AXES, axis=0, tiled=True)

    d_x1_b, d0_b, d1_b, d_x1_a, d0_a, d1_a, grad_up_out, grad_gain2 = mlp_back(
        (slope_b, d_act, x1_b, d_x2, *mixed_b),
        (slope_a, d_act, x1_a, d_x2, *mixed_a),
        w_all, gain2, own_b, block,
    )
    d_mixed_a, d_mixed_b = (d0_a, d1_a), (d0_b, d1_b)

    d_alls, d_groups_a = [], []
    for group in range(groups):
        d_all = attend_back_apart(
            qkvs_a[group], qkvs_a[group], d_mixed_a[group], mixed_a[group],
            outs_a[group][2], pairs, span_a, seq * span_a,
        )
        d_alls.append(d_all)
        d_groups_a += [
            shift(d_all[step * span_a : (step + 1) * span_a], "y", seq - step)
            for step in range(1, seq)
        ]
    own_up_out = lax.psum_scatter(
        after(grad_up_out, image_rows, *d_alls), AXES, scatter_dimension=0, tiled=True
    ).astype(F32)
    core = lax.axis_index("core").reshape(1).astype(jnp.int32)
    blocks = lax.axis_size("z") * lax.axis_size("x")
    d_groups_b, own_groups = [], []
    ready = d_alls[-1]
    for group in range(groups):
        got, away, own = attend_back_grad(
            qkvs_b[group],
            after(d_mixed_b[group], ready),
            mixed_b[group], outs_b[group][2],
            h1_b, h1_all, d_alls[group], core, pairs, own_b, whole_b, blocks,
        )
        if group:
            away, own, own_groups[-1] = lax.optimization_barrier((away, own, own_groups[-1]))
        else:
            away, own, *d_groups_a = lax.optimization_barrier((away, own, *d_groups_a))
        d_groups_b.append(got)
        own_groups.append(scatter_rows(away, own))
        ready = got
    moved = seq - 1
    d_groups_a = [
        (d_all, *d_groups_a[group * moved : (group + 1) * moved])
        for group, d_all in enumerate(d_alls)
    ]
    away, own = embed_back(
        x0_b, after(d_x1_b, ready), tab_b, parts_b, d_groups_b,
        x0_a, d_x1_a, tab_a, flat_a, d_groups_a,
        gain1, grad_gain2, w_all, core, blocks, own_b, depths,
    )
    away, own, own_up_out, *own_groups = lax.optimization_barrier(
        (away, own, own_up_out, *own_groups)
    )
    own_qkv = jnp.stack([block_sum(got, rows_own) for got in own_groups], 1)
    own_qkv = own_qkv.reshape(rows_own, groups * pairs, 3, 128)
    own_qkv = own_qkv.transpose(0, 2, 1, 3).reshape(rows_own, 3 * width)
    small_parts = scatter_rows(away, own)

    columns = lambda lo: lax.dynamic_slice_in_dim(
        image_rows[:, lo : lo + width], flat_index * rows_own, rows_own, 1
    )
    own_down = lax.dot_general(
        columns(hidden + width), image_rows[:, :hidden], ROWS_DIM, preferred_element_type=F32
    )
    own_head = lax.dot_general(
        columns(hidden),
        image_rows[:, hidden + 2 * width : hidden + 2 * width + classes],
        ROWS_DIM,
        preferred_element_type=F32,
    )
    own_up, own_out = own_up_out[:, :hidden], own_up_out[:, hidden:]
    square_sum = sum(
        jnp.sum(piece * piece) for piece in (own_up_out, own_down, own_head, own_qkv)
    )
    sums = padded_cols(jnp.concatenate([square_sum.reshape(1), loss_sums])[None], lanes)
    sent, own_small = resize_back(
        small_parts, [jnp.asarray(table) for table in tables], sums, rows_own, depths[0],
        count_all, lanes,
    )
    got = lax.all_to_all(sent, AXES, split_axis=0, concat_axis=0, tiled=True)
    counts = padded_cols(jnp.pad(count, ((0, 0), (1, 0))), lanes)
    turn = lambda arrays: [array.T if at == 4 else array for at, array in enumerate(arrays)]
    *done, grad_norm, size_stats = update(
        got, own_small, (own_qkv, own_out, own_up, own_down, own_head), counts,
        turn(masters), turn(firsts), turn(seconds), rows_kern,
    )
    done = [item for at in (0, 7, 14) for item in turn(done[at : at + 7])]
    return (*done, size_stats.reshape(2), grad_norm.reshape(()))


def fits_fast(mesh, pixels_a, pixels_b):
    dp, seq = mesh.shape["dp"], mesh.shape["seq"]
    images_b, rows_b, grid_b, _ = pixels_b.shape
    rows_a, grid_a = pixels_a.shape[1:3]
    return (
        dp % 8 == 0
        and rows_b % seq == 0
        and rows_a % seq == 0
        and images_b % (dp * seq) == 0
        and images_b // dp <= 256
        and pixels_a.shape[0] == dp
        and grid_b * grid_b % 256 == 0
        and rows_a // seq * grid_a % 32 == 0
    )


def fast_on_device(*args):
    return fast_step(*args[:6], args[6:13], args[13:20], args[20:27])


def on_device(
    pixels_a,
    pixels_b,
    labels_a,
    labels_b,
    live_a,
    live_b,
    qkv_w,
    out_w,
    mlp_w,
    kern_w,
    pos_w,
    head_w,
    gains,
    qkv_m,
    out_m,
    mlp_m,
    kern_m,
    pos_m,
    head_m,
    gains_m,
    qkv_v,
    out_v,
    mlp_v,
    kern_v,
    pos_v,
    head_v,
    gains_v,
):
    masters = (qkv_w, out_w, mlp_w, kern_w, pos_w, head_w, gains)
    firsts = (qkv_m, out_m, mlp_m, kern_m, pos_m, head_m, gains_m)
    seconds = (qkv_v, out_v, mlp_v, kern_v, pos_v, head_v, gains_v)
    bf16 = jnp.bfloat16
    w_qkv, w_out, w_mlp, w_kern, w_pos, w_head, w_gain = (
        lax.all_gather(qkv_w.astype(bf16), ("dp", "seq"), axis=0, tiled=True),
        lax.all_gather(out_w.astype(bf16), ("dp", "seq"), axis=0, tiled=True),
        lax.all_gather(mlp_w.astype(bf16), ("dp", "seq"), axis=1, tiled=True),
        lax.all_gather(kern_w.astype(bf16), ("dp", "seq"), axis=0, tiled=True),
        lax.all_gather(pos_w.astype(bf16), ("dp", "seq"), axis=1, tiled=True),
        lax.all_gather(head_w.astype(bf16), ("dp", "seq"), axis=0, tiled=True),
        lax.all_gather(gains.astype(bf16), ("dp", "seq"), axis=1, tiled=True),
    )
    seq_count = lax.axis_size("seq")
    seq_place = lax.axis_index("seq")
    gain_full = w_gain.astype(jnp.float32)
    kern_full = w_kern.astype(jnp.float32)
    pos_full = w_pos.astype(jnp.float32)
    size_sets = ((pixels_a, labels_a, live_a, PATCH_A), (pixels_b, labels_b, live_b, PATCH_B))
    embeds, flats, kern_backs, pos_backs, layouts = ([], [], [], [], [])
    start = 0
    for pixels, labels, live, patch in size_sets:
        images, rows, grid, depth = pixels.shape
        flat = pixels.reshape(images * rows * grid, depth)
        resized, kern_back = jax.vjp(partial(kernel_resize, patch=patch), kern_full)
        row_table = lax.dynamic_slice_in_dim(interp_matrix(grid, 7), seq_place * rows, rows, 0)
        place, pos_back = jax.vjp(partial(grid_resize, row_table=row_table, grid=grid), pos_full)
        embed = jnp.dot(flat, resized.astype(bf16), preferred_element_type=jnp.float32)
        embed = embed.reshape(images, rows * grid, -1) + place.reshape(1, rows * grid, -1)
        embeds.append(embed.reshape(images * rows * grid, -1))
        flats.append(flat)
        kern_backs.append(kern_back)
        pos_backs.append(pos_back)
        layouts.append((start, start + images * rows * grid, images, rows * grid, grid * grid))
        start = start + images * rows * grid
    x0 = jnp.concatenate(embeds, 0)
    h1_full, norm1_back = jax.vjp(layer_norm, x0, gain_full[0])
    h1 = h1_full.astype(bf16)
    qkv = jnp.dot(h1, w_qkv, preferred_element_type=jnp.float32).astype(bf16)
    width = qkv.shape[1] // 3
    local_kv = qkv[:, width:]
    blocks = [local_kv]
    moving = local_kv
    for turn in range(1, seq_count):
        moving = from_behind(moving, "seq", 1)
        blocks.append(moving)
    all_kv = jnp.stack(blocks, 0)
    mixed_parts, saved = ([], [])
    for first_row, last_row, images, length, whole in layouts:
        query = qkv[first_row:last_row, :width].reshape(images, length, HEADS, HEAD_DIM)
        remote = all_kv[:, first_row:last_row].reshape(
            seq_count, images, length, 2, HEADS, HEAD_DIM
        )
        remote = remote.transpose(1, 0, 2, 3, 4, 5).reshape(
            images, seq_count * length, 2, HEADS, HEAD_DIM
        )
        keys, values = (remote[:, :, 0], remote[:, :, 1])
        attended, norm_log = attend(query, keys, values)
        mixed_parts.append(attended.reshape(last_row - first_row, width))
        saved.append((query, keys, values, norm_log))
    mixed = jnp.concatenate(mixed_parts, 0).astype(bf16)
    x1 = x0 + jnp.dot(mixed, w_out, preferred_element_type=jnp.float32)
    h2_full, norm2_back = jax.vjp(layer_norm, x1, gain_full[1])
    h2 = h2_full.astype(bf16)
    inner = jnp.dot(h2, w_mlp[0], preferred_element_type=jnp.float32)
    act_full, gelu_back = jax.vjp(partial(jax.nn.gelu, approximate=False), inner)
    act = act_full.astype(bf16)
    x2 = x1 + lax.dot_general(act, w_mlp[1], COLS_DIM, preferred_element_type=jnp.float32)
    sum_a = x2[layouts[0][0] : layouts[0][1]].reshape(layouts[0][2], layouts[0][3], -1).sum(1)
    sum_b = x2[layouts[1][0] : layouts[1][1]].reshape(layouts[1][2], layouts[1][3], -1).sum(1)
    pooled_sums = lax.psum((sum_a, sum_b), "seq")
    stats, head_parts = ([], [])
    for index in range(2):
        labels, live = (size_sets[index][1], size_sets[index][2])
        pooled_low = (pooled_sums[index] / float(layouts[index][4])).astype(bf16)
        logits = jnp.dot(pooled_low, w_head, preferred_element_type=jnp.float32)
        norm_log = jax.nn.logsumexp(logits, -1)
        hot = (labels[:, None] == jnp.arange(logits.shape[1], dtype=jnp.int32)[None, :]).astype(
            jnp.float32
        )
        true_logit = jnp.sum(hot * logits, -1)
        alive = live.astype(jnp.float32)
        stats.append(jnp.stack([jnp.sum(alive * (norm_log - true_logit)), jnp.sum(alive)]))
        head_parts.append((pooled_low, jnp.exp(logits - norm_log[:, None]) - hot, alive))
    stats_a, stats_b = lax.psum((stats[0], stats[1]), "dp")
    total = jnp.maximum(stats_a[1] + stats_b[1], 1.0)
    grad_head = jnp.zeros(w_head.shape, jnp.float32)
    d_x2_parts = []
    for index in range(2):
        pooled_low, soft_minus, alive = head_parts[index]
        d_logits = (soft_minus * alive[:, None] / total).astype(bf16)
        grad_head = grad_head + lax.dot_general(
            pooled_low, d_logits, ROWS_DIM, preferred_element_type=jnp.float32
        )
        d_pooled = lax.dot_general(d_logits, w_head, COLS_DIM, preferred_element_type=jnp.float32)
        images, length, whole = (layouts[index][2], layouts[index][3], layouts[index][4])
        spread = jnp.broadcast_to(
            (d_pooled / float(whole))[:, None, :], (images, length, d_pooled.shape[1])
        )
        d_x2_parts.append(spread.reshape(images * length, -1))
    d_x2 = jnp.concatenate(d_x2_parts, 0)
    d_mix = d_x2.astype(bf16)
    grad_down = lax.dot_general(d_mix, act, ROWS_DIM, preferred_element_type=jnp.float32)
    d_act = jnp.dot(d_mix, w_mlp[1], preferred_element_type=jnp.float32)
    d_inner = gelu_back(d_act)[0].astype(bf16)
    grad_up = lax.dot_general(h2, d_inner, ROWS_DIM, preferred_element_type=jnp.float32)
    d_h2 = lax.dot_general(d_inner, w_mlp[0], COLS_DIM, preferred_element_type=jnp.float32)
    d_x1_norm, grad_gain2 = norm2_back(d_h2)
    d_x1 = d_x2 + d_x1_norm
    d_attn = d_x1.astype(bf16)
    grad_out = lax.dot_general(mixed, d_attn, ROWS_DIM, preferred_element_type=jnp.float32)
    d_mixed = lax.dot_general(d_attn, w_out, COLS_DIM, preferred_element_type=jnp.float32).astype(
        bf16
    )
    d_query_parts, d_kv_parts = ([], [])
    for index in range(2):
        first_row, last_row, images, length, whole = layouts[index]
        query, keys, values, norm_log = saved[index]
        d_out = d_mixed[first_row:last_row].reshape(images, length, HEADS, HEAD_DIM)
        d_query, d_keys, d_values = attend_back(query, keys, values, norm_log, d_out)
        d_query_parts.append(d_query.reshape(last_row - first_row, width))
        paired = jnp.stack([d_keys, d_values], 2).reshape(images, seq_count, length, 2 * width)
        d_kv_parts.append(
            paired.transpose(1, 0, 2, 3).reshape(seq_count, last_row - first_row, 2 * width)
        )
    d_all = jnp.concatenate(d_kv_parts, 1)
    mine_kv = d_all[1 % seq_count]
    for turn in range(1, seq_count):
        mine_kv = (
            from_behind(mine_kv.astype(jnp.bfloat16), "seq", 1).astype(mine_kv.dtype)
            + d_all[(turn + 1) % seq_count]
        )
    d_qkv = jnp.concatenate([jnp.concatenate(d_query_parts, 0), mine_kv], 1).astype(bf16)
    grad_qkv = lax.dot_general(h1, d_qkv, ROWS_DIM, preferred_element_type=jnp.float32)
    d_h1 = lax.dot_general(d_qkv, w_qkv, COLS_DIM, preferred_element_type=jnp.float32)
    d_x0_norm, grad_gain1 = norm1_back(d_h1)
    d_x0 = d_x1 + d_x0_norm
    grad_kern = jnp.zeros(kern_full.shape, jnp.float32)
    grad_pos = jnp.zeros(pos_full.shape, jnp.float32)
    for index in range(2):
        first_row, last_row, images, length, whole = layouts[index]
        d_rows = d_x0[first_row:last_row]
        d_kernel = lax.dot_general(
            flats[index], d_rows.astype(bf16), ROWS_DIM, preferred_element_type=jnp.float32
        )
        grad_kern = grad_kern + kern_backs[index](d_kernel)[0]
        d_place = d_rows.reshape(images, length, -1).sum(0)
        grad_pos = grad_pos + pos_backs[index](d_place.reshape(grid_shape(size_sets, index)))[0]
    grad_mlp = jnp.stack([grad_up, grad_down], 0)
    grad_gain = jnp.stack([grad_gain1, grad_gain2], 0)
    grad_head = grad_head / float(seq_count)
    owned = (
        lax.psum_scatter(grad_qkv, ("dp", "seq"), scatter_dimension=0, tiled=True),
        lax.psum_scatter(grad_out, ("dp", "seq"), scatter_dimension=0, tiled=True),
        lax.psum_scatter(grad_mlp, ("dp", "seq"), scatter_dimension=1, tiled=True),
        lax.psum_scatter(grad_kern, ("dp", "seq"), scatter_dimension=0, tiled=True),
        lax.psum_scatter(grad_pos, ("dp", "seq"), scatter_dimension=1, tiled=True),
        lax.psum_scatter(grad_head, ("dp", "seq"), scatter_dimension=0, tiled=True),
        lax.psum_scatter(grad_gain, ("dp", "seq"), scatter_dimension=1, tiled=True),
    )
    square_sum = sum((jnp.sum(piece * piece) for piece in owned))
    grad_norm = jnp.sqrt(lax.psum(square_sum, ("dp", "seq")))
    factor = jnp.minimum(1.0, CLIP / (grad_norm + 1e-06))
    done = [adamw(masters[i], firsts[i], seconds[i], owned[i] * factor, RATES[i]) for i in range(7)]
    size_stats = jnp.stack(
        [stats_a[0] / jnp.maximum(stats_a[1], 1.0), stats_b[0] / jnp.maximum(stats_b[1], 1.0)]
    )
    return (
        done[0][0],
        done[1][0],
        done[2][0],
        done[3][0],
        done[4][0],
        done[5][0],
        done[6][0],
        done[0][1],
        done[1][1],
        done[2][1],
        done[3][1],
        done[4][1],
        done[5][1],
        done[6][1],
        done[0][2],
        done[1][2],
        done[2][2],
        done[3][2],
        done[4][2],
        done[5][2],
        done[6][2],
        size_stats,
        grad_norm,
    )


def specs(row, col):
    both = (*row, *col)
    owned = (
        P(both, None), P(both, None), P(None, both, None), P(both, None), P(None, both),
        P(both, None), P(None, both),
    )
    images = P(row, col, None, None)
    return (images, images, P(row), P(row), P(row), P(row), *owned * 3), (*owned * 3, P(), P())


def solution(mesh):
    dp, seq = mesh.shape["dp"], mesh.shape["seq"]

    def run(*args):
        if fits_fast(mesh, args[0], args[1]):
            split = Mesh(mesh.devices.reshape(4, dp // 8, 2, seq), AXES)
            placed, given = specs(AXES[:3], AXES[3:])
            step = jax.shard_map(
                fast_on_device, mesh=split, in_specs=placed, out_specs=given, check_vma=False
            )
        else:
            placed, given = specs(("dp",), ("seq",))
            step = jax.shard_map(
                on_device, mesh=mesh, in_specs=placed, out_specs=given, check_vma=False
            )
        return step(*args)

    return run
```

```python
import math
from functools import partial

import jax
import jax.numpy as jnp
import ml_dtypes
import numpy as np
from jax import lax
from jax.experimental import pallas as pl
from jax.experimental.pallas import tpu as pltpu
from jax.sharding import Mesh
from jax.sharding import PartitionSpec as P

HEADS = 12
HEAD_DIM = 64
BASE = 32
PATCH_A = 10
PATCH_B = 12


HIGH = lax.Precision.HIGHEST
RATES = (0.012, 0.2, 0.012, 0.03, 0.15, 0.06, 0.25)
CLIP = 0.001
ROWS_DIM = (((0,), (0,)), ((), ()))
COLS_DIM = (((1,), (1,)), ((), ()))


def from_behind(value, axis, steps):
    count = lax.axis_size(axis)
    pairs = [(source, (source + steps) % count) for source in range(count)]
    return lax.ppermute(value, axis, pairs)


def interp_matrix(n_out, n_in):
    places = jnp.arange(n_out, dtype=jnp.float32) * ((n_in - 1) / (n_out - 1))
    return jnp.maximum(
        0.0, 1.0 - jnp.abs(places[:, None] - jnp.arange(n_in, dtype=jnp.float32)[None, :])
    )


def pinv_table(patch):
    basis = interp_matrix(patch, BASE)
    gram = jnp.dot(basis, basis.T, precision=HIGH)
    factor = jnp.linalg.cholesky(gram)
    return jax.scipy.linalg.cho_solve((factor, True), basis)


def layer_norm(values, gain):
    centred = values - jnp.mean(values, -1, keepdims=True)
    spread = jnp.mean(centred * centred, -1, keepdims=True)
    return centred * lax.rsqrt(spread + 1e-06) * gain


def kernel_resize(kernel, patch):
    table = pinv_table(patch)
    shaped = kernel.reshape(3, BASE, BASE, -1)
    return jnp.einsum("ia,jb,cabd->cijd", table, table, shaped, precision=HIGH).reshape(
        3 * patch * patch, -1
    )


def grid_resize(position, row_table, grid):
    table = interp_matrix(grid, 7)
    return jnp.einsum(
        "ia,jb,abd->ijd", row_table, table, position.reshape(7, 7, -1), precision=HIGH
    )


def adamw(weight, first, second, grad, rate):
    first = 0.9 * first + 0.1 * grad
    second = 0.999 * second + 0.001 * grad * grad
    step_dir = first / (1.0 - 0.9**3) / (jnp.sqrt(second / (1.0 - 0.999**3)) + 1e-08)
    return (weight - rate * (step_dir + 0.1 * weight), first, second)


def attend(query, keys, values):
    scores = jnp.einsum(
        "ithe,ishe->ihts", query, keys, preferred_element_type=jnp.float32
    ) * HEAD_DIM ** (-0.5)
    norm_log = jax.nn.logsumexp(scores, -1, keepdims=True)
    probs = jnp.exp(scores - norm_log).astype(jnp.bfloat16)
    return (
        jnp.einsum("ihts,ishe->ithe", probs, values, preferred_element_type=jnp.float32),
        norm_log,
    )


def attend_back(query, keys, values, norm_log, d_out):
    scale = HEAD_DIM ** (-0.5)
    scores = jnp.einsum("ithe,ishe->ihts", query, keys, preferred_element_type=jnp.float32) * scale
    probs = jnp.exp(scores - norm_log)
    d_probs = jnp.einsum("ithe,ishe->ihts", d_out, values, preferred_element_type=jnp.float32)
    d_scores = (probs * (d_probs - jnp.sum(probs * d_probs, -1, keepdims=True))).astype(
        jnp.bfloat16
    )
    d_query = (
        jnp.einsum("ihts,ishe->ithe", d_scores, keys, preferred_element_type=jnp.float32) * scale
    )
    d_keys = (
        jnp.einsum("ihts,ithe->ishe", d_scores, query, preferred_element_type=jnp.float32) * scale
    )
    d_values = jnp.einsum(
        "ihts,ithe->ishe", probs.astype(jnp.bfloat16), d_out, preferred_element_type=jnp.float32
    )
    return (d_query, d_keys, d_values)


def grid_shape(size_sets, index):
    pixels = size_sets[index][0]
    return (pixels.shape[1], pixels.shape[2], -1)


AXES = ("z", "x", "core", "y")
CHIPS = ("z", "x", "y")
NT = (((1,), (1,)), ((), ()))
NN = (((1,), (0,)), ((), ()))
BF = jnp.bfloat16
F32 = jnp.float32
VMEM_BYTES = 58 << 20
QUERY_SCALE = HEAD_DIM**-0.5 * math.log2(math.e)


def shift(value, axis, steps):
    count = lax.axis_size(axis)
    pairs = [(source, (source + steps) % count) for source in range(count)]
    return lax.ppermute(value, axis, pairs)


def chip_sizes():
    return tuple(lax.axis_size(axis) for axis in CHIPS)


def gather_rows(value, beside):
    rows, cols = value.shape
    z, x, y = chip_sizes()
    chips = z * x * y
    copies = jnp.broadcast_to(value[None], (chips, rows, cols)).reshape(chips * rows, cols)
    mine = lax.all_to_all(copies, CHIPS, split_axis=0, concat_axis=0, tiled=True)
    mine, *beside = lax.optimization_barrier((mine, *beside))
    other = shift(mine, "core", 1)
    parts = [part.reshape(z, x, 1, y, rows, cols) for part in (mine, other)]
    first = lax.axis_index("core") == 0
    both = jnp.concatenate(
        [jnp.where(first, parts[0], parts[1]), jnp.where(first, parts[1], parts[0])], 2
    )
    return both.reshape(2 * chips * rows, cols), beside


STAGES = (*CHIPS, "core")


def stage(held, axis):
    return [held] + [shift(held, axis, step) for step in range(1, lax.axis_size(axis))]


def stage_owners():
    strides, stride = {}, 1
    for axis in reversed(AXES):
        strides[axis] = stride
        stride = stride * lax.axis_size(axis)
    shifts = [{}]
    for axis in STAGES:
        shifts = [{**known, axis: step} for step in range(lax.axis_size(axis)) for known in shifts]
    owner = jnp.zeros((stride,), jnp.int32)
    for axis in AXES:
        steps = np.array([known[axis] for known in shifts], np.int32)
        owner = owner + ((lax.axis_index(axis) - steps) % lax.axis_size(axis)) * strides[axis]
    return owner


def place_blocks_kernel(owner_ref, *refs):
    *pieces, out_ref, sems = refs
    copies = []
    for piece in pieces:
        for index in range(piece.shape[0]):
            block = len(copies)
            copies.append(
                pltpu.make_async_copy(
                    piece.at[index], out_ref.at[owner_ref[block]], sems.at[block]
                )
            )
    for copy in copies:
        copy.start()
    for copy in copies:
        copy.wait()


def place_blocks(pieces, owner):
    count = owner.shape[0]
    _, rows, cols = pieces[0].shape
    out = pl.pallas_call(
        place_blocks_kernel,
        out_shape=jax.ShapeDtypeStruct((count, rows, cols), BF),
        in_specs=[pl.BlockSpec(memory_space=pltpu.SMEM)]
        + [pl.BlockSpec(memory_space=pl.ANY)] * len(pieces),
        out_specs=pl.BlockSpec(memory_space=pltpu.VMEM),
        scratch_shapes=[pltpu.SemaphoreType.DMA((count,))],
        compiler_params=pltpu.CompilerParams(vmem_limit_bytes=VMEM_BYTES),
        cost_estimate=estimate(0, count * rows * cols * 4, 1),
        name="place_blocks",
    )(owner, *pieces)
    return out.reshape(count * rows, cols)


def scatter_rows(away, own):
    both = (own.astype(F32) + shift(away, "core", 1).astype(F32)).astype(BF)
    return lax.all_to_all(both, CHIPS, split_axis=0, concat_axis=0, tiled=True)


def block_sum(got):
    return jnp.sum(got.astype(F32), 0)


def store_by_core(core, acc, away_ref, own_ref, cols, count):
    blocks, rows, _ = own_ref.shape
    per = blocks // count
    for pair in range(count):
        for side, ref in ((core, own_ref), (1 - core, away_ref)):
            for block in range(per):
                first = pl.multiple_of(((2 * pair + side) * per + block) * rows, rows)
                ref[pair * per + block, :, cols] = acc[pl.ds(first, rows), :].astype(BF)


def interp_table(n_out, n_in):
    places = np.arange(n_out) * ((n_in - 1) / (n_out - 1))
    return np.maximum(0.0, 1.0 - np.abs(places[:, None] - np.arange(n_in)[None, :]))


def resize_table(patch):
    basis = interp_table(patch, BASE)
    table = np.linalg.solve(basis @ basis.T, basis)
    return np.kron(table, table).astype(np.float32)


def place_table(grid):
    table = interp_table(grid, 7)
    full = np.kron(table, table).astype(np.float32)
    high = full.astype(ml_dtypes.bfloat16)
    low = (full - high.astype(np.float32)).astype(ml_dtypes.bfloat16)
    return np.concatenate([high, low, np.zeros((grid * grid, 30), ml_dtypes.bfloat16)], 1)


def dot(left, right, dims):
    return lax.dot_general(left, right, dims, preferred_element_type=F32)


def estimate(flops, nbytes, share=32):
    return pl.CostEstimate(
        flops=int(flops) // share, bytes_accessed=int(nbytes) // share, transcendentals=0
    )


def normed(values):
    centred = values - jnp.mean(values, -1, keepdims=True)
    scale = lax.rsqrt(jnp.mean(centred * centred, -1, keepdims=True) + 1e-06)
    return centred * scale, scale


def norm_back(d_out, gain, hat, scale):
    d_hat = d_out * gain
    return scale * (
        d_hat
        - jnp.mean(d_hat, -1, keepdims=True)
        - hat * jnp.mean(d_hat * hat, -1, keepdims=True)
    )


def embed_kernel(*refs, pieces, at, depth, spot):
    pixel_refs, (tab_ref, weight_ref, gain_ref, *rest) = refs[:pieces], refs[pieces:]
    x0_ref, h1_ref = rest
    shares = 2 if tab_ref.shape[0] % 512 == 0 else 1
    count = tab_ref.shape[0] // shares

    def body(pixel_ref):
        for share in range(shares):
            rows = slice(share * count, (share + 1) * count)
            x0 = dot(tab_ref[rows], weight_ref[:, spot : spot + tab_ref.shape[1]], NT)
            x0 = x0 + dot(pixel_ref[rows], weight_ref[:, at : at + depth], NT)
            x0_ref[rows] = x0
            h1_ref[rows] = (normed(x0)[0] * gain_ref[...]).astype(BF)

    for piece, pixel_ref in enumerate(pixel_refs):
        pl.when(pl.program_id(1) == piece)(partial(body, pixel_ref))


def embed(pieces, tab, weight, at, spot, gain, images):
    count, depth = len(pieces), pieces[0].shape[1]
    block = tab.shape[0] // count
    rows, width = images * tab.shape[0], weight.shape[0]
    still = lambda array: pl.BlockSpec(array.shape, lambda i, j: (0, 0))
    moving = lambda cols: pl.BlockSpec((block, cols), lambda i, j: (i * count + j, 0))
    outs = [(width, F32), (width, BF)]
    return pl.pallas_call(
        partial(embed_kernel, pieces=count, at=at, depth=depth, spot=spot),
        out_shape=tuple(jax.ShapeDtypeStruct((rows, cols), kind) for cols, kind in outs),
        grid=(images, count),
        in_specs=[pl.BlockSpec((block, depth), lambda i, j: (i, 0))] * count
        + [pl.BlockSpec((block, tab.shape[1]), lambda i, j: (j, 0)), still(weight), still(gain)],
        out_specs=[moving(cols) for cols, _ in outs],
        compiler_params=pltpu.CompilerParams(vmem_limit_bytes=VMEM_BYTES),
        cost_estimate=estimate(2 * rows * width * width, rows * width * 8, 1),
        name="embed",
    )(*pieces, tab, weight, gain)


def head_split(first, values):
    zero = jnp.zeros((), values.dtype)
    return jnp.where(first, values, zero), jnp.where(first, zero, values)


def attend_pair(rows_ref, n_query, out_ref, log_ref, between=None):
    lane = lax.broadcasted_iota(jnp.int32, (1, 128), 1)
    first = lane < HEAD_DIM
    one = jnp.ones((), BF)
    values = rows_ref[:, 256:]
    keys = head_split(first, rows_ref[:, 128:256])
    sided = (jnp.where(first, values, one).T, jnp.where(first, one, values).T)
    query = rows_ref[:n_query, :128]
    scores = [dot(keys[head], query, NT) for head in range(2)]
    if between is not None:
        between()
    tops, probs, mixed = [], [], []
    for head in range(2):
        tops.append(jnp.max(scores[head], 0, keepdims=True))
        probs.append(jnp.exp2(scores[head] - tops[head]).astype(BF))
        mixed.append(dot(sided[head], probs[head], NN))
    outs = []
    for head in range(2):
        at = HEAD_DIM * (1 - head)
        total = mixed[head][at : at + 1]
        own = HEAD_DIM * head
        outs.append(mixed[head][own : own + HEAD_DIM] / total)
        log_ref[0, 0, head : head + 1, :] = tops[head] + jnp.log2(total)
    out_ref[...] = jnp.concatenate(outs, 0).T.astype(BF)


def attend_kernel(h1_ref, weight_ref, qkv_ref, out_ref, log_ref, held, *, items, n_query):
    step = pl.program_id(0)

    def project():
        lane = lax.broadcasted_iota(jnp.int32, (1, 384), 1)
        scale = jnp.where(lane < 128, QUERY_SCALE, 1.0)
        rows = (dot(h1_ref[...], weight_ref[...], NN) * scale).astype(BF)
        qkv_ref[...] = rows
        held[step % 2] = rows

    def attend(between=None):
        attend_pair(held.at[(step + 1) % 2], n_query, out_ref, log_ref, between)

    @pl.when(step == 0)
    def _():
        project()

    @pl.when((step > 0) & (step < items))
    def _():
        attend(project)

    @pl.when(step == items)
    def _():
        attend()


def attend_pairs(h1, weight, first, pairs, images, n_query):
    rows, width = h1.shape
    count = rows // images
    items = images * pairs
    now = lambda s: jnp.minimum(s, items - 1)
    last = lambda s: jnp.maximum(s - 1, 0)
    return pl.pallas_call(
        partial(attend_kernel, items=items, n_query=n_query),
        out_shape=(
            jax.ShapeDtypeStruct((rows, pairs * 384), BF),
            jax.ShapeDtypeStruct((images * n_query, pairs * 128), BF),
            jax.ShapeDtypeStruct((images, pairs, 2, n_query), F32),
        ),
        grid=(items + 1,),
        in_specs=[
            pl.BlockSpec((count, width), lambda s: (now(s) // pairs, 0)),
            pl.BlockSpec((width, 384), lambda s: (0, first + now(s) % pairs)),
        ],
        out_specs=[
            pl.BlockSpec((count, 384), lambda s: (now(s) // pairs, now(s) % pairs)),
            pl.BlockSpec((n_query, 128), lambda s: (last(s) // pairs, last(s) % pairs)),
            pl.BlockSpec(
                (1, 1, 2, n_query), lambda s: (last(s) // pairs, last(s) % pairs, 0, 0)
            ),
        ],
        scratch_shapes=[pltpu.VMEM((2, count, 384), BF)],
        compiler_params=pltpu.CompilerParams(vmem_limit_bytes=VMEM_BYTES),
        cost_estimate=estimate(
            2 * items * count * (n_query * 1200 + width * 384), rows * width * 8, 1
        ),
        name="attend",
    )(h1, weight)


def attend_back_pair(q_ref, kv_ref, do_ref, o_ref, log_ref):
    lane = lax.broadcasted_iota(jnp.int32, (1, 128), 1)
    first = lane < HEAD_DIM
    scale = jnp.asarray(HEAD_DIM**-0.5, BF)
    keys_all = kv_ref[:, 128:256]
    keys = head_split(first, keys_all)
    values = head_split(first, kv_ref[:, 256:])
    query = q_ref[:, :128]
    d_out = do_ref[...]
    queries = head_split(first, query)
    d_outs = head_split(first, d_out)
    keys_t = tuple(part.T for part in head_split(first, keys_all * scale))
    both = (d_out.astype(F32) * o_ref[...].astype(F32)).T
    d_query, d_keys, d_values = 0.0, 0.0, 0.0
    for head in range(2):
        row = jnp.sum(both[HEAD_DIM * head : HEAD_DIM * (head + 1)], 0, keepdims=True)
        scores = dot(keys[head], query, NT)
        probs = jnp.exp2(scores - log_ref[0, 0, head : head + 1, :])
        d_probs = dot(values[head], d_out, NT)
        d_scores = (probs * (d_probs - row)).astype(BF)
        d_keys = d_keys + dot(d_scores, queries[head], NN)
        d_values = d_values + dot(probs.astype(BF), d_outs[head], NN)
        d_query = d_query + dot(keys_t[head], d_scores, NN)
    return d_query.astype(BF), (d_keys * math.log(2.0)).astype(BF), d_values.astype(BF)


def attend_back_kernel(q_ref, kv_ref, do_ref, o_ref, log_ref, d_ref):
    parts = attend_back_pair(q_ref, kv_ref, do_ref, o_ref, log_ref)
    rows = parts[0].shape[1]
    d_ref[:rows, :128] = parts[0].T
    d_ref[rows:, :128] = jnp.zeros((d_ref.shape[0] - rows, 128), BF)
    for index, part in enumerate(parts[1:], 1):
        d_ref[:, 128 * index : 128 * (index + 1)] = part


def attend_back_apart(query, keys, d_out, out, log, pairs, n_query, n_key):
    over_q = lambda cols: pl.BlockSpec((n_query, cols), lambda h: (0, h))
    over_k = lambda cols: pl.BlockSpec((n_key, cols), lambda h: (0, h))
    return pl.pallas_call(
        attend_back_kernel,
        out_shape=jax.ShapeDtypeStruct((n_key, pairs * 384), BF),
        grid=(pairs,),
        in_specs=[
            over_q(384),
            over_k(384),
            over_q(128),
            over_q(128),
            pl.BlockSpec((1, 1, 2, n_query), lambda h: (0, h, 0, 0)),
        ],
        out_specs=over_k(384),
        compiler_params=pltpu.CompilerParams(vmem_limit_bytes=VMEM_BYTES),
        cost_estimate=estimate(2 * pairs * n_query * n_key * 2400, (n_query + n_key) * pairs * 1024),
        name="attend_back_apart",
    )(query, keys, d_out, out, log)


def attend_back_grad_kernel(
    core_ref, qkv_ref, do_ref, o_ref, log_ref, h1_ref, h1_a_ref, d_a_ref,
    d_ref, away_ref, own_ref, acc, turned, *, images, blocks
):
    image = pl.program_id(1)

    @pl.when(image == 0)
    def _():
        acc[...] = dot(d_a_ref[...].T, h1_a_ref[...], NN)

    d_query, d_keys, d_values = attend_back_pair(qkv_ref, qkv_ref, do_ref, o_ref, log_ref)
    d_ref[:, :128] = d_query.T
    d_ref[:, 128:256] = d_keys
    d_ref[:, 256:] = d_values
    d_turned = jnp.concatenate([d_query, d_keys.T, d_values.T], 0)
    acc[...] += dot(d_turned, h1_ref[...], NN)

    @pl.when(image == images - 1)
    def _():
        turned[...] = acc[...].T
        store_by_core(core_ref[0], turned, away_ref, own_ref, slice(None), blocks)


def attend_back_grad(
    qkv, d_out, out, log, h1, h1_a, d_a, core, pairs, images, count, blocks, count_y
):
    width = h1.shape[1]
    rows_a = h1_a.shape[0]
    over = lambda cols: pl.BlockSpec((count, cols), lambda h, i: (i, h))
    held = (count_y * blocks, width // (2 * count_y * blocks))
    grad = pl.BlockSpec((*held, 384), lambda h, i: (0, 0, h))
    return pl.pallas_call(
        partial(attend_back_grad_kernel, images=images, blocks=blocks),
        out_shape=(
            jax.ShapeDtypeStruct((images * count, pairs * 384), BF),
            jax.ShapeDtypeStruct((*held, pairs * 384), BF),
            jax.ShapeDtypeStruct((*held, pairs * 384), BF),
        ),
        grid=(pairs, images),
        in_specs=[
            pl.BlockSpec(memory_space=pltpu.SMEM),
            over(384),
            over(128),
            over(128),
            pl.BlockSpec((1, 1, 2, count), lambda h, i: (i, h, 0, 0)),
            pl.BlockSpec((count, width), lambda h, i: (i, 0)),
            pl.BlockSpec((rows_a, width), lambda h, i: (0, 0)),
            pl.BlockSpec((rows_a, 384), lambda h, i: (0, h)),
        ],
        out_specs=[over(384), grad, grad],
        scratch_shapes=[
            pltpu.VMEM((384, width), F32),
            pltpu.VMEM((width, 384), F32),
        ],
        compiler_params=pltpu.CompilerParams(vmem_limit_bytes=VMEM_BYTES),
        cost_estimate=estimate(
            images * 2 * pairs * count * count * 2800, images * count * pairs * 2048
        ),
        name="attend_back",
    )(core, qkv, d_out, out, log, h1, h1_a, d_a)


def gelu_parts(inner):
    scaled = inner * (0.5**0.5)
    upper = 0.5 * lax.erf(scaled) + 0.5
    bell = jnp.exp2(scaled * scaled * -math.log2(math.e) - 0.5 * math.log2(2.0 * math.pi))
    return upper, inner * bell


def mlp_kernel(
    x0_ref, mixed0_ref, mixed1_ref, wout_ref, gain_ref, wup_ref,
    x1_ref, slope_ref, xsum_ref, asum_ref, *, per
):
    mixed = jnp.concatenate([mixed0_ref[...], mixed1_ref[...]], 1)
    x1 = x0_ref[...] + dot(mixed, wout_ref[...], NN)
    x1_ref[...] = x1
    h2 = (normed(x1)[0] * gain_ref[...]).astype(BF)

    @pl.when(pl.program_id(0) % per == 0)
    def _():
        xsum_ref[...] = jnp.zeros_like(xsum_ref)
        asum_ref[...] = jnp.zeros_like(asum_ref)

    xsum_ref[0] += jnp.sum(x1, 0, keepdims=True)
    width = 512
    for first in range(0, wup_ref.shape[1], width):
        cols = slice(first, first + width)
        inner = dot(h2, wup_ref[:, cols], NN)
        upper, slope = gelu_parts(inner)
        slope_ref[:, cols] = (upper + slope).astype(BF)
        asum_ref[0, :, cols] += jnp.sum(inner * upper, 0, keepdims=True)


def mlp(x0, mixed, w_all, hidden, gain, images, block):
    rows, width = x0.shape
    per = rows // images // block
    return pl.pallas_call(
        partial(mlp_kernel, per=per),
        out_shape=(
            jax.ShapeDtypeStruct((rows, width), F32),
            jax.ShapeDtypeStruct((rows, hidden), BF),
            jax.ShapeDtypeStruct((images, 1, width), F32),
            jax.ShapeDtypeStruct((images, 1, hidden), F32),
        ),
        grid=(rows // block,),
        in_specs=[
            pl.BlockSpec((block, width), lambda i: (i, 0)),
            pl.BlockSpec((block, width // 2), lambda i: (i, 0)),
            pl.BlockSpec((block, width // 2), lambda i: (i, 0)),
            pl.BlockSpec((width, width), lambda i: (0, 3)),
            pl.BlockSpec((1, width), lambda i: (0, 0)),
            pl.BlockSpec((width, hidden), lambda i: (0, 4 * width // hidden)),
        ],
        out_specs=[
            pl.BlockSpec((block, width), lambda i: (i, 0)),
            pl.BlockSpec((block, hidden), lambda i: (i, 0)),
            pl.BlockSpec((1, 1, width), lambda i: (i // per, 0, 0)),
            pl.BlockSpec((1, 1, hidden), lambda i: (i // per, 0, 0)),
        ],
        compiler_params=pltpu.CompilerParams(vmem_limit_bytes=VMEM_BYTES),
        cost_estimate=estimate(4 * rows * width * (hidden + width), rows * hidden * 4),
        name="mlp",
    )(x0, *mixed, w_all, gain, w_all)


def head_kernel(
    image_ref, xsum_ref, asum_ref, sums_a_ref, down_ref, head_ref, whole_ref, total_ref,
    loss_ref, rows_ref, dx2_ref, dact_ref, *, classes, own, slots
):
    width, hidden = down_ref.shape
    fill = rows_ref.shape[0] - own - 1
    place_y = image_ref[2 * slots + 2]

    def column(values):
        row = lax.broadcasted_iota(jnp.int32, (own + 1 + fill, 1), 0)
        out = jnp.zeros_like(row)
        for index, value in enumerate(values):
            out = jnp.where(row == index, value, out)
        return out

    def of_images(first, last):
        return column([image_ref[first + place_y * own + i] for i in range(own)] + [image_ref[last]])

    label = of_images(0, 2 * slots)
    alive = of_images(slots, 2 * slots + 1).astype(F32)
    once = column([1] * own + [jnp.where(place_y == 0, 1, 0)]).astype(F32)

    def stacked(ref, cols):
        rows = [ref[image] for image in range(own)] + [sums_a_ref[:, cols]]
        return jnp.concatenate(rows + [jnp.zeros((fill, rows[0].shape[1]), F32)], 0)

    xsum = stacked(xsum_ref, slice(0, width))
    asum = stacked(asum_ref, slice(width, width + hidden))
    high = asum.astype(BF)
    low = (asum - high.astype(F32)).astype(BF)
    whole = whole_ref[...]
    down = down_ref[...]
    both = dot(jnp.concatenate([high, low], 0), down, NT)
    pooled = (xsum + (both[: both.shape[0] // 2] + both[both.shape[0] // 2 :])) / whole
    pooled_low = pooled.astype(BF)
    head = head_ref[...]
    place = lax.broadcasted_iota(jnp.int32, (1, head.shape[1]), 1)
    logits = jnp.where(place < classes, dot(pooled_low, head, NN), -1e30)
    top = jnp.max(logits, -1, keepdims=True)
    norm_log = top + jnp.log(jnp.sum(jnp.exp(logits - top), -1, keepdims=True))
    hot = place == label
    true_logit = jnp.sum(jnp.where(hot, logits, 0.0), -1, keepdims=True)
    loss = (norm_log - true_logit) * alive * once
    lane = lax.broadcasted_iota(jnp.int32, (1, loss_ref.shape[1]), 1)
    loss_a, loss_b = loss[own : own + 1], jnp.sum(loss[:own], 0, keepdims=True)
    loss_ref[...] = jnp.where(lane == 1, loss_a, jnp.where(lane == 2, loss_b, 0.0))
    soft = jnp.exp(logits - norm_log) - hot.astype(F32)
    d_logits = (soft * alive / total_ref[...]).astype(BF)
    d_x2 = dot(d_logits, head, NT) / whole
    d_mix = d_x2.astype(BF)
    d_act = dot(d_mix, down, NN)
    for image in range(own + 1):
        dx2_ref[image] = d_x2[image : image + 1]
        dact_ref[image] = d_act[image : image + 1]
    rows_ref[:, :hidden] = high
    rows_ref[:, hidden : hidden + width] = pooled_low
    rows_ref[:, hidden + width : hidden + 2 * width] = (d_mix * once).astype(BF)
    rows_ref[:, hidden + 2 * width :] = (d_logits * once).astype(BF)


def head_step(images, xsum, asum, sums_a, w_down_head, whole, total, classes):
    own, _, width = xsum.shape
    hidden = asum.shape[2]
    rows = whole.shape[0]
    padded = w_down_head.shape[1] - hidden
    spec = lambda shape, *place: pl.BlockSpec(shape, lambda i: place or (0,) * len(shape))
    shapes = (
        ((1, 128), F32),
        ((rows, hidden + 2 * width + padded), BF),
        ((own + 1, 1, width), F32),
        ((own + 1, 1, hidden), F32),
    )
    return pl.pallas_call(
        partial(head_kernel, classes=classes, own=own, slots=(images.shape[0] - 3) // 2),
        out_shape=tuple(jax.ShapeDtypeStruct(*shape) for shape in shapes),
        grid=(1,),
        in_specs=[
            pl.BlockSpec(memory_space=pltpu.SMEM),
            spec(xsum.shape),
            spec(asum.shape),
            spec(sums_a.shape),
            spec((width, hidden), 0, 0),
            spec((width, padded), 0, hidden // padded),
            spec((rows, 1)),
            spec((1, 1)),
        ],
        out_specs=[spec(shape[0]) for shape in shapes],
        compiler_params=pltpu.CompilerParams(vmem_limit_bytes=VMEM_BYTES),
        cost_estimate=estimate(1 << 32, 8 << 20),
        name="head",
    )(images, xsum, asum, sums_a, w_down_head, w_down_head, whole, total)


def mlp_back_kernel(*refs, steps):
    parts = (refs[0:6], refs[6:12])
    wout_ref, gain_ref, wup_ref = refs[12:15]
    outs = (refs[15:18], refs[18:21])
    grad_ref, ggain_ref = refs[21:23]
    up_acc, out_acc = refs[23:25]
    step = pl.program_id(0)

    def body(inputs, outputs, begin):
        slope_ref, dact_ref, x1_ref, dx2_ref, *mixed_refs = inputs
        dx1_ref, *dmixed_refs = outputs
        gain = gain_ref[...]
        hat, scale = normed(x1_ref[...])
        h2_t = (hat * gain).astype(BF).T
        width = 768
        cuts = [slice(first, first + width) for first in range(0, slope_ref.shape[1], width)]
        d_inner = [
            (slope_ref[:, cols].astype(F32) * dact_ref[0, :, cols]).astype(BF) for cols in cuts
        ]
        d_h2 = sum(dot(part, wup_ref[:, cols], NT) for part, cols in zip(d_inner, cuts))
        gain_grad = jnp.sum(d_h2 * hat, 0, keepdims=True)
        ggain_ref[...] = gain_grad if begin else ggain_ref[...] + gain_grad
        rows = x1_ref.shape[0] // len(cuts)
        for index, (part, cols) in enumerate(zip(d_inner, cuts)):
            share = slice(index * rows, (index + 1) * rows)
            grad = dot(h2_t, part, NN)
            up_acc[:, cols] = grad if begin else up_acc[:, cols] + grad
            dx1_ref[share] = dx2_ref[0] + norm_back(d_h2[share], gain, hat[share], scale[share])
        d_attn = dx1_ref[...].astype(BF)
        mixed = jnp.concatenate([mixed_ref[...] for mixed_ref in mixed_refs], 1)
        grad = dot(mixed.T, d_attn, NN)
        out_acc[...] = grad if begin else out_acc[...] + grad
        d_mixed = dot(d_attn, wout_ref[...], NT).astype(BF)
        half = mixed_refs[0].shape[1]
        for index, dmixed_ref in enumerate(dmixed_refs):
            dmixed_ref[...] = d_mixed[:, index * half : (index + 1) * half]

    @pl.when(step == 0)
    def _():
        body(parts[1], outs[1], True)

    @pl.when(step > 0)
    def _():
        body(parts[0], outs[0], False)

    @pl.when(step == steps)
    def _():
        hidden = up_acc.shape[1]
        grad_ref[:, :hidden] = up_acc[...].astype(BF)
        grad_ref[:, hidden:] = out_acc[...].astype(BF)


def mlp_back(part_b, part_a, w_all, gain, images, block):
    rows, width = part_b[2].shape
    rows_a = part_a[2].shape[0]
    hidden = part_b[0].shape[1]
    steps = rows // block
    per = steps // images
    at = lambda i: jnp.maximum(i - 1, 0)
    moving = lambda cols: pl.BlockSpec((block, cols), lambda i: (at(i), 0))
    still = lambda shape: pl.BlockSpec(shape, lambda i: (0,) * len(shape))
    image = lambda cols: pl.BlockSpec((1, 1, cols), lambda i: (at(i) // per, 0, 0))
    last = lambda cols: pl.BlockSpec((1, 1, cols), lambda i: (images, 0, 0))
    half = width // 2
    outs = []
    for count in (rows, rows_a):
        outs += [
            jax.ShapeDtypeStruct((count, width), F32),
            jax.ShapeDtypeStruct((count, half), BF),
            jax.ShapeDtypeStruct((count, half), BF),
        ]
    return pl.pallas_call(
        partial(mlp_back_kernel, steps=steps),
        out_shape=(
            *outs,
            jax.ShapeDtypeStruct((width, hidden + width), BF),
            jax.ShapeDtypeStruct((1, width), F32),
        ),
        grid=(steps + 1,),
        in_specs=[
            moving(hidden), image(hidden), moving(width), image(width), moving(half), moving(half),
            still((rows_a, hidden)), last(hidden), still((rows_a, width)),
            last(width), still((rows_a, half)), still((rows_a, half)),
            pl.BlockSpec((width, width), lambda i: (0, 3)),
            still((1, width)),
            pl.BlockSpec((width, hidden), lambda i: (0, 4 * width // hidden)),
        ],
        out_specs=[
            moving(width), moving(half), moving(half),
            still((rows_a, width)), still((rows_a, half)), still((rows_a, half)),
            still((width, hidden + width)), still((1, width)),
        ],
        scratch_shapes=[pltpu.VMEM((width, hidden), F32), pltpu.VMEM((width, width), F32)],
        compiler_params=pltpu.CompilerParams(vmem_limit_bytes=VMEM_BYTES),
        cost_estimate=estimate(
            4 * (rows + rows_a) * width * (hidden + width), (rows + rows_a) * hidden * 4
        ),
        name="mlp_back",
    )(*part_b, *part_a, w_all, gain, w_all)


def embed_back_kernel(core_ref, *refs, steps, groups, pieces, blocks, parts_b, parts_a):
    n_b, n_a = 3 + pieces + groups, 4 + groups * parts_a
    inputs_b, inputs_a = refs[:n_b], refs[n_b : n_b + n_a]
    gain_ref, gain_grad_ref, *rest = refs[n_b + n_a :]
    weight_refs = rest[:groups]
    away_ref, own_ref, acc_b, acc_a, acc_tab, gain_acc = rest[groups:]
    step = pl.program_id(0)

    def body(inputs, acc, parts, pixel_ref, terms):
        x0_ref, dx1_ref, tab_ref = inputs[:3]
        gain = gain_ref[...]
        count = x0_ref.shape[0] // parts
        turned = []
        for part in range(parts):
            rows = slice(part * count, (part + 1) * count)
            hat, scale = normed(x0_ref[rows])
            d_h1 = 0.0
            for group, weight_ref in enumerate(weight_refs):
                term_refs = inputs[len(inputs) - (groups - group) * terms :][:terms]
                d_qkv = term_refs[0][rows]
                if terms > 1:
                    d_qkv = sum(ref[rows].astype(F32) for ref in term_refs).astype(BF)
                d_h1 = d_h1 + dot(d_qkv, weight_ref[...], NT)
            gain_acc[0:1] += jnp.sum(d_h1 * hat, 0, keepdims=True)
            d_x0 = dx1_ref[rows] + norm_back(d_h1, gain, hat, scale)
            turned.append(d_x0.astype(BF).T)
        turned = jnp.concatenate(turned, 1)
        acc_tab[...] += dot(turned, tab_ref[...], NN)
        acc[:, : pixel_ref.shape[1]] += dot(turned, pixel_ref[...], NN)

    @pl.when(step == 0)
    def _():
        for acc in (acc_b, acc_a, acc_tab, gain_acc):
            acc[...] = jnp.zeros_like(acc)
        gain_acc[1:2] = gain_grad_ref[...]
        body(inputs_a, acc_a, 1, inputs_a[3], parts_a)

    for piece in range(pieces):

        @pl.when((step > 0) & ((step - 1) % pieces == piece))
        def _(piece=piece):
            body(inputs_b, acc_b, parts_b, inputs_b[3 + piece], 1)

    @pl.when(step == steps)
    def _():
        place = lax.broadcasted_iota(jnp.int32, (8, 128), 1)
        row = lax.broadcasted_iota(jnp.int32, (8, 128), 0)
        spots = jnp.where((place == 126 + row) & (row < 2), 1.0, 0.0).astype(BF)
        acc_tab[...] += lax.dot_general(
            gain_acc[...].astype(BF), spots, ROWS_DIM, preferred_element_type=F32
        )
        at = 0
        for acc in (acc_b, acc_a, acc_tab):
            cols = slice(at, at + acc.shape[1])
            at += acc.shape[1]
            store_by_core(core_ref[0], acc, away_ref, own_ref, cols, blocks)


def embed_back(
    x0_b, dx1_b, tab_b, pixels_b, d_b, x0_a, dx1_a, tab_a, pixels_a, d_a, gain, gain_grad, w_all,
    core, blocks, images, depths, count_y
):
    rows, width = x0_b.shape
    pieces = len(pixels_b)
    steps = images * pieces
    block = rows // steps
    at = lambda i: jnp.maximum(i - 1, 0)
    moving = lambda array: pl.BlockSpec((block, array.shape[1]), lambda i: (at(i), 0))
    still = lambda shape: pl.BlockSpec(shape, lambda i: (0,) * len(shape))
    inputs_a = (x0_a, dx1_a, tab_a, pixels_a, *sum(d_a, ()))
    rows_a = x0_a.shape[0]
    grad = (count_y * blocks, width // (2 * count_y * blocks), sum(depths) + 128)
    return pl.pallas_call(
        partial(
            embed_back_kernel, steps=steps, groups=len(d_b), pieces=pieces, blocks=blocks,
            parts_b=max(1, block // 256), parts_a=len(d_a[0]),
        ),
        out_shape=(jax.ShapeDtypeStruct(grad, BF), jax.ShapeDtypeStruct(grad, BF)),
        grid=(steps + 1,),
        in_specs=[pl.BlockSpec(memory_space=pltpu.SMEM)]
        + [moving(x0_b), moving(dx1_b)]
        + [pl.BlockSpec((block, 128), lambda i: (at(i) % pieces, 0))]
        + [
            pl.BlockSpec((block, array.shape[1]), lambda i: (at(i) // pieces, 0))
            for array in pixels_b
        ]
        + [moving(array) for array in d_b]
        + [still((rows_a, array.shape[1])) for array in inputs_a]
        + [still((1, width)), still((1, width))]
        + [
            pl.BlockSpec((width, array.shape[1]), partial(lambda group, i: (0, group), group))
            for group, array in enumerate(d_b)
        ],
        out_specs=[still(grad), still(grad)],
        scratch_shapes=[pltpu.VMEM((width, depth), F32) for depth in (*depths, 128)]
        + [pltpu.VMEM((8, width), F32)],
        compiler_params=pltpu.CompilerParams(vmem_limit_bytes=VMEM_BYTES),
        cost_estimate=estimate(2 * rows * width * (3 * width + 640), rows * 10000),
        name="embed_back",
    )(core, x0_b, dx1_b, tab_b, *pixels_b, *d_b, *inputs_a, gain, gain_grad, *[w_all] * len(d_b))


def resize_back_kernel(got_ref, table_b_ref, table_a_ref, sums_ref, sent_ref, small_ref, *, rows, at):
    owners, _, lanes = sent_ref.shape
    total = jnp.zeros(small_ref.shape, F32)
    for block in range(got_ref.shape[0]):
        total = total + got_ref[block].astype(F32)
    small_ref[...] = total
    parts, square = [], 0.0
    for channel in range(3):
        part = 0.0
        for table_ref, first in ((table_b_ref, 0), (table_a_ref, at)):
            size = table_ref.shape[0]
            part = part + lax.dot_general(
                total[:, first + channel * size : first + (channel + 1) * size],
                table_ref[...],
                NN,
                precision=HIGH,
                preferred_element_type=F32,
            )
        square = square + jnp.sum(part * part)
        parts.append(part)
    width = BASE * BASE * 3 // owners
    kern = jnp.concatenate(parts + [jnp.zeros((rows, lanes), F32)], 1)
    lane = lax.broadcasted_iota(jnp.int32, (1, lanes), 1)
    last = total[:, total.shape[1] - lanes :]
    pos = jnp.where(lane < 49, last + pltpu.roll(last, lanes - 49, 1), 0.0)
    last = jnp.where(lane < 126, pos, last)
    small_ref[:, total.shape[1] - lanes :] = last
    square = square + jnp.sum(last * last) + jnp.sum(jnp.where(lane == 0, sums_ref[...], 0.0))
    beside = jnp.where(lane == width, square, 0.0)
    for index in (1, 2):
        beside = beside + jnp.where(lane == width + index, pltpu.roll(sums_ref[...], width, 1), 0.0)
    for owner in range(owners):
        sent_ref[owner] = jnp.where(
            lane < width, kern[:, owner * width : owner * width + lanes], beside
        )


def resize_back(got, tables, sums, rows, at, owners, lanes):
    cols = got.shape[2]
    return pl.pallas_call(
        partial(resize_back_kernel, rows=rows, at=at),
        out_shape=(
            jax.ShapeDtypeStruct((owners, rows, lanes), F32),
            jax.ShapeDtypeStruct((rows, cols), F32),
        ),
        in_specs=[pl.BlockSpec(memory_space=pltpu.VMEM)] * 4,
        out_specs=[pl.BlockSpec(memory_space=pltpu.VMEM)] * 2,
        compiler_params=pltpu.CompilerParams(vmem_limit_bytes=VMEM_BYTES),
        cost_estimate=estimate(1 << 28, 4 << 20),
        name="resize_back",
    )(got, *tables, sums)


def update_kernel(got_ref, small_ref, qkv_ref, out_ref, up_ref, down_ref, head_ref, count_ref, *refs, width):
    masters, firsts, seconds = refs[0:7], refs[7:14], refs[14:21]
    new, new_firsts, new_seconds = refs[21:28], refs[28:35], refs[35:42]
    norm_ref, stat_ref = refs[42:]
    owners, rows, lanes = got_ref.shape
    sums = got_ref[0, 0:1, :]
    for owner in range(1, owners):
        sums = sums + got_ref[owner, 0:1, :]
    lane = lax.broadcasted_iota(jnp.int32, (1, lanes), 1)
    norm = jnp.sqrt(jnp.sum(jnp.where(lane == width, sums, 0.0), 1, keepdims=True))
    factor = jnp.minimum(1.0, CLIP / (norm + 1e-06))
    sums = pltpu.roll(sums, lanes - width, 1)
    ratio = sums / jnp.maximum(count_ref[...], 1.0)
    norm_ref[...] = norm
    stat_ref[...] = ratio[:, 1:3]
    kern = jnp.concatenate([got_ref[owner] for owner in range(owners)], 0).T[:width]
    small = small_ref[:, small_ref.shape[1] - lanes :]
    grads = (
        (Ellipsis, qkv_ref[...]),
        (Ellipsis, out_ref[...]),
        (0, up_ref[...]),
        (1, down_ref[...]),
        (Ellipsis, kern),
        (Ellipsis, small[:, :49]),
        (Ellipsis, head_ref[...]),
        (Ellipsis, small[:, 126:128].T),
    )
    for index, (at, grad) in zip((0, 1, 2, 2, 3, 4, 5, 6), grads):
        new[index][at], new_firsts[index][at], new_seconds[index][at] = adamw(
            masters[index][at], firsts[index][at], seconds[index][at], grad * factor, RATES[index]
        )


def update(got, small, grads, count, masters, firsts, seconds, width):
    full = pl.BlockSpec(memory_space=pltpu.VMEM)
    shapes = [jax.ShapeDtypeStruct(array.shape, F32) for array in masters]
    inputs = (got, small, *grads, count, *masters, *firsts, *seconds)
    return pl.pallas_call(
        partial(update_kernel, width=width),
        out_shape=(
            *shapes * 3, jax.ShapeDtypeStruct((1, 1), F32), jax.ShapeDtypeStruct((1, 2), F32)
        ),
        in_specs=[full] * len(inputs),
        out_specs=[full] * 23,
        compiler_params=pltpu.CompilerParams(vmem_limit_bytes=VMEM_BYTES),
        cost_estimate=estimate(1 << 28, 16 << 20),
        name="update",
    )(*inputs)


def after(value, *others):
    return lax.optimization_barrier((value, *others))[0]


def padded_cols(array, width):
    return jnp.pad(array, ((0, 0), (0, width - array.shape[1])))


def round_up(count, unit):
    return -(-count // unit) * unit


def fast_step(
    pixels_a, pixels_b, labels_a, labels_b, live_a, live_b, masters, firsts, seconds
):
    qkv_w, out_w, mlp_w, kern_w, pos_w, head_w, gains = masters
    seq = lax.axis_size("y")
    row = lax.axis_index("y")
    count_all = seq * lax.axis_size("z") * lax.axis_size("x") * 2
    flat_index = lax.axis_index(AXES)
    lead = (row == 0).astype(F32)
    width = HEADS * HEAD_DIM
    hidden = mlp_w.shape[2]
    classes = head_w.shape[1]
    classes_up = round_up(classes, 1024)
    rows_own = qkv_w.shape[0]
    rows_kern = kern_w.shape[0]
    groups = 2
    span = width // groups
    pairs = span // 128

    images_a, rows_a, grid_a, depth_a = pixels_a.shape
    images_b, rows_b, grid_b, depth_b = pixels_b.shape
    own_b = images_b // seq
    parts_b, tabs_b, slices = [], [], []
    table_b = jnp.asarray(place_table(grid_b))
    table_a = jnp.asarray(place_table(grid_a))
    span_b, span_a = rows_b * grid_b, rows_a * grid_a
    for step in range(seq):
        part = lax.dynamic_slice_in_dim(
            pixels_b, ((row + step) % seq) * own_b, own_b, 0
        )
        part = part.reshape(own_b * rows_b * grid_b, depth_b)
        slices.append(part)
        parts_b.append(shift(part, "y", step) if step else part)
        tabs_b.append(lax.dynamic_slice_in_dim(table_b, ((row - step) % seq) * span_b, span_b, 0))
    tab_a = lax.dynamic_slice_in_dim(table_a, row * span_a, span_a, 0)
    whole_a, whole_b = grid_a * grid_a, grid_b * grid_b

    alive_a = live_a.astype(F32)[:, None]
    counts = jnp.stack([lead * jnp.sum(alive_a), lead * jnp.sum(live_b.astype(F32))]).astype(BF)
    lanes = round_up(rows_kern + 2, 128)
    sent = jnp.concatenate(
        [
            kern_w.astype(BF).T,
            jnp.broadcast_to(counts[None], (width, 2)),
            jnp.zeros((width, lanes - rows_kern - 2), BF),
        ],
        1,
    )
    sent = after(sent, *slices)
    got = lax.all_to_all(sent, AXES, split_axis=0, concat_axis=0, tiled=True)
    def group_cols(array, group):
        shaped = array.reshape(rows_own, 3, groups, pairs, 128)[:, :, group]
        return shaped.transpose(0, 2, 1, 3).reshape(rows_own, 3 * span)

    qkv_low = qkv_w.astype(BF)
    held = jnp.concatenate(stage(group_cols(qkv_low, 0)[None], STAGES[0]), 0)
    held = jnp.concatenate(stage(held, STAGES[1]), 0)
    packed = jnp.concatenate(
        [group_cols(qkv_low, group) for group in range(groups)]
        + [out_w.astype(BF), mlp_w[0].astype(BF)],
        1,
    )
    got, held, packed, tab_a, tab_b, *parts_b = lax.optimization_barrier(
        (got, held, packed, tab_a, jnp.concatenate(tabs_b, 0), *parts_b)
    )
    held = stage(held, STAGES[2])
    got = got.reshape(count_all, rows_own, lanes)
    counts = got[:, 0, rows_kern : rows_kern + 2]
    got = got.astype(F32)
    kern_cols = got[:, :, :rows_kern].transpose(1, 0, 2).reshape(rows_own, 3, BASE * BASE)

    w_all = lax.all_gather(packed, AXES, axis=0, tiled=True)

    tables = [resize_table(PATCH_B), resize_table(PATCH_A)]
    sizes = [3 * table.shape[0] for table in tables]
    resized = [
        jnp.einsum("dck,pk->dcp", kern_cols, jnp.asarray(table), precision=HIGH).reshape(
            rows_own, -1
        )
        for table in tables
    ]
    depths = [round_up(size, 128) for size in sizes]
    spot = sum(depths)
    pos_t = pos_w.astype(BF).T
    edge = jnp.zeros((rows_own, 28), BF)
    small = jnp.concatenate(
        [padded_cols(piece.astype(BF), depth) for piece, depth in zip(resized, depths)]
        + [pos_t, pos_t, edge, gains.astype(BF).T],
        1,
    )
    w_small, held = gather_rows(small, held)
    held = jnp.concatenate(held, 0)
    w_down_head = lax.all_gather(
        after(
            jnp.concatenate([mlp_w[1].astype(BF), padded_cols(head_w.astype(BF), classes_up)], 1),
            w_small,
        ),
        AXES, axis=0, tiled=True,
    )

    gain_rows = w_small[:, spot + 126 :].T.astype(F32)
    gain1, gain2 = gain_rows[0:1], gain_rows[1:2]
    flat_a = pixels_a.reshape(span_a, depth_a)
    block = min(512, whole_b)
    x0_a, h1_a = embed([flat_a], tab_a, w_small, depths[0], spot, gain1, 1)
    h1_a, *held = lax.optimization_barrier((h1_a, *stage(held, STAGES[3])))
    w_first = place_blocks(held, stage_owners())
    h1_all = jnp.concatenate([h1_a] + [shift(h1_a, "y", step) for step in range(1, seq)], 0)
    x0_b, h1_b = embed(
        [after(parts_b[0], h1_a), *parts_b[1:]], tab_b, w_small, 0, spot, gain1, own_b
    )
    h1_b, h1_all = lax.optimization_barrier((h1_b, h1_all))
    outs_a, outs_b = [], []
    ready = h1_b
    for group in range(groups):
        outs_b.append(
            attend_pairs(
                after(h1_b, ready), *((w_all, group * pairs) if group else (w_first, 0)),
                pairs, own_b, whole_b,
            )
        )
        ready = outs_b[-1][0]
    for group in range(groups):
        outs_a.append(attend_pairs(after(h1_all, ready), w_all, group * pairs, pairs, 1, span_a))
    qkvs_a, qkvs_b = [out[0] for out in outs_a], [out[0] for out in outs_b]
    mixed_a, mixed_b = [out[1] for out in outs_a], [out[1] for out in outs_b]

    x1_a, slope_a, xsum_a, asum_a = mlp(x0_a, mixed_a, w_all, hidden, gain2, 1, span_a)
    sums_a = jnp.concatenate([xsum_a[0], asum_a[0]], 1)
    sums_a = sum([shift(sums_a, "y", step) for step in range(1, seq)], sums_a)
    x1_b, slope_b, xsum_b, asum_b = mlp(after(x0_b, x1_a), mixed_b, w_all, hidden, gain2, own_b, block)

    images = jnp.concatenate([labels_b, live_b, labels_a, live_a, row.reshape(1).astype(jnp.int32)])
    images, counts, h1_b = lax.optimization_barrier((images, counts, h1_b))
    count = jnp.sum(counts.astype(F32), 0, keepdims=True)
    total = jnp.maximum(jnp.sum(count), 1.0)
    rows_up = round_up(own_b + 1, 8)
    whole = np.ones((rows_up, 1), np.float32)
    whole[:own_b], whole[own_b] = whole_b, whole_a
    loss_sums, rows_out, d_x2, d_act = head_step(
        images, xsum_b, asum_b, sums_a, w_down_head, jnp.asarray(whole), total.reshape(1, 1), classes
    )

    image_rows = lax.all_gather(rows_out, AXES, axis=0, tiled=True)

    d_x1_b, d0_b, d1_b, d_x1_a, d0_a, d1_a, grad_up_out, grad_gain2 = mlp_back(
        (slope_b, d_act, x1_b, d_x2, *mixed_b),
        (slope_a, d_act, x1_a, d_x2, *mixed_a),
        w_all, gain2, own_b, block,
    )
    d_mixed_a, d_mixed_b = (d0_a, d1_a), (d0_b, d1_b)

    d_alls, d_groups_a = [], []
    for group in range(groups):
        d_all = attend_back_apart(
            qkvs_a[group], qkvs_a[group], d_mixed_a[group], mixed_a[group],
            outs_a[group][2], pairs, span_a, seq * span_a,
        )
        d_alls.append(d_all)
        d_groups_a += [
            shift(d_all[step * span_a : (step + 1) * span_a], "y", seq - step)
            for step in range(1, seq)
        ]
    own_up_out = lax.psum_scatter(
        after(grad_up_out, image_rows, *d_alls), AXES, scatter_dimension=0, tiled=True
    ).astype(F32)
    core = lax.axis_index("core").reshape(1).astype(jnp.int32)
    blocks = lax.axis_size("z") * lax.axis_size("x")
    d_groups_b, own_groups = [], []
    ready = d_alls[-1]
    for group in range(groups):
        got, away, own = attend_back_grad(
            qkvs_b[group],
            after(d_mixed_b[group], ready),
            mixed_b[group], outs_b[group][2],
            h1_b, h1_all, d_alls[group], core, pairs, own_b, whole_b, blocks, seq,
        )
        if group:
            away, own, own_groups[-1] = lax.optimization_barrier((away, own, own_groups[-1]))
        else:
            away, own, *d_groups_a = lax.optimization_barrier((away, own, *d_groups_a))
        d_groups_b.append(got)
        own_groups.append(scatter_rows(away, own))
        ready = got
    moved = seq - 1
    d_groups_a = [
        (d_all, *d_groups_a[group * moved : (group + 1) * moved])
        for group, d_all in enumerate(d_alls)
    ]
    away, own = embed_back(
        x0_b, after(d_x1_b, ready), tab_b, parts_b, d_groups_b,
        x0_a, d_x1_a, tab_a, flat_a, d_groups_a,
        gain1, grad_gain2, w_all, core, blocks, own_b, depths, seq,
    )
    away, own, own_up_out, *own_groups = lax.optimization_barrier(
        (away, own, own_up_out, *own_groups)
    )
    own_qkv = jnp.stack([block_sum(got) for got in own_groups], 1)
    own_qkv = own_qkv.reshape(rows_own, groups * pairs, 3, 128)
    own_qkv = own_qkv.transpose(0, 2, 1, 3).reshape(rows_own, 3 * width)
    small_parts = scatter_rows(away, own)

    columns = lambda lo: lax.dynamic_slice_in_dim(
        image_rows[:, lo : lo + width], flat_index * rows_own, rows_own, 1
    )
    own_down = lax.dot_general(
        columns(hidden + width), image_rows[:, :hidden], ROWS_DIM, preferred_element_type=F32
    )
    own_head = lax.dot_general(
        columns(hidden),
        image_rows[:, hidden + 2 * width : hidden + 2 * width + classes],
        ROWS_DIM,
        preferred_element_type=F32,
    )
    own_up, own_out = own_up_out[:, :hidden], own_up_out[:, hidden:]
    square_sum = sum(
        jnp.sum(piece * piece) for piece in (own_up_out, own_down, own_head, own_qkv)
    )
    sums = loss_sums + padded_cols(square_sum.reshape(1, 1), lanes)
    sent, own_small = resize_back(
        small_parts, [jnp.asarray(table) for table in tables], sums, rows_own, depths[0],
        count_all, lanes,
    )
    got = lax.all_to_all(sent, AXES, split_axis=0, concat_axis=0, tiled=True)
    counts = padded_cols(jnp.pad(count, ((0, 0), (1, 0))), lanes)
    turn = lambda arrays: [array.T if at == 4 else array for at, array in enumerate(arrays)]
    *done, grad_norm, size_stats = update(
        got, own_small, (own_qkv, own_out, own_up, own_down, own_head), counts,
        turn(masters), turn(firsts), turn(seconds), rows_kern,
    )
    done = [item for at in (0, 7, 14) for item in turn(done[at : at + 7])]
    return (*done, size_stats.reshape(2), grad_norm.reshape(()))


def fits_fast(mesh, pixels_a, pixels_b):
    dp, seq = mesh.shape["dp"], mesh.shape["seq"]
    images_b, rows_b, grid_b, _ = pixels_b.shape
    rows_a, grid_a = pixels_a.shape[1:3]
    return (
        dp % 8 == 0
        and rows_b % seq == 0
        and rows_a % seq == 0
        and images_b % (dp * seq) == 0
        and images_b // dp <= 256
        and pixels_a.shape[0] == dp
        and grid_b * grid_b % 256 == 0
        and rows_a // seq * grid_a % 32 == 0
    )


def fast_on_device(*args):
    return fast_step(*args[:6], args[6:13], args[13:20], args[20:27])


def on_device(
    pixels_a,
    pixels_b,
    labels_a,
    labels_b,
    live_a,
    live_b,
    qkv_w,
    out_w,
    mlp_w,
    kern_w,
    pos_w,
    head_w,
    gains,
    qkv_m,
    out_m,
    mlp_m,
    kern_m,
    pos_m,
    head_m,
    gains_m,
    qkv_v,
    out_v,
    mlp_v,
    kern_v,
    pos_v,
    head_v,
    gains_v,
):
    masters = (qkv_w, out_w, mlp_w, kern_w, pos_w, head_w, gains)
    firsts = (qkv_m, out_m, mlp_m, kern_m, pos_m, head_m, gains_m)
    seconds = (qkv_v, out_v, mlp_v, kern_v, pos_v, head_v, gains_v)
    bf16 = jnp.bfloat16
    w_qkv, w_out, w_mlp, w_kern, w_pos, w_head, w_gain = (
        lax.all_gather(qkv_w.astype(bf16), ("dp", "seq"), axis=0, tiled=True),
        lax.all_gather(out_w.astype(bf16), ("dp", "seq"), axis=0, tiled=True),
        lax.all_gather(mlp_w.astype(bf16), ("dp", "seq"), axis=1, tiled=True),
        lax.all_gather(kern_w.astype(bf16), ("dp", "seq"), axis=0, tiled=True),
        lax.all_gather(pos_w.astype(bf16), ("dp", "seq"), axis=1, tiled=True),
        lax.all_gather(head_w.astype(bf16), ("dp", "seq"), axis=0, tiled=True),
        lax.all_gather(gains.astype(bf16), ("dp", "seq"), axis=1, tiled=True),
    )
    seq_count = lax.axis_size("seq")
    seq_place = lax.axis_index("seq")
    gain_full = w_gain.astype(jnp.float32)
    kern_full = w_kern.astype(jnp.float32)
    pos_full = w_pos.astype(jnp.float32)
    size_sets = ((pixels_a, labels_a, live_a, PATCH_A), (pixels_b, labels_b, live_b, PATCH_B))
    embeds, flats, kern_backs, pos_backs, layouts = ([], [], [], [], [])
    start = 0
    for pixels, labels, live, patch in size_sets:
        images, rows, grid, depth = pixels.shape
        flat = pixels.reshape(images * rows * grid, depth)
        resized, kern_back = jax.vjp(partial(kernel_resize, patch=patch), kern_full)
        row_table = lax.dynamic_slice_in_dim(interp_matrix(grid, 7), seq_place * rows, rows, 0)
        place, pos_back = jax.vjp(partial(grid_resize, row_table=row_table, grid=grid), pos_full)
        embed = jnp.dot(flat, resized.astype(bf16), preferred_element_type=jnp.float32)
        embed = embed.reshape(images, rows * grid, -1) + place.reshape(1, rows * grid, -1)
        embeds.append(embed.reshape(images * rows * grid, -1))
        flats.append(flat)
        kern_backs.append(kern_back)
        pos_backs.append(pos_back)
        layouts.append((start, start + images * rows * grid, images, rows * grid, grid * grid))
        start = start + images * rows * grid
    x0 = jnp.concatenate(embeds, 0)
    h1_full, norm1_back = jax.vjp(layer_norm, x0, gain_full[0])
    h1 = h1_full.astype(bf16)
    qkv = jnp.dot(h1, w_qkv, preferred_element_type=jnp.float32).astype(bf16)
    width = qkv.shape[1] // 3
    local_kv = qkv[:, width:]
    blocks = [local_kv]
    moving = local_kv
    for turn in range(1, seq_count):
        moving = from_behind(moving, "seq", 1)
        blocks.append(moving)
    all_kv = jnp.stack(blocks, 0)
    mixed_parts, saved = ([], [])
    for first_row, last_row, images, length, whole in layouts:
        query = qkv[first_row:last_row, :width].reshape(images, length, HEADS, HEAD_DIM)
        remote = all_kv[:, first_row:last_row].reshape(
            seq_count, images, length, 2, HEADS, HEAD_DIM
        )
        remote = remote.transpose(1, 0, 2, 3, 4, 5).reshape(
            images, seq_count * length, 2, HEADS, HEAD_DIM
        )
        keys, values = (remote[:, :, 0], remote[:, :, 1])
        attended, norm_log = attend(query, keys, values)
        mixed_parts.append(attended.reshape(last_row - first_row, width))
        saved.append((query, keys, values, norm_log))
    mixed = jnp.concatenate(mixed_parts, 0).astype(bf16)
    x1 = x0 + jnp.dot(mixed, w_out, preferred_element_type=jnp.float32)
    h2_full, norm2_back = jax.vjp(layer_norm, x1, gain_full[1])
    h2 = h2_full.astype(bf16)
    inner = jnp.dot(h2, w_mlp[0], preferred_element_type=jnp.float32)
    act_full, gelu_back = jax.vjp(partial(jax.nn.gelu, approximate=False), inner)
    act = act_full.astype(bf16)
    x2 = x1 + lax.dot_general(act, w_mlp[1], COLS_DIM, preferred_element_type=jnp.float32)
    sum_a = x2[layouts[0][0] : layouts[0][1]].reshape(layouts[0][2], layouts[0][3], -1).sum(1)
    sum_b = x2[layouts[1][0] : layouts[1][1]].reshape(layouts[1][2], layouts[1][3], -1).sum(1)
    pooled_sums = lax.psum((sum_a, sum_b), "seq")
    stats, head_parts = ([], [])
    for index in range(2):
        labels, live = (size_sets[index][1], size_sets[index][2])
        pooled_low = (pooled_sums[index] / float(layouts[index][4])).astype(bf16)
        logits = jnp.dot(pooled_low, w_head, preferred_element_type=jnp.float32)
        norm_log = jax.nn.logsumexp(logits, -1)
        hot = (labels[:, None] == jnp.arange(logits.shape[1], dtype=jnp.int32)[None, :]).astype(
            jnp.float32
        )
        true_logit = jnp.sum(hot * logits, -1)
        alive = live.astype(jnp.float32)
        stats.append(jnp.stack([jnp.sum(alive * (norm_log - true_logit)), jnp.sum(alive)]))
        head_parts.append((pooled_low, jnp.exp(logits - norm_log[:, None]) - hot, alive))
    stats_a, stats_b = lax.psum((stats[0], stats[1]), "dp")
    total = jnp.maximum(stats_a[1] + stats_b[1], 1.0)
    grad_head = jnp.zeros(w_head.shape, jnp.float32)
    d_x2_parts = []
    for index in range(2):
        pooled_low, soft_minus, alive = head_parts[index]
        d_logits = (soft_minus * alive[:, None] / total).astype(bf16)
        grad_head = grad_head + lax.dot_general(
            pooled_low, d_logits, ROWS_DIM, preferred_element_type=jnp.float32
        )
        d_pooled = lax.dot_general(d_logits, w_head, COLS_DIM, preferred_element_type=jnp.float32)
        images, length, whole = (layouts[index][2], layouts[index][3], layouts[index][4])
        spread = jnp.broadcast_to(
            (d_pooled / float(whole))[:, None, :], (images, length, d_pooled.shape[1])
        )
        d_x2_parts.append(spread.reshape(images * length, -1))
    d_x2 = jnp.concatenate(d_x2_parts, 0)
    d_mix = d_x2.astype(bf16)
    grad_down = lax.dot_general(d_mix, act, ROWS_DIM, preferred_element_type=jnp.float32)
    d_act = jnp.dot(d_mix, w_mlp[1], preferred_element_type=jnp.float32)
    d_inner = gelu_back(d_act)[0].astype(bf16)
    grad_up = lax.dot_general(h2, d_inner, ROWS_DIM, preferred_element_type=jnp.float32)
    d_h2 = lax.dot_general(d_inner, w_mlp[0], COLS_DIM, preferred_element_type=jnp.float32)
    d_x1_norm, grad_gain2 = norm2_back(d_h2)
    d_x1 = d_x2 + d_x1_norm
    d_attn = d_x1.astype(bf16)
    grad_out = lax.dot_general(mixed, d_attn, ROWS_DIM, preferred_element_type=jnp.float32)
    d_mixed = lax.dot_general(d_attn, w_out, COLS_DIM, preferred_element_type=jnp.float32).astype(
        bf16
    )
    d_query_parts, d_kv_parts = ([], [])
    for index in range(2):
        first_row, last_row, images, length, whole = layouts[index]
        query, keys, values, norm_log = saved[index]
        d_out = d_mixed[first_row:last_row].reshape(images, length, HEADS, HEAD_DIM)
        d_query, d_keys, d_values = attend_back(query, keys, values, norm_log, d_out)
        d_query_parts.append(d_query.reshape(last_row - first_row, width))
        paired = jnp.stack([d_keys, d_values], 2).reshape(images, seq_count, length, 2 * width)
        d_kv_parts.append(
            paired.transpose(1, 0, 2, 3).reshape(seq_count, last_row - first_row, 2 * width)
        )
    d_all = jnp.concatenate(d_kv_parts, 1)
    mine_kv = d_all[1 % seq_count]
    for turn in range(1, seq_count):
        mine_kv = (
            from_behind(mine_kv.astype(jnp.bfloat16), "seq", 1).astype(mine_kv.dtype)
            + d_all[(turn + 1) % seq_count]
        )
    d_qkv = jnp.concatenate([jnp.concatenate(d_query_parts, 0), mine_kv], 1).astype(bf16)
    grad_qkv = lax.dot_general(h1, d_qkv, ROWS_DIM, preferred_element_type=jnp.float32)
    d_h1 = lax.dot_general(d_qkv, w_qkv, COLS_DIM, preferred_element_type=jnp.float32)
    d_x0_norm, grad_gain1 = norm1_back(d_h1)
    d_x0 = d_x1 + d_x0_norm
    grad_kern = jnp.zeros(kern_full.shape, jnp.float32)
    grad_pos = jnp.zeros(pos_full.shape, jnp.float32)
    for index in range(2):
        first_row, last_row, images, length, whole = layouts[index]
        d_rows = d_x0[first_row:last_row]
        d_kernel = lax.dot_general(
            flats[index], d_rows.astype(bf16), ROWS_DIM, preferred_element_type=jnp.float32
        )
        grad_kern = grad_kern + kern_backs[index](d_kernel)[0]
        d_place = d_rows.reshape(images, length, -1).sum(0)
        grad_pos = grad_pos + pos_backs[index](d_place.reshape(grid_shape(size_sets, index)))[0]
    grad_mlp = jnp.stack([grad_up, grad_down], 0)
    grad_gain = jnp.stack([grad_gain1, grad_gain2], 0)
    grad_head = grad_head / float(seq_count)
    owned = (
        lax.psum_scatter(grad_qkv, ("dp", "seq"), scatter_dimension=0, tiled=True),
        lax.psum_scatter(grad_out, ("dp", "seq"), scatter_dimension=0, tiled=True),
        lax.psum_scatter(grad_mlp, ("dp", "seq"), scatter_dimension=1, tiled=True),
        lax.psum_scatter(grad_kern, ("dp", "seq"), scatter_dimension=0, tiled=True),
        lax.psum_scatter(grad_pos, ("dp", "seq"), scatter_dimension=1, tiled=True),
        lax.psum_scatter(grad_head, ("dp", "seq"), scatter_dimension=0, tiled=True),
        lax.psum_scatter(grad_gain, ("dp", "seq"), scatter_dimension=1, tiled=True),
    )
    square_sum = sum((jnp.sum(piece * piece) for piece in owned))
    grad_norm = jnp.sqrt(lax.psum(square_sum, ("dp", "seq")))
    factor = jnp.minimum(1.0, CLIP / (grad_norm + 1e-06))
    done = [adamw(masters[i], firsts[i], seconds[i], owned[i] * factor, RATES[i]) for i in range(7)]
    size_stats = jnp.stack(
        [stats_a[0] / jnp.maximum(stats_a[1], 1.0), stats_b[0] / jnp.maximum(stats_b[1], 1.0)]
    )
    return (
        done[0][0],
        done[1][0],
        done[2][0],
        done[3][0],
        done[4][0],
        done[5][0],
        done[6][0],
        done[0][1],
        done[1][1],
        done[2][1],
        done[3][1],
        done[4][1],
        done[5][1],
        done[6][1],
        done[0][2],
        done[1][2],
        done[2][2],
        done[3][2],
        done[4][2],
        done[5][2],
        done[6][2],
        size_stats,
        grad_norm,
    )


def specs(row, col):
    both = (*row, *col)
    owned = (
        P(both, None), P(both, None), P(None, both, None), P(both, None), P(None, both),
        P(both, None), P(None, both),
    )
    images = P(row, col, None, None)
    return (images, images, P(row), P(row), P(row), P(row), *owned * 3), (*owned * 3, P(), P())


def solution(mesh):
    dp, seq = mesh.shape["dp"], mesh.shape["seq"]

    def run(*args):
        if fits_fast(mesh, args[0], args[1]):
            split = Mesh(mesh.devices.reshape(4, dp // 8, 2, seq), AXES)
            placed, given = specs(AXES[:3], AXES[3:])
            step = jax.shard_map(
                fast_on_device, mesh=split, in_specs=placed, out_specs=given, check_vma=False
            )
        else:
            placed, given = specs(("dp",), ("seq",))
            step = jax.shard_map(
                on_device, mesh=mesh, in_specs=placed, out_specs=given, check_vma=False
            )
        return step(*args)

    return run
```

```python
import math
from functools import partial

import jax
import jax.numpy as jnp
import ml_dtypes
import numpy as np
from jax import lax
from jax.experimental import pallas as pl
from jax.experimental.pallas import tpu as pltpu
from jax.sharding import Mesh
from jax.sharding import PartitionSpec as P

HEADS = 12
HEAD_DIM = 64
BASE = 32
PATCH_A = 10
PATCH_B = 12


HIGH = lax.Precision.HIGHEST
RATES = (0.012, 0.2, 0.012, 0.03, 0.15, 0.06, 0.25)
CLIP = 0.001
ROWS_DIM = (((0,), (0,)), ((), ()))
COLS_DIM = (((1,), (1,)), ((), ()))


def from_behind(value, axis, steps):
    count = lax.axis_size(axis)
    pairs = [(source, (source + steps) % count) for source in range(count)]
    return lax.ppermute(value, axis, pairs)


def interp_matrix(n_out, n_in):
    places = jnp.arange(n_out, dtype=jnp.float32) * ((n_in - 1) / (n_out - 1))
    return jnp.maximum(
        0.0, 1.0 - jnp.abs(places[:, None] - jnp.arange(n_in, dtype=jnp.float32)[None, :])
    )


def pinv_table(patch):
    basis = interp_matrix(patch, BASE)
    gram = jnp.dot(basis, basis.T, precision=HIGH)
    factor = jnp.linalg.cholesky(gram)
    return jax.scipy.linalg.cho_solve((factor, True), basis)


def layer_norm(values, gain):
    centred = values - jnp.mean(values, -1, keepdims=True)
    spread = jnp.mean(centred * centred, -1, keepdims=True)
    return centred * lax.rsqrt(spread + 1e-06) * gain


def kernel_resize(kernel, patch):
    table = pinv_table(patch)
    shaped = kernel.reshape(3, BASE, BASE, -1)
    return jnp.einsum("ia,jb,cabd->cijd", table, table, shaped, precision=HIGH).reshape(
        3 * patch * patch, -1
    )


def grid_resize(position, row_table, grid):
    table = interp_matrix(grid, 7)
    return jnp.einsum(
        "ia,jb,abd->ijd", row_table, table, position.reshape(7, 7, -1), precision=HIGH
    )


def adamw(weight, first, second, grad, rate):
    first = 0.9 * first + 0.1 * grad
    second = 0.999 * second + 0.001 * grad * grad
    step_dir = first / (1.0 - 0.9**3) / (jnp.sqrt(second / (1.0 - 0.999**3)) + 1e-08)
    return (weight - rate * (step_dir + 0.1 * weight), first, second)


def attend(query, keys, values):
    scores = jnp.einsum(
        "ithe,ishe->ihts", query, keys, preferred_element_type=jnp.float32
    ) * HEAD_DIM ** (-0.5)
    norm_log = jax.nn.logsumexp(scores, -1, keepdims=True)
    probs = jnp.exp(scores - norm_log).astype(jnp.bfloat16)
    return (
        jnp.einsum("ihts,ishe->ithe", probs, values, preferred_element_type=jnp.float32),
        norm_log,
    )


def attend_back(query, keys, values, norm_log, d_out):
    scale = HEAD_DIM ** (-0.5)
    scores = jnp.einsum("ithe,ishe->ihts", query, keys, preferred_element_type=jnp.float32) * scale
    probs = jnp.exp(scores - norm_log)
    d_probs = jnp.einsum("ithe,ishe->ihts", d_out, values, preferred_element_type=jnp.float32)
    d_scores = (probs * (d_probs - jnp.sum(probs * d_probs, -1, keepdims=True))).astype(
        jnp.bfloat16
    )
    d_query = (
        jnp.einsum("ihts,ishe->ithe", d_scores, keys, preferred_element_type=jnp.float32) * scale
    )
    d_keys = (
        jnp.einsum("ihts,ithe->ishe", d_scores, query, preferred_element_type=jnp.float32) * scale
    )
    d_values = jnp.einsum(
        "ihts,ithe->ishe", probs.astype(jnp.bfloat16), d_out, preferred_element_type=jnp.float32
    )
    return (d_query, d_keys, d_values)


def grid_shape(size_sets, index):
    pixels = size_sets[index][0]
    return (pixels.shape[1], pixels.shape[2], -1)


AXES = ("z", "x", "core", "y")
CHIPS = ("z", "x", "y")
NT = (((1,), (1,)), ((), ()))
NN = (((1,), (0,)), ((), ()))
BF = jnp.bfloat16
F32 = jnp.float32
VMEM_BYTES = 58 << 20
QUERY_SCALE = HEAD_DIM**-0.5 * math.log2(math.e)


def shift(value, axis, steps):
    count = lax.axis_size(axis)
    pairs = [(source, (source + steps) % count) for source in range(count)]
    return lax.ppermute(value, axis, pairs)


def chip_sizes():
    return tuple(lax.axis_size(axis) for axis in CHIPS)


def gather_rows(value, beside):
    rows, cols = value.shape
    z, x, y = chip_sizes()
    chips = z * x * y
    copies = jnp.broadcast_to(value[None], (chips, rows, cols)).reshape(chips * rows, cols)
    mine = lax.all_to_all(copies, CHIPS, split_axis=0, concat_axis=0, tiled=True)
    mine, *beside = lax.optimization_barrier((mine, *beside))
    other = shift(mine, "core", 1)
    parts = [part.reshape(z, x, 1, y, rows, cols) for part in (mine, other)]
    first = lax.axis_index("core") == 0
    both = jnp.concatenate(
        [jnp.where(first, parts[0], parts[1]), jnp.where(first, parts[1], parts[0])], 2
    )
    return both.reshape(2 * chips * rows, cols), beside


STAGES = (*CHIPS, "core")


def stage(held, axis):
    return [held] + [shift(held, axis, step) for step in range(1, lax.axis_size(axis))]


def stage_owners():
    strides, stride = {}, 1
    for axis in reversed(AXES):
        strides[axis] = stride
        stride = stride * lax.axis_size(axis)
    shifts = [{}]
    for axis in STAGES:
        shifts = [{**known, axis: step} for step in range(lax.axis_size(axis)) for known in shifts]
    owner = jnp.zeros((stride,), jnp.int32)
    for axis in AXES:
        steps = np.array([known[axis] for known in shifts], np.int32)
        owner = owner + ((lax.axis_index(axis) - steps) % lax.axis_size(axis)) * strides[axis]
    return owner


def place_blocks_kernel(owner_ref, *refs):
    *pieces, out_ref, sems = refs
    copies = []
    for piece in pieces:
        for index in range(piece.shape[0]):
            block = len(copies)
            copies.append(
                pltpu.make_async_copy(
                    piece.at[index], out_ref.at[owner_ref[block]], sems.at[block]
                )
            )
    for copy in copies:
        copy.start()
    for copy in copies:
        copy.wait()


def place_blocks(pieces, owner):
    count = owner.shape[0]
    _, rows, cols = pieces[0].shape
    out = pl.pallas_call(
        place_blocks_kernel,
        out_shape=jax.ShapeDtypeStruct((count, rows, cols), BF),
        in_specs=[pl.BlockSpec(memory_space=pltpu.SMEM)]
        + [pl.BlockSpec(memory_space=pl.ANY)] * len(pieces),
        out_specs=pl.BlockSpec(memory_space=pltpu.VMEM),
        scratch_shapes=[pltpu.SemaphoreType.DMA((count,))],
        compiler_params=pltpu.CompilerParams(vmem_limit_bytes=VMEM_BYTES),
        cost_estimate=estimate(0, count * rows * cols * 4, 1),
        name="place_blocks",
    )(owner, *pieces)
    return out.reshape(count * rows, cols)


def scatter_rows(away, own):
    both = (own.astype(F32) + shift(away, "core", 1).astype(F32)).astype(BF)
    return lax.all_to_all(both, CHIPS, split_axis=0, concat_axis=0, tiled=True)


def block_sum(got):
    return jnp.sum(got.astype(F32), 0)


def store_by_core(core, acc, away_ref, own_ref, cols, count):
    blocks, rows, _ = own_ref.shape
    per = blocks // count
    for pair in range(count):
        for side, ref in ((core, own_ref), (1 - core, away_ref)):
            for block in range(per):
                first = pl.multiple_of(((2 * pair + side) * per + block) * rows, rows)
                ref[pair * per + block, :, cols] = acc[pl.ds(first, rows), :].astype(BF)


def interp_table(n_out, n_in):
    places = np.arange(n_out) * ((n_in - 1) / (n_out - 1))
    return np.maximum(0.0, 1.0 - np.abs(places[:, None] - np.arange(n_in)[None, :]))


def resize_table(patch):
    basis = interp_table(patch, BASE)
    table = np.linalg.solve(basis @ basis.T, basis)
    return np.kron(table, table).astype(np.float32)


def place_table(grid):
    table = interp_table(grid, 7)
    full = np.kron(table, table).astype(np.float32)
    high = full.astype(ml_dtypes.bfloat16)
    low = (full - high.astype(np.float32)).astype(ml_dtypes.bfloat16)
    return np.concatenate([high, low, np.zeros((grid * grid, 30), ml_dtypes.bfloat16)], 1)


def dot(left, right, dims):
    return lax.dot_general(left, right, dims, preferred_element_type=F32)


def estimate(flops, nbytes, share=32):
    return pl.CostEstimate(
        flops=int(flops) // share, bytes_accessed=int(nbytes) // share, transcendentals=0
    )


def normed(values):
    centred = values - jnp.mean(values, -1, keepdims=True)
    scale = lax.rsqrt(jnp.mean(centred * centred, -1, keepdims=True) + 1e-06)
    return centred * scale, scale


def norm_back(d_out, gain, hat, scale):
    d_hat = d_out * gain
    return scale * (
        d_hat
        - jnp.mean(d_hat, -1, keepdims=True)
        - hat * jnp.mean(d_hat * hat, -1, keepdims=True)
    )


def embed_kernel(*refs, pieces, at, depth, spot):
    pixel_refs, (tab_ref, weight_ref, gain_ref, *rest) = refs[:pieces], refs[pieces:]
    x0_ref, h1_ref = rest
    shares = 2 if tab_ref.shape[0] % 512 == 0 else 1
    count = tab_ref.shape[0] // shares

    def body(pixel_ref):
        for share in range(shares):
            rows = slice(share * count, (share + 1) * count)
            x0 = dot(tab_ref[rows], weight_ref[:, spot : spot + tab_ref.shape[1]], NT)
            x0 = x0 + dot(pixel_ref[rows], weight_ref[:, at : at + depth], NT)
            x0_ref[rows] = x0
            h1_ref[rows] = (normed(x0)[0] * gain_ref[...]).astype(BF)

    for piece, pixel_ref in enumerate(pixel_refs):
        pl.when(pl.program_id(1) == piece)(partial(body, pixel_ref))


def embed(pieces, tab, weight, at, spot, gain, images):
    count, depth = len(pieces), pieces[0].shape[1]
    block = tab.shape[0] // count
    rows, width = images * tab.shape[0], weight.shape[0]
    still = lambda array: pl.BlockSpec(array.shape, lambda i, j: (0, 0))
    moving = lambda cols: pl.BlockSpec((block, cols), lambda i, j: (i * count + j, 0))
    outs = [(width, F32), (width, BF)]
    return pl.pallas_call(
        partial(embed_kernel, pieces=count, at=at, depth=depth, spot=spot),
        out_shape=tuple(jax.ShapeDtypeStruct((rows, cols), kind) for cols, kind in outs),
        grid=(images, count),
        in_specs=[pl.BlockSpec((block, depth), lambda i, j: (i, 0))] * count
        + [pl.BlockSpec((block, tab.shape[1]), lambda i, j: (j, 0)), still(weight), still(gain)],
        out_specs=[moving(cols) for cols, _ in outs],
        compiler_params=pltpu.CompilerParams(vmem_limit_bytes=VMEM_BYTES),
        cost_estimate=estimate(2 * rows * width * width, rows * width * 8, 1),
        name="embed",
    )(*pieces, tab, weight, gain)


def head_split(first, values):
    zero = jnp.zeros((), values.dtype)
    return jnp.where(first, values, zero), jnp.where(first, zero, values)


def attend_pair(rows_ref, n_query, out_ref, log_ref, between=None):
    lane = lax.broadcasted_iota(jnp.int32, (1, 128), 1)
    first = lane < HEAD_DIM
    one = jnp.ones((), BF)
    values = rows_ref[:, 256:]
    keys = head_split(first, rows_ref[:, 128:256])
    sided = (jnp.where(first, values, one).T, jnp.where(first, one, values).T)
    query = rows_ref[:n_query, :128]
    scores = [dot(keys[head], query, NT) for head in range(2)]
    if between is not None:
        between()
    tops, probs, mixed = [], [], []
    for head in range(2):
        tops.append(jnp.max(scores[head], 0, keepdims=True))
        probs.append(jnp.exp2(scores[head] - tops[head]).astype(BF))
        mixed.append(dot(sided[head], probs[head], NN))
    outs = []
    for head in range(2):
        at = HEAD_DIM * (1 - head)
        total = mixed[head][at : at + 1]
        own = HEAD_DIM * head
        outs.append(mixed[head][own : own + HEAD_DIM] / total)
        log_ref[0, 0, head : head + 1, :] = tops[head] + jnp.log2(total)
    out_ref[...] = jnp.concatenate(outs, 0).T.astype(BF)


def attend_kernel(h1_ref, weight_ref, qkv_ref, out_ref, log_ref, held, *, items, n_query):
    step = pl.program_id(0)

    def project():
        lane = lax.broadcasted_iota(jnp.int32, (1, 384), 1)
        scale = jnp.where(lane < 128, QUERY_SCALE, 1.0)
        rows = (dot(h1_ref[...], weight_ref[...], NN) * scale).astype(BF)
        qkv_ref[...] = rows
        held[step % 2] = rows

    def attend(between=None):
        attend_pair(held.at[(step + 1) % 2], n_query, out_ref, log_ref, between)

    @pl.when(step == 0)
    def _():
        project()

    @pl.when((step > 0) & (step < items))
    def _():
        attend(project)

    @pl.when(step == items)
    def _():
        attend()


def attend_pairs(h1, weight, first, pairs, images, n_query):
    rows, width = h1.shape
    count = rows // images
    items = images * pairs
    now = lambda s: jnp.minimum(s, items - 1)
    last = lambda s: jnp.maximum(s - 1, 0)
    return pl.pallas_call(
        partial(attend_kernel, items=items, n_query=n_query),
        out_shape=(
            jax.ShapeDtypeStruct((rows, pairs * 384), BF),
            jax.ShapeDtypeStruct((images * n_query, pairs * 128), BF),
            jax.ShapeDtypeStruct((images, pairs, 2, n_query), F32),
        ),
        grid=(items + 1,),
        in_specs=[
            pl.BlockSpec((count, width), lambda s: (now(s) // pairs, 0)),
            pl.BlockSpec((width, 384), lambda s: (0, first + now(s) % pairs)),
        ],
        out_specs=[
            pl.BlockSpec((count, 384), lambda s: (now(s) // pairs, now(s) % pairs)),
            pl.BlockSpec((n_query, 128), lambda s: (last(s) // pairs, last(s) % pairs)),
            pl.BlockSpec(
                (1, 1, 2, n_query), lambda s: (last(s) // pairs, last(s) % pairs, 0, 0)
            ),
        ],
        scratch_shapes=[pltpu.VMEM((2, count, 384), BF)],
        compiler_params=pltpu.CompilerParams(vmem_limit_bytes=VMEM_BYTES),
        cost_estimate=estimate(
            2 * items * count * (n_query * 1200 + width * 384), rows * width * 8, 1
        ),
        name="attend",
    )(h1, weight)


def attend_back_pair(q_ref, kv_ref, do_ref, o_ref, log_ref):
    lane = lax.broadcasted_iota(jnp.int32, (1, 128), 1)
    first = lane < HEAD_DIM
    scale = jnp.asarray(HEAD_DIM**-0.5, BF)
    keys_all = kv_ref[:, 128:256]
    keys = head_split(first, keys_all)
    values = head_split(first, kv_ref[:, 256:])
    query = q_ref[:, :128]
    d_out = do_ref[...]
    queries = head_split(first, query)
    d_outs = head_split(first, d_out)
    keys_t = tuple(part.T for part in head_split(first, keys_all * scale))
    both = (d_out.astype(F32) * o_ref[...].astype(F32)).T
    d_query, d_keys, d_values = 0.0, 0.0, 0.0
    for head in range(2):
        row = jnp.sum(both[HEAD_DIM * head : HEAD_DIM * (head + 1)], 0, keepdims=True)
        scores = dot(keys[head], query, NT)
        probs = jnp.exp2(scores - log_ref[0, 0, head : head + 1, :])
        d_probs = dot(values[head], d_out, NT)
        d_scores = (probs * (d_probs - row)).astype(BF)
        d_keys = d_keys + dot(d_scores, queries[head], NN)
        d_values = d_values + dot(probs.astype(BF), d_outs[head], NN)
        d_query = d_query + dot(keys_t[head], d_scores, NN)
    return d_query.astype(BF), (d_keys * math.log(2.0)).astype(BF), d_values.astype(BF)


def attend_back_kernel(q_ref, kv_ref, do_ref, o_ref, log_ref, d_ref):
    parts = attend_back_pair(q_ref, kv_ref, do_ref, o_ref, log_ref)
    rows = parts[0].shape[1]
    d_ref[:rows, :128] = parts[0].T
    d_ref[rows:, :128] = jnp.zeros((d_ref.shape[0] - rows, 128), BF)
    for index, part in enumerate(parts[1:], 1):
        d_ref[:, 128 * index : 128 * (index + 1)] = part


def attend_back_apart(query, keys, d_out, out, log, pairs, n_query, n_key):
    over_q = lambda cols: pl.BlockSpec((n_query, cols), lambda h: (0, h))
    over_k = lambda cols: pl.BlockSpec((n_key, cols), lambda h: (0, h))
    return pl.pallas_call(
        attend_back_kernel,
        out_shape=jax.ShapeDtypeStruct((n_key, pairs * 384), BF),
        grid=(pairs,),
        in_specs=[
            over_q(384),
            over_k(384),
            over_q(128),
            over_q(128),
            pl.BlockSpec((1, 1, 2, n_query), lambda h: (0, h, 0, 0)),
        ],
        out_specs=over_k(384),
        compiler_params=pltpu.CompilerParams(vmem_limit_bytes=VMEM_BYTES),
        cost_estimate=estimate(2 * pairs * n_query * n_key * 2400, (n_query + n_key) * pairs * 1024),
        name="attend_back_apart",
    )(query, keys, d_out, out, log)


def attend_back_grad_kernel(
    core_ref, qkv_ref, do_ref, o_ref, log_ref, h1_ref, h1_a_ref, d_a_ref,
    d_ref, away_ref, own_ref, acc, turned, *, images, blocks
):
    image = pl.program_id(1)

    @pl.when(image == 0)
    def _():
        acc[...] = dot(d_a_ref[...].T, h1_a_ref[...], NN)

    d_query, d_keys, d_values = attend_back_pair(qkv_ref, qkv_ref, do_ref, o_ref, log_ref)
    d_ref[:, :128] = d_query.T
    d_ref[:, 128:256] = d_keys
    d_ref[:, 256:] = d_values
    d_turned = jnp.concatenate([d_query, d_keys.T, d_values.T], 0)
    acc[...] += dot(d_turned, h1_ref[...], NN)

    @pl.when(image == images - 1)
    def _():
        turned[...] = acc[...].T
        store_by_core(core_ref[0], turned, away_ref, own_ref, slice(None), blocks)


def attend_back_grad(
    qkv, d_out, out, log, h1, h1_a, d_a, core, pairs, images, count, blocks, count_y
):
    width = h1.shape[1]
    rows_a = h1_a.shape[0]
    over = lambda cols: pl.BlockSpec((count, cols), lambda h, i: (i, h))
    held = (count_y * blocks, width // (2 * count_y * blocks))
    grad = pl.BlockSpec((*held, 384), lambda h, i: (0, 0, h))
    return pl.pallas_call(
        partial(attend_back_grad_kernel, images=images, blocks=blocks),
        out_shape=(
            jax.ShapeDtypeStruct((images * count, pairs * 384), BF),
            jax.ShapeDtypeStruct((*held, pairs * 384), BF),
            jax.ShapeDtypeStruct((*held, pairs * 384), BF),
        ),
        grid=(pairs, images),
        in_specs=[
            pl.BlockSpec(memory_space=pltpu.SMEM),
            over(384),
            over(128),
            over(128),
            pl.BlockSpec((1, 1, 2, count), lambda h, i: (i, h, 0, 0)),
            pl.BlockSpec((count, width), lambda h, i: (i, 0)),
            pl.BlockSpec((rows_a, width), lambda h, i: (0, 0)),
            pl.BlockSpec((rows_a, 384), lambda h, i: (0, h)),
        ],
        out_specs=[over(384), grad, grad],
        scratch_shapes=[
            pltpu.VMEM((384, width), F32),
            pltpu.VMEM((width, 384), F32),
        ],
        compiler_params=pltpu.CompilerParams(vmem_limit_bytes=VMEM_BYTES),
        cost_estimate=estimate(
            images * 2 * pairs * count * count * 2800, images * count * pairs * 2048
        ),
        name="attend_back",
    )(core, qkv, d_out, out, log, h1, h1_a, d_a)


def gelu_parts(inner):
    scaled = inner * (0.5**0.5)
    upper = 0.5 * lax.erf(scaled) + 0.5
    bell = jnp.exp2(scaled * scaled * -math.log2(math.e) - 0.5 * math.log2(2.0 * math.pi))
    return upper, inner * bell


def mlp_kernel(
    x0_ref, mixed0_ref, mixed1_ref, wout_ref, gain_ref, wup_ref,
    x1_ref, slope_ref, xsum_ref, asum_ref, *, per
):
    mixed = jnp.concatenate([mixed0_ref[...], mixed1_ref[...]], 1)
    x1 = x0_ref[...] + dot(mixed, wout_ref[...], NN)
    x1_ref[...] = x1
    h2 = (normed(x1)[0] * gain_ref[...]).astype(BF)

    @pl.when(pl.program_id(0) % per == 0)
    def _():
        xsum_ref[...] = jnp.zeros_like(xsum_ref)
        asum_ref[...] = jnp.zeros_like(asum_ref)

    xsum_ref[0] += jnp.sum(x1, 0, keepdims=True)
    width = 512
    for first in range(0, wup_ref.shape[1], width):
        cols = slice(first, first + width)
        inner = dot(h2, wup_ref[:, cols], NN)
        upper, slope = gelu_parts(inner)
        slope_ref[:, cols] = (upper + slope).astype(BF)
        asum_ref[0, :, cols] += jnp.sum(inner * upper, 0, keepdims=True)


def mlp(x0, mixed, w_all, hidden, gain, images, block):
    rows, width = x0.shape
    per = rows // images // block
    return pl.pallas_call(
        partial(mlp_kernel, per=per),
        out_shape=(
            jax.ShapeDtypeStruct((rows, width), F32),
            jax.ShapeDtypeStruct((rows, hidden), BF),
            jax.ShapeDtypeStruct((images, 1, width), F32),
            jax.ShapeDtypeStruct((images, 1, hidden), F32),
        ),
        grid=(rows // block,),
        in_specs=[
            pl.BlockSpec((block, width), lambda i: (i, 0)),
            pl.BlockSpec((block, width // 2), lambda i: (i, 0)),
            pl.BlockSpec((block, width // 2), lambda i: (i, 0)),
            pl.BlockSpec((width, width), lambda i: (0, 3)),
            pl.BlockSpec((1, width), lambda i: (0, 0)),
            pl.BlockSpec((width, hidden), lambda i: (0, 4 * width // hidden)),
        ],
        out_specs=[
            pl.BlockSpec((block, width), lambda i: (i, 0)),
            pl.BlockSpec((block, hidden), lambda i: (i, 0)),
            pl.BlockSpec((1, 1, width), lambda i: (i // per, 0, 0)),
            pl.BlockSpec((1, 1, hidden), lambda i: (i // per, 0, 0)),
        ],
        compiler_params=pltpu.CompilerParams(vmem_limit_bytes=VMEM_BYTES),
        cost_estimate=estimate(4 * rows * width * (hidden + width), rows * hidden * 4),
        name="mlp",
    )(x0, *mixed, w_all, gain, w_all)


def head_kernel(
    image_ref, xsum_ref, asum_ref, sums_a_ref, down_ref, head_ref, whole_ref, total_ref,
    loss_ref, rows_ref, dx2_ref, dact_ref, *, classes, own, slots
):
    width, hidden = down_ref.shape
    fill = rows_ref.shape[0] - own - 1
    place_y = image_ref[2 * slots + 2]

    def column(values):
        row = lax.broadcasted_iota(jnp.int32, (own + 1 + fill, 1), 0)
        out = jnp.zeros_like(row)
        for index, value in enumerate(values):
            out = jnp.where(row == index, value, out)
        return out

    def of_images(first, last):
        return column([image_ref[first + place_y * own + i] for i in range(own)] + [image_ref[last]])

    label = of_images(0, 2 * slots)
    alive = of_images(slots, 2 * slots + 1).astype(F32)
    once = column([1] * own + [jnp.where(place_y == 0, 1, 0)]).astype(F32)

    def stacked(ref, cols):
        rows = [ref[image] for image in range(own)] + [sums_a_ref[:, cols]]
        return jnp.concatenate(rows + [jnp.zeros((fill, rows[0].shape[1]), F32)], 0)

    xsum = stacked(xsum_ref, slice(0, width))
    asum = stacked(asum_ref, slice(width, width + hidden))
    high = asum.astype(BF)
    low = (asum - high.astype(F32)).astype(BF)
    whole = whole_ref[...]
    down = down_ref[...]
    both = dot(jnp.concatenate([high, low], 0), down, NT)
    pooled = (xsum + (both[: both.shape[0] // 2] + both[both.shape[0] // 2 :])) / whole
    pooled_low = pooled.astype(BF)
    head = head_ref[...]
    place = lax.broadcasted_iota(jnp.int32, (1, head.shape[1]), 1)
    logits = jnp.where(place < classes, dot(pooled_low, head, NN), -1e30)
    top = jnp.max(logits, -1, keepdims=True)
    norm_log = top + jnp.log(jnp.sum(jnp.exp(logits - top), -1, keepdims=True))
    hot = place == label
    true_logit = jnp.sum(jnp.where(hot, logits, 0.0), -1, keepdims=True)
    loss = (norm_log - true_logit) * alive * once
    lane = lax.broadcasted_iota(jnp.int32, (1, loss_ref.shape[1]), 1)
    loss_a, loss_b = loss[own : own + 1], jnp.sum(loss[:own], 0, keepdims=True)
    loss_ref[...] = jnp.where(lane == 1, loss_a, jnp.where(lane == 2, loss_b, 0.0))
    soft = jnp.exp(logits - norm_log) - hot.astype(F32)
    d_logits = (soft * alive / total_ref[...]).astype(BF)
    d_x2 = dot(d_logits, head, NT) / whole
    d_mix = d_x2.astype(BF)
    d_act = dot(d_mix, down, NN)
    for image in range(own + 1):
        dx2_ref[image] = d_x2[image : image + 1]
        dact_ref[image] = d_act[image : image + 1]
    rows_ref[:, :hidden] = high
    rows_ref[:, hidden : hidden + width] = pooled_low
    rows_ref[:, hidden + width : hidden + 2 * width] = (d_mix * once).astype(BF)
    rows_ref[:, hidden + 2 * width :] = (d_logits * once).astype(BF)


def head_step(images, xsum, asum, sums_a, w_down_head, whole, total, classes):
    own, _, width = xsum.shape
    hidden = asum.shape[2]
    rows = whole.shape[0]
    padded = w_down_head.shape[1] - hidden
    spec = lambda shape, *place: pl.BlockSpec(shape, lambda i: place or (0,) * len(shape))
    shapes = (
        ((1, 128), F32),
        ((rows, hidden + 2 * width + padded), BF),
        ((own + 1, 1, width), F32),
        ((own + 1, 1, hidden), F32),
    )
    return pl.pallas_call(
        partial(head_kernel, classes=classes, own=own, slots=(images.shape[0] - 3) // 2),
        out_shape=tuple(jax.ShapeDtypeStruct(*shape) for shape in shapes),
        grid=(1,),
        in_specs=[
            pl.BlockSpec(memory_space=pltpu.SMEM),
            spec(xsum.shape),
            spec(asum.shape),
            spec(sums_a.shape),
            spec((width, hidden), 0, 0),
            spec((width, padded), 0, hidden // padded),
            spec((rows, 1)),
            spec((1, 1)),
        ],
        out_specs=[spec(shape[0]) for shape in shapes],
        compiler_params=pltpu.CompilerParams(vmem_limit_bytes=VMEM_BYTES),
        cost_estimate=estimate(1 << 32, 8 << 20),
        name="head",
    )(images, xsum, asum, sums_a, w_down_head, w_down_head, whole, total)


def mlp_back_kernel(*refs, steps):
    parts = (refs[0:6], refs[6:12])
    wout_ref, gain_ref, wup_ref = refs[12:15]
    outs = (refs[15:18], refs[18:21])
    grad_ref, ggain_ref = refs[21:23]
    up_acc, out_acc = refs[23:25]
    step = pl.program_id(0)

    def body(inputs, outputs, begin):
        slope_ref, dact_ref, x1_ref, dx2_ref, *mixed_refs = inputs
        dx1_ref, *dmixed_refs = outputs
        gain = gain_ref[...]
        hat, scale = normed(x1_ref[...])
        h2_t = (hat * gain).astype(BF).T
        width = 768
        cuts = [slice(first, first + width) for first in range(0, slope_ref.shape[1], width)]
        d_inner = [
            (slope_ref[:, cols].astype(F32) * dact_ref[0, :, cols]).astype(BF) for cols in cuts
        ]
        d_h2 = sum(dot(part, wup_ref[:, cols], NT) for part, cols in zip(d_inner, cuts))
        gain_grad = jnp.sum(d_h2 * hat, 0, keepdims=True)
        ggain_ref[...] = gain_grad if begin else ggain_ref[...] + gain_grad
        rows = x1_ref.shape[0] // len(cuts)
        for index, (part, cols) in enumerate(zip(d_inner, cuts)):
            share = slice(index * rows, (index + 1) * rows)
            grad = dot(h2_t, part, NN)
            up_acc[:, cols] = grad if begin else up_acc[:, cols] + grad
            dx1_ref[share] = dx2_ref[0] + norm_back(d_h2[share], gain, hat[share], scale[share])
        d_attn = dx1_ref[...].astype(BF)
        mixed = jnp.concatenate([mixed_ref[...] for mixed_ref in mixed_refs], 1)
        grad = dot(mixed.T, d_attn, NN)
        out_acc[...] = grad if begin else out_acc[...] + grad
        d_mixed = dot(d_attn, wout_ref[...], NT).astype(BF)
        half = mixed_refs[0].shape[1]
        for index, dmixed_ref in enumerate(dmixed_refs):
            dmixed_ref[...] = d_mixed[:, index * half : (index + 1) * half]

    @pl.when(step == 0)
    def _():
        body(parts[1], outs[1], True)

    @pl.when(step > 0)
    def _():
        body(parts[0], outs[0], False)

    @pl.when(step == steps)
    def _():
        hidden = up_acc.shape[1]
        grad_ref[:, :hidden] = up_acc[...].astype(BF)
        grad_ref[:, hidden:] = out_acc[...].astype(BF)


def mlp_back(part_b, part_a, w_all, gain, images, block):
    rows, width = part_b[2].shape
    rows_a = part_a[2].shape[0]
    hidden = part_b[0].shape[1]
    steps = rows // block
    per = steps // images
    at = lambda i: jnp.maximum(i - 1, 0)
    moving = lambda cols: pl.BlockSpec((block, cols), lambda i: (at(i), 0))
    still = lambda shape: pl.BlockSpec(shape, lambda i: (0,) * len(shape))
    image = lambda cols: pl.BlockSpec((1, 1, cols), lambda i: (at(i) // per, 0, 0))
    last = lambda cols: pl.BlockSpec((1, 1, cols), lambda i: (images, 0, 0))
    half = width // 2
    outs = []
    for count in (rows, rows_a):
        outs += [
            jax.ShapeDtypeStruct((count, width), F32),
            jax.ShapeDtypeStruct((count, half), BF),
            jax.ShapeDtypeStruct((count, half), BF),
        ]
    return pl.pallas_call(
        partial(mlp_back_kernel, steps=steps),
        out_shape=(
            *outs,
            jax.ShapeDtypeStruct((width, hidden + width), BF),
            jax.ShapeDtypeStruct((1, width), F32),
        ),
        grid=(steps + 1,),
        in_specs=[
            moving(hidden), image(hidden), moving(width), image(width), moving(half), moving(half),
            still((rows_a, hidden)), last(hidden), still((rows_a, width)),
            last(width), still((rows_a, half)), still((rows_a, half)),
            pl.BlockSpec((width, width), lambda i: (0, 3)),
            still((1, width)),
            pl.BlockSpec((width, hidden), lambda i: (0, 4 * width // hidden)),
        ],
        out_specs=[
            moving(width), moving(half), moving(half),
            still((rows_a, width)), still((rows_a, half)), still((rows_a, half)),
            still((width, hidden + width)), still((1, width)),
        ],
        scratch_shapes=[pltpu.VMEM((width, hidden), F32), pltpu.VMEM((width, width), F32)],
        compiler_params=pltpu.CompilerParams(vmem_limit_bytes=VMEM_BYTES),
        cost_estimate=estimate(
            4 * (rows + rows_a) * width * (hidden + width), (rows + rows_a) * hidden * 4
        ),
        name="mlp_back",
    )(*part_b, *part_a, w_all, gain, w_all)


def embed_back_kernel(core_ref, *refs, steps, groups, pieces, blocks, parts_b, parts_a):
    n_b, n_a = 3 + pieces + groups, 4 + groups * parts_a
    inputs_b, inputs_a = refs[:n_b], refs[n_b : n_b + n_a]
    gain_ref, gain_grad_ref, *rest = refs[n_b + n_a :]
    weight_refs = rest[:groups]
    away_ref, own_ref, acc_b, acc_a, acc_tab, gain_acc = rest[groups:]
    step = pl.program_id(0)

    def body(inputs, acc, parts, pixel_ref, terms):
        x0_ref, dx1_ref, tab_ref = inputs[:3]
        gain = gain_ref[...]
        count = x0_ref.shape[0] // parts
        turned = []
        for part in range(parts):
            rows = slice(part * count, (part + 1) * count)
            hat, scale = normed(x0_ref[rows])
            d_h1 = 0.0
            for group, weight_ref in enumerate(weight_refs):
                term_refs = inputs[len(inputs) - (groups - group) * terms :][:terms]
                d_qkv = term_refs[0][rows]
                if terms > 1:
                    d_qkv = sum(ref[rows].astype(F32) for ref in term_refs).astype(BF)
                d_h1 = d_h1 + dot(d_qkv, weight_ref[...], NT)
            gain_acc[0:1] += jnp.sum(d_h1 * hat, 0, keepdims=True)
            d_x0 = dx1_ref[rows] + norm_back(d_h1, gain, hat, scale)
            turned.append(d_x0.astype(BF).T)
        turned = jnp.concatenate(turned, 1)
        acc_tab[...] += dot(turned, tab_ref[...], NN)
        acc[:, : pixel_ref.shape[1]] += dot(turned, pixel_ref[...], NN)

    @pl.when(step == 0)
    def _():
        for acc in (acc_b, acc_a, acc_tab, gain_acc):
            acc[...] = jnp.zeros_like(acc)
        gain_acc[1:2] = gain_grad_ref[...]
        body(inputs_a, acc_a, 1, inputs_a[3], parts_a)

    for piece in range(pieces):

        @pl.when((step > 0) & ((step - 1) % pieces == piece))
        def _(piece=piece):
            body(inputs_b, acc_b, parts_b, inputs_b[3 + piece], 1)

    @pl.when(step == steps)
    def _():
        place = lax.broadcasted_iota(jnp.int32, (8, 128), 1)
        row = lax.broadcasted_iota(jnp.int32, (8, 128), 0)
        spots = jnp.where((place == 126 + row) & (row < 2), 1.0, 0.0).astype(BF)
        acc_tab[...] += lax.dot_general(
            gain_acc[...].astype(BF), spots, ROWS_DIM, preferred_element_type=F32
        )
        at = 0
        for acc in (acc_b, acc_a, acc_tab):
            cols = slice(at, at + acc.shape[1])
            at += acc.shape[1]
            store_by_core(core_ref[0], acc, away_ref, own_ref, cols, blocks)


def embed_back(
    x0_b, dx1_b, tab_b, pixels_b, d_b, x0_a, dx1_a, tab_a, pixels_a, d_a, gain, gain_grad, w_all,
    core, blocks, images, depths, count_y
):
    rows, width = x0_b.shape
    pieces = len(pixels_b)
    steps = images * pieces
    block = rows // steps
    at = lambda i: jnp.maximum(i - 1, 0)
    moving = lambda array: pl.BlockSpec((block, array.shape[1]), lambda i: (at(i), 0))
    still = lambda shape: pl.BlockSpec(shape, lambda i: (0,) * len(shape))
    inputs_a = (x0_a, dx1_a, tab_a, pixels_a, *sum(d_a, ()))
    rows_a = x0_a.shape[0]
    grad = (count_y * blocks, width // (2 * count_y * blocks), sum(depths) + 128)
    return pl.pallas_call(
        partial(
            embed_back_kernel, steps=steps, groups=len(d_b), pieces=pieces, blocks=blocks,
            parts_b=max(1, block // 256), parts_a=len(d_a[0]),
        ),
        out_shape=(jax.ShapeDtypeStruct(grad, BF), jax.ShapeDtypeStruct(grad, BF)),
        grid=(steps + 1,),
        in_specs=[pl.BlockSpec(memory_space=pltpu.SMEM)]
        + [moving(x0_b), moving(dx1_b)]
        + [pl.BlockSpec((block, 128), lambda i: (at(i) % pieces, 0))]
        + [
            pl.BlockSpec((block, array.shape[1]), lambda i: (at(i) // pieces, 0))
            for array in pixels_b
        ]
        + [moving(array) for array in d_b]
        + [still((rows_a, array.shape[1])) for array in inputs_a]
        + [still((1, width)), still((1, width))]
        + [
            pl.BlockSpec((width, array.shape[1]), partial(lambda group, i: (0, group), group))
            for group, array in enumerate(d_b)
        ],
        out_specs=[still(grad), still(grad)],
        scratch_shapes=[pltpu.VMEM((width, depth), F32) for depth in (*depths, 128)]
        + [pltpu.VMEM((8, width), F32)],
        compiler_params=pltpu.CompilerParams(vmem_limit_bytes=VMEM_BYTES),
        cost_estimate=estimate(2 * rows * width * (3 * width + 640), rows * 10000),
        name="embed_back",
    )(core, x0_b, dx1_b, tab_b, *pixels_b, *d_b, *inputs_a, gain, gain_grad, *[w_all] * len(d_b))


def resize_back_kernel(got_ref, table_b_ref, table_a_ref, sums_ref, sent_ref, small_ref, *, rows, at):
    owners, _, lanes = sent_ref.shape
    total = jnp.zeros(small_ref.shape, F32)
    for block in range(got_ref.shape[0]):
        total = total + got_ref[block].astype(F32)
    small_ref[...] = total
    parts, square = [], 0.0
    for channel in range(3):
        part = 0.0
        for table_ref, first in ((table_b_ref, 0), (table_a_ref, at)):
            size = table_ref.shape[0]
            part = part + lax.dot_general(
                total[:, first + channel * size : first + (channel + 1) * size],
                table_ref[...],
                NN,
                precision=HIGH,
                preferred_element_type=F32,
            )
        square = square + jnp.sum(part * part)
        parts.append(part)
    width = BASE * BASE * 3 // owners
    kern = jnp.concatenate(parts + [jnp.zeros((rows, lanes), F32)], 1)
    lane = lax.broadcasted_iota(jnp.int32, (1, lanes), 1)
    last = total[:, total.shape[1] - lanes :]
    pos = jnp.where(lane < 49, last + pltpu.roll(last, lanes - 49, 1), 0.0)
    last = jnp.where(lane < 126, pos, last)
    small_ref[:, total.shape[1] - lanes :] = last
    square = square + jnp.sum(last * last) + jnp.sum(jnp.where(lane == 0, sums_ref[...], 0.0))
    beside = jnp.where(lane == width, square, 0.0)
    for index in (1, 2):
        beside = beside + jnp.where(lane == width + index, pltpu.roll(sums_ref[...], width, 1), 0.0)
    for owner in range(owners):
        sent_ref[owner] = jnp.where(
            lane < width, kern[:, owner * width : owner * width + lanes], beside
        )


def resize_back(got, tables, sums, rows, at, owners, lanes):
    cols = got.shape[2]
    return pl.pallas_call(
        partial(resize_back_kernel, rows=rows, at=at),
        out_shape=(
            jax.ShapeDtypeStruct((owners, rows, lanes), F32),
            jax.ShapeDtypeStruct((rows, cols), F32),
        ),
        in_specs=[pl.BlockSpec(memory_space=pltpu.VMEM)] * 4,
        out_specs=[pl.BlockSpec(memory_space=pltpu.VMEM)] * 2,
        compiler_params=pltpu.CompilerParams(vmem_limit_bytes=VMEM_BYTES),
        cost_estimate=estimate(1 << 28, 4 << 20),
        name="resize_back",
    )(got, *tables, sums)


def update_kernel(got_ref, small_ref, qkv_ref, out_ref, up_ref, down_ref, head_ref, count_ref, *refs, width):
    masters, firsts, seconds = refs[0:7], refs[7:14], refs[14:21]
    new, new_firsts, new_seconds = refs[21:28], refs[28:35], refs[35:42]
    norm_ref, stat_ref = refs[42:]
    owners, rows, lanes = got_ref.shape
    sums = got_ref[0, 0:1, :]
    for owner in range(1, owners):
        sums = sums + got_ref[owner, 0:1, :]
    lane = lax.broadcasted_iota(jnp.int32, (1, lanes), 1)
    norm = jnp.sqrt(jnp.sum(jnp.where(lane == width, sums, 0.0), 1, keepdims=True))
    factor = jnp.minimum(1.0, CLIP / (norm + 1e-06))
    sums = pltpu.roll(sums, lanes - width, 1)
    ratio = sums / jnp.maximum(count_ref[...], 1.0)
    norm_ref[...] = norm
    stat_ref[...] = ratio[:, 1:3]
    kern = jnp.concatenate([got_ref[owner] for owner in range(owners)], 0).T[:width]
    small = small_ref[:, small_ref.shape[1] - lanes :]
    grads = (
        (Ellipsis, qkv_ref[...]),
        (Ellipsis, out_ref[...]),
        (0, up_ref[...]),
        (1, down_ref[...]),
        (Ellipsis, kern),
        (Ellipsis, small[:, :49]),
        (Ellipsis, head_ref[...]),
        (Ellipsis, small[:, 126:128].T),
    )
    for index, (at, grad) in zip((0, 1, 2, 2, 3, 4, 5, 6), grads):
        new[index][at], new_firsts[index][at], new_seconds[index][at] = adamw(
            masters[index][at], firsts[index][at], seconds[index][at], grad * factor, RATES[index]
        )


def update(got, small, grads, count, masters, firsts, seconds, width):
    full = pl.BlockSpec(memory_space=pltpu.VMEM)
    shapes = [jax.ShapeDtypeStruct(array.shape, F32) for array in masters]
    inputs = (got, small, *grads, count, *masters, *firsts, *seconds)
    return pl.pallas_call(
        partial(update_kernel, width=width),
        out_shape=(
            *shapes * 3, jax.ShapeDtypeStruct((1, 1), F32), jax.ShapeDtypeStruct((1, 2), F32)
        ),
        in_specs=[full] * len(inputs),
        out_specs=[full] * 23,
        compiler_params=pltpu.CompilerParams(vmem_limit_bytes=VMEM_BYTES),
        cost_estimate=estimate(1 << 28, 16 << 20),
        name="update",
    )(*inputs)


def after(value, *others):
    return lax.optimization_barrier((value, *others))[0]


def padded_cols(array, width):
    return jnp.pad(array, ((0, 0), (0, width - array.shape[1])))


def round_up(count, unit):
    return -(-count // unit) * unit


def fast_step(
    pixels_a, pixels_b, labels_a, labels_b, live_a, live_b, masters, firsts, seconds
):
    qkv_w, out_w, mlp_w, kern_w, pos_w, head_w, gains = masters
    seq = lax.axis_size("y")
    row = lax.axis_index("y")
    count_all = seq * lax.axis_size("z") * lax.axis_size("x") * 2
    flat_index = lax.axis_index(AXES)
    lead = (row == 0).astype(F32)
    width = HEADS * HEAD_DIM
    hidden = mlp_w.shape[2]
    classes = head_w.shape[1]
    classes_up = round_up(classes, 1024)
    rows_own = qkv_w.shape[0]
    rows_kern = kern_w.shape[0]
    groups = 2
    span = width // groups
    pairs = span // 128

    images_a, rows_a, grid_a, depth_a = pixels_a.shape
    images_b, rows_b, grid_b, depth_b = pixels_b.shape
    own_b = images_b // seq
    parts_b, tabs_b, slices = [], [], []
    table_b = jnp.asarray(place_table(grid_b))
    table_a = jnp.asarray(place_table(grid_a))
    span_b, span_a = rows_b * grid_b, rows_a * grid_a
    for step in range(seq):
        part = lax.dynamic_slice_in_dim(
            pixels_b, ((row + step) % seq) * own_b, own_b, 0
        )
        part = part.reshape(own_b * rows_b * grid_b, depth_b)
        if step:
            slices.append(part)
        parts_b.append(shift(part, "y", step) if step else part)
        tabs_b.append(lax.dynamic_slice_in_dim(table_b, ((row - step) % seq) * span_b, span_b, 0))
    tab_a = lax.dynamic_slice_in_dim(table_a, row * span_a, span_a, 0)
    whole_a, whole_b = grid_a * grid_a, grid_b * grid_b

    flags = (jnp.concatenate([live_a, live_b]).astype(F32) * lead).astype(BF)
    slots = flags.shape[0]
    lanes = round_up(rows_kern + slots, 128)
    sent = jnp.concatenate(
        [
            kern_w.astype(BF).T,
            jnp.broadcast_to(flags[None], (width, slots)),
            jnp.zeros((width, lanes - rows_kern - slots), BF),
        ],
        1,
    )
    sent = after(sent, *slices)
    got = lax.all_to_all(sent, AXES, split_axis=0, concat_axis=0, tiled=True)
    def group_cols(array, group):
        shaped = array.reshape(rows_own, 3, groups, pairs, 128)[:, :, group]
        return shaped.transpose(0, 2, 1, 3).reshape(rows_own, 3 * span)

    qkv_low = qkv_w.astype(BF)
    held = jnp.concatenate(stage(group_cols(qkv_low, 0)[None], STAGES[0]), 0)
    held = jnp.concatenate(stage(held, STAGES[1]), 0)
    packed = jnp.concatenate(
        [group_cols(qkv_low, group) for group in range(groups)]
        + [out_w.astype(BF), mlp_w[0].astype(BF)],
        1,
    )
    got, held, packed, tab_a, tab_b, *parts_b = lax.optimization_barrier(
        (got, held, packed, tab_a, jnp.concatenate(tabs_b, 0), *parts_b)
    )
    held = stage(held, STAGES[2])
    got = got.reshape(count_all, rows_own, lanes)
    counts = got[:, 0, rows_kern : rows_kern + slots]
    got = got.astype(F32)
    kern_cols = got[:, :, :rows_kern].transpose(1, 0, 2).reshape(rows_own, 3, BASE * BASE)

    w_all = lax.all_gather(packed, AXES, axis=0, tiled=True)

    tables = [resize_table(PATCH_B), resize_table(PATCH_A)]
    sizes = [3 * table.shape[0] for table in tables]
    resized = [
        jnp.einsum("dck,pk->dcp", kern_cols, jnp.asarray(table), precision=HIGH).reshape(
            rows_own, -1
        )
        for table in tables
    ]
    depths = [round_up(size, 128) for size in sizes]
    spot = sum(depths)
    pos_t = pos_w.astype(BF).T
    edge = jnp.zeros((rows_own, 28), BF)
    small = jnp.concatenate(
        [padded_cols(piece.astype(BF), depth) for piece, depth in zip(resized, depths)]
        + [pos_t, pos_t, edge, gains.astype(BF).T],
        1,
    )
    w_small, held = gather_rows(small, held)
    held = jnp.concatenate(held, 0)
    w_down_head = lax.all_gather(
        after(
            jnp.concatenate([mlp_w[1].astype(BF), padded_cols(head_w.astype(BF), classes_up)], 1),
            w_small,
        ),
        AXES, axis=0, tiled=True,
    )

    gain_rows = w_small[:, spot + 126 :].T.astype(F32)
    gain1, gain2 = gain_rows[0:1], gain_rows[1:2]
    flat_a = pixels_a.reshape(span_a, depth_a)
    block = min(512, whole_b)
    x0_a, h1_a = embed([flat_a], tab_a, w_small, depths[0], spot, gain1, 1)
    h1_a, *held = lax.optimization_barrier((h1_a, *stage(held, STAGES[3])))
    w_first = place_blocks(held, stage_owners())
    h1_all = jnp.concatenate([h1_a] + [shift(h1_a, "y", step) for step in range(1, seq)], 0)
    x0_b, h1_b = embed(
        [after(parts_b[0], h1_a), *parts_b[1:]], tab_b, w_small, 0, spot, gain1, own_b
    )
    h1_b, h1_all = lax.optimization_barrier((h1_b, h1_all))
    outs_a, outs_b = [], []
    ready = h1_b
    for group in range(groups):
        outs_b.append(
            attend_pairs(
                after(h1_b, ready), *((w_all, group * pairs) if group else (w_first, 0)),
                pairs, own_b, whole_b,
            )
        )
        ready = outs_b[-1][0]
    for group in range(groups):
        outs_a.append(attend_pairs(after(h1_all, ready), w_all, group * pairs, pairs, 1, span_a))
    qkvs_a, qkvs_b = [out[0] for out in outs_a], [out[0] for out in outs_b]
    mixed_a, mixed_b = [out[1] for out in outs_a], [out[1] for out in outs_b]

    x1_a, slope_a, xsum_a, asum_a = mlp(x0_a, mixed_a, w_all, hidden, gain2, 1, span_a)
    sums_a = jnp.concatenate([xsum_a[0], asum_a[0]], 1)
    sums_a = sum([shift(sums_a, "y", step) for step in range(1, seq)], sums_a)
    x1_b, slope_b, xsum_b, asum_b = mlp(after(x0_b, x1_a), mixed_b, w_all, hidden, gain2, own_b, block)

    images = jnp.concatenate([labels_b, live_b, labels_a, live_a, row.reshape(1).astype(jnp.int32)])
    images, counts, h1_b = lax.optimization_barrier((images, counts, h1_b))
    counts = jnp.sum(counts.astype(F32), 0, keepdims=True)
    split = live_a.shape[0]
    count = jnp.concatenate(
        [jnp.sum(part, 1, keepdims=True) for part in (counts[:, :split], counts[:, split:])], 1
    )
    total = jnp.maximum(jnp.sum(count), 1.0)
    rows_up = round_up(own_b + 1, 8)
    whole = np.ones((rows_up, 1), np.float32)
    whole[:own_b], whole[own_b] = whole_b, whole_a
    loss_sums, rows_out, d_x2, d_act = head_step(
        images, xsum_b, asum_b, sums_a, w_down_head, jnp.asarray(whole), total.reshape(1, 1), classes
    )

    image_rows = lax.all_gather(rows_out, AXES, axis=0, tiled=True)

    d_x1_b, d0_b, d1_b, d_x1_a, d0_a, d1_a, grad_up_out, grad_gain2 = mlp_back(
        (slope_b, d_act, x1_b, d_x2, *mixed_b),
        (slope_a, d_act, x1_a, d_x2, *mixed_a),
        w_all, gain2, own_b, block,
    )
    d_mixed_a, d_mixed_b = (d0_a, d1_a), (d0_b, d1_b)

    d_alls, d_groups_a = [], []
    for group in range(groups):
        d_all = attend_back_apart(
            qkvs_a[group], qkvs_a[group], d_mixed_a[group], mixed_a[group],
            outs_a[group][2], pairs, span_a, seq * span_a,
        )
        d_alls.append(d_all)
        d_groups_a += [
            shift(d_all[step * span_a : (step + 1) * span_a], "y", seq - step)
            for step in range(1, seq)
        ]
    own_up_out = lax.psum_scatter(
        after(grad_up_out, image_rows, *d_alls), AXES, scatter_dimension=0, tiled=True
    ).astype(F32)
    core = lax.axis_index("core").reshape(1).astype(jnp.int32)
    blocks = lax.axis_size("z") * lax.axis_size("x")
    d_groups_b, own_groups = [], []
    ready = d_alls[-1]
    for group in range(groups):
        got, away, own = attend_back_grad(
            qkvs_b[group],
            after(d_mixed_b[group], ready),
            mixed_b[group], outs_b[group][2],
            h1_b, h1_all, d_alls[group], core, pairs, own_b, whole_b, blocks, seq,
        )
        if group:
            away, own, own_groups[-1] = lax.optimization_barrier((away, own, own_groups[-1]))
        else:
            away, own, *d_groups_a = lax.optimization_barrier((away, own, *d_groups_a))
        d_groups_b.append(got)
        own_groups.append(scatter_rows(away, own))
        ready = got
    moved = seq - 1
    d_groups_a = [
        (d_all, *d_groups_a[group * moved : (group + 1) * moved])
        for group, d_all in enumerate(d_alls)
    ]
    away, own = embed_back(
        x0_b, after(d_x1_b, ready), tab_b, parts_b, d_groups_b,
        x0_a, d_x1_a, tab_a, flat_a, d_groups_a,
        gain1, grad_gain2, w_all, core, blocks, own_b, depths, seq,
    )
    away, own, own_up_out, *own_groups = lax.optimization_barrier(
        (away, own, own_up_out, *own_groups)
    )
    own_qkv = jnp.stack([block_sum(got) for got in own_groups], 1)
    own_qkv = own_qkv.reshape(rows_own, groups * pairs, 3, 128)
    own_qkv = own_qkv.transpose(0, 2, 1, 3).reshape(rows_own, 3 * width)
    small_parts = scatter_rows(away, own)

    columns = lambda lo: lax.dynamic_slice_in_dim(
        image_rows[:, lo : lo + width], flat_index * rows_own, rows_own, 1
    )
    own_down = lax.dot_general(
        columns(hidden + width), image_rows[:, :hidden], ROWS_DIM, preferred_element_type=F32
    )
    own_head = lax.dot_general(
        columns(hidden),
        image_rows[:, hidden + 2 * width : hidden + 2 * width + classes],
        ROWS_DIM,
        preferred_element_type=F32,
    )
    own_up, own_out = own_up_out[:, :hidden], own_up_out[:, hidden:]
    square_sum = sum(
        jnp.sum(piece * piece) for piece in (own_up_out, own_down, own_head, own_qkv)
    )
    sums = loss_sums + padded_cols(square_sum.reshape(1, 1), lanes)
    sent, own_small = resize_back(
        small_parts, [jnp.asarray(table) for table in tables], sums, rows_own, depths[0],
        count_all, lanes,
    )
    got = lax.all_to_all(sent, AXES, split_axis=0, concat_axis=0, tiled=True)
    counts = padded_cols(jnp.pad(count, ((0, 0), (1, 0))), lanes)
    turn = lambda arrays: [array.T if at == 4 else array for at, array in enumerate(arrays)]
    *done, grad_norm, size_stats = update(
        got, own_small, (own_qkv, own_out, own_up, own_down, own_head), counts,
        turn(masters), turn(firsts), turn(seconds), rows_kern,
    )
    done = [item for at in (0, 7, 14) for item in turn(done[at : at + 7])]
    return (*done, size_stats.reshape(2), grad_norm.reshape(()))


def fits_fast(mesh, pixels_a, pixels_b):
    dp, seq = mesh.shape["dp"], mesh.shape["seq"]
    images_b, rows_b, grid_b, _ = pixels_b.shape
    rows_a, grid_a = pixels_a.shape[1:3]
    return (
        dp % 8 == 0
        and rows_b % seq == 0
        and rows_a % seq == 0
        and images_b % (dp * seq) == 0
        and images_b // dp <= 256
        and pixels_a.shape[0] == dp
        and grid_b * grid_b % 256 == 0
        and rows_a // seq * grid_a % 32 == 0
    )


def fast_on_device(*args):
    return fast_step(*args[:6], args[6:13], args[13:20], args[20:27])


def on_device(
    pixels_a,
    pixels_b,
    labels_a,
    labels_b,
    live_a,
    live_b,
    qkv_w,
    out_w,
    mlp_w,
    kern_w,
    pos_w,
    head_w,
    gains,
    qkv_m,
    out_m,
    mlp_m,
    kern_m,
    pos_m,
    head_m,
    gains_m,
    qkv_v,
    out_v,
    mlp_v,
    kern_v,
    pos_v,
    head_v,
    gains_v,
):
    masters = (qkv_w, out_w, mlp_w, kern_w, pos_w, head_w, gains)
    firsts = (qkv_m, out_m, mlp_m, kern_m, pos_m, head_m, gains_m)
    seconds = (qkv_v, out_v, mlp_v, kern_v, pos_v, head_v, gains_v)
    bf16 = jnp.bfloat16
    w_qkv, w_out, w_mlp, w_kern, w_pos, w_head, w_gain = (
        lax.all_gather(qkv_w.astype(bf16), ("dp", "seq"), axis=0, tiled=True),
        lax.all_gather(out_w.astype(bf16), ("dp", "seq"), axis=0, tiled=True),
        lax.all_gather(mlp_w.astype(bf16), ("dp", "seq"), axis=1, tiled=True),
        lax.all_gather(kern_w.astype(bf16), ("dp", "seq"), axis=0, tiled=True),
        lax.all_gather(pos_w.astype(bf16), ("dp", "seq"), axis=1, tiled=True),
        lax.all_gather(head_w.astype(bf16), ("dp", "seq"), axis=0, tiled=True),
        lax.all_gather(gains.astype(bf16), ("dp", "seq"), axis=1, tiled=True),
    )
    seq_count = lax.axis_size("seq")
    seq_place = lax.axis_index("seq")
    gain_full = w_gain.astype(jnp.float32)
    kern_full = w_kern.astype(jnp.float32)
    pos_full = w_pos.astype(jnp.float32)
    size_sets = ((pixels_a, labels_a, live_a, PATCH_A), (pixels_b, labels_b, live_b, PATCH_B))
    embeds, flats, kern_backs, pos_backs, layouts = ([], [], [], [], [])
    start = 0
    for pixels, labels, live, patch in size_sets:
        images, rows, grid, depth = pixels.shape
        flat = pixels.reshape(images * rows * grid, depth)
        resized, kern_back = jax.vjp(partial(kernel_resize, patch=patch), kern_full)
        row_table = lax.dynamic_slice_in_dim(interp_matrix(grid, 7), seq_place * rows, rows, 0)
        place, pos_back = jax.vjp(partial(grid_resize, row_table=row_table, grid=grid), pos_full)
        embed = jnp.dot(flat, resized.astype(bf16), preferred_element_type=jnp.float32)
        embed = embed.reshape(images, rows * grid, -1) + place.reshape(1, rows * grid, -1)
        embeds.append(embed.reshape(images * rows * grid, -1))
        flats.append(flat)
        kern_backs.append(kern_back)
        pos_backs.append(pos_back)
        layouts.append((start, start + images * rows * grid, images, rows * grid, grid * grid))
        start = start + images * rows * grid
    x0 = jnp.concatenate(embeds, 0)
    h1_full, norm1_back = jax.vjp(layer_norm, x0, gain_full[0])
    h1 = h1_full.astype(bf16)
    qkv = jnp.dot(h1, w_qkv, preferred_element_type=jnp.float32).astype(bf16)
    width = qkv.shape[1] // 3
    local_kv = qkv[:, width:]
    blocks = [local_kv]
    moving = local_kv
    for turn in range(1, seq_count):
        moving = from_behind(moving, "seq", 1)
        blocks.append(moving)
    all_kv = jnp.stack(blocks, 0)
    mixed_parts, saved = ([], [])
    for first_row, last_row, images, length, whole in layouts:
        query = qkv[first_row:last_row, :width].reshape(images, length, HEADS, HEAD_DIM)
        remote = all_kv[:, first_row:last_row].reshape(
            seq_count, images, length, 2, HEADS, HEAD_DIM
        )
        remote = remote.transpose(1, 0, 2, 3, 4, 5).reshape(
            images, seq_count * length, 2, HEADS, HEAD_DIM
        )
        keys, values = (remote[:, :, 0], remote[:, :, 1])
        attended, norm_log = attend(query, keys, values)
        mixed_parts.append(attended.reshape(last_row - first_row, width))
        saved.append((query, keys, values, norm_log))
    mixed = jnp.concatenate(mixed_parts, 0).astype(bf16)
    x1 = x0 + jnp.dot(mixed, w_out, preferred_element_type=jnp.float32)
    h2_full, norm2_back = jax.vjp(layer_norm, x1, gain_full[1])
    h2 = h2_full.astype(bf16)
    inner = jnp.dot(h2, w_mlp[0], preferred_element_type=jnp.float32)
    act_full, gelu_back = jax.vjp(partial(jax.nn.gelu, approximate=False), inner)
    act = act_full.astype(bf16)
    x2 = x1 + lax.dot_general(act, w_mlp[1], COLS_DIM, preferred_element_type=jnp.float32)
    sum_a = x2[layouts[0][0] : layouts[0][1]].reshape(layouts[0][2], layouts[0][3], -1).sum(1)
    sum_b = x2[layouts[1][0] : layouts[1][1]].reshape(layouts[1][2], layouts[1][3], -1).sum(1)
    pooled_sums = lax.psum((sum_a, sum_b), "seq")
    stats, head_parts = ([], [])
    for index in range(2):
        labels, live = (size_sets[index][1], size_sets[index][2])
        pooled_low = (pooled_sums[index] / float(layouts[index][4])).astype(bf16)
        logits = jnp.dot(pooled_low, w_head, preferred_element_type=jnp.float32)
        norm_log = jax.nn.logsumexp(logits, -1)
        hot = (labels[:, None] == jnp.arange(logits.shape[1], dtype=jnp.int32)[None, :]).astype(
            jnp.float32
        )
        true_logit = jnp.sum(hot * logits, -1)
        alive = live.astype(jnp.float32)
        stats.append(jnp.stack([jnp.sum(alive * (norm_log - true_logit)), jnp.sum(alive)]))
        head_parts.append((pooled_low, jnp.exp(logits - norm_log[:, None]) - hot, alive))
    stats_a, stats_b = lax.psum((stats[0], stats[1]), "dp")
    total = jnp.maximum(stats_a[1] + stats_b[1], 1.0)
    grad_head = jnp.zeros(w_head.shape, jnp.float32)
    d_x2_parts = []
    for index in range(2):
        pooled_low, soft_minus, alive = head_parts[index]
        d_logits = (soft_minus * alive[:, None] / total).astype(bf16)
        grad_head = grad_head + lax.dot_general(
            pooled_low, d_logits, ROWS_DIM, preferred_element_type=jnp.float32
        )
        d_pooled = lax.dot_general(d_logits, w_head, COLS_DIM, preferred_element_type=jnp.float32)
        images, length, whole = (layouts[index][2], layouts[index][3], layouts[index][4])
        spread = jnp.broadcast_to(
            (d_pooled / float(whole))[:, None, :], (images, length, d_pooled.shape[1])
        )
        d_x2_parts.append(spread.reshape(images * length, -1))
    d_x2 = jnp.concatenate(d_x2_parts, 0)
    d_mix = d_x2.astype(bf16)
    grad_down = lax.dot_general(d_mix, act, ROWS_DIM, preferred_element_type=jnp.float32)
    d_act = jnp.dot(d_mix, w_mlp[1], preferred_element_type=jnp.float32)
    d_inner = gelu_back(d_act)[0].astype(bf16)
    grad_up = lax.dot_general(h2, d_inner, ROWS_DIM, preferred_element_type=jnp.float32)
    d_h2 = lax.dot_general(d_inner, w_mlp[0], COLS_DIM, preferred_element_type=jnp.float32)
    d_x1_norm, grad_gain2 = norm2_back(d_h2)
    d_x1 = d_x2 + d_x1_norm
    d_attn = d_x1.astype(bf16)
    grad_out = lax.dot_general(mixed, d_attn, ROWS_DIM, preferred_element_type=jnp.float32)
    d_mixed = lax.dot_general(d_attn, w_out, COLS_DIM, preferred_element_type=jnp.float32).astype(
        bf16
    )
    d_query_parts, d_kv_parts = ([], [])
    for index in range(2):
        first_row, last_row, images, length, whole = layouts[index]
        query, keys, values, norm_log = saved[index]
        d_out = d_mixed[first_row:last_row].reshape(images, length, HEADS, HEAD_DIM)
        d_query, d_keys, d_values = attend_back(query, keys, values, norm_log, d_out)
        d_query_parts.append(d_query.reshape(last_row - first_row, width))
        paired = jnp.stack([d_keys, d_values], 2).reshape(images, seq_count, length, 2 * width)
        d_kv_parts.append(
            paired.transpose(1, 0, 2, 3).reshape(seq_count, last_row - first_row, 2 * width)
        )
    d_all = jnp.concatenate(d_kv_parts, 1)
    mine_kv = d_all[1 % seq_count]
    for turn in range(1, seq_count):
        mine_kv = (
            from_behind(mine_kv.astype(jnp.bfloat16), "seq", 1).astype(mine_kv.dtype)
            + d_all[(turn + 1) % seq_count]
        )
    d_qkv = jnp.concatenate([jnp.concatenate(d_query_parts, 0), mine_kv], 1).astype(bf16)
    grad_qkv = lax.dot_general(h1, d_qkv, ROWS_DIM, preferred_element_type=jnp.float32)
    d_h1 = lax.dot_general(d_qkv, w_qkv, COLS_DIM, preferred_element_type=jnp.float32)
    d_x0_norm, grad_gain1 = norm1_back(d_h1)
    d_x0 = d_x1 + d_x0_norm
    grad_kern = jnp.zeros(kern_full.shape, jnp.float32)
    grad_pos = jnp.zeros(pos_full.shape, jnp.float32)
    for index in range(2):
        first_row, last_row, images, length, whole = layouts[index]
        d_rows = d_x0[first_row:last_row]
        d_kernel = lax.dot_general(
            flats[index], d_rows.astype(bf16), ROWS_DIM, preferred_element_type=jnp.float32
        )
        grad_kern = grad_kern + kern_backs[index](d_kernel)[0]
        d_place = d_rows.reshape(images, length, -1).sum(0)
        grad_pos = grad_pos + pos_backs[index](d_place.reshape(grid_shape(size_sets, index)))[0]
    grad_mlp = jnp.stack([grad_up, grad_down], 0)
    grad_gain = jnp.stack([grad_gain1, grad_gain2], 0)
    grad_head = grad_head / float(seq_count)
    owned = (
        lax.psum_scatter(grad_qkv, ("dp", "seq"), scatter_dimension=0, tiled=True),
        lax.psum_scatter(grad_out, ("dp", "seq"), scatter_dimension=0, tiled=True),
        lax.psum_scatter(grad_mlp, ("dp", "seq"), scatter_dimension=1, tiled=True),
        lax.psum_scatter(grad_kern, ("dp", "seq"), scatter_dimension=0, tiled=True),
        lax.psum_scatter(grad_pos, ("dp", "seq"), scatter_dimension=1, tiled=True),
        lax.psum_scatter(grad_head, ("dp", "seq"), scatter_dimension=0, tiled=True),
        lax.psum_scatter(grad_gain, ("dp", "seq"), scatter_dimension=1, tiled=True),
    )
    square_sum = sum((jnp.sum(piece * piece) for piece in owned))
    grad_norm = jnp.sqrt(lax.psum(square_sum, ("dp", "seq")))
    factor = jnp.minimum(1.0, CLIP / (grad_norm + 1e-06))
    done = [adamw(masters[i], firsts[i], seconds[i], owned[i] * factor, RATES[i]) for i in range(7)]
    size_stats = jnp.stack(
        [stats_a[0] / jnp.maximum(stats_a[1], 1.0), stats_b[0] / jnp.maximum(stats_b[1], 1.0)]
    )
    return (
        done[0][0],
        done[1][0],
        done[2][0],
        done[3][0],
        done[4][0],
        done[5][0],
        done[6][0],
        done[0][1],
        done[1][1],
        done[2][1],
        done[3][1],
        done[4][1],
        done[5][1],
        done[6][1],
        done[0][2],
        done[1][2],
        done[2][2],
        done[3][2],
        done[4][2],
        done[5][2],
        done[6][2],
        size_stats,
        grad_norm,
    )


def specs(row, col):
    both = (*row, *col)
    owned = (
        P(both, None), P(both, None), P(None, both, None), P(both, None), P(None, both),
        P(both, None), P(None, both),
    )
    images = P(row, col, None, None)
    return (images, images, P(row), P(row), P(row), P(row), *owned * 3), (*owned * 3, P(), P())


def solution(mesh):
    dp, seq = mesh.shape["dp"], mesh.shape["seq"]

    def run(*args):
        if fits_fast(mesh, args[0], args[1]):
            split = Mesh(mesh.devices.reshape(4, dp // 8, 2, seq), AXES)
            placed, given = specs(AXES[:3], AXES[3:])
            step = jax.shard_map(
                fast_on_device, mesh=split, in_specs=placed, out_specs=given, check_vma=False
            )
        else:
            placed, given = specs(("dp",), ("seq",))
            step = jax.shard_map(
                on_device, mesh=mesh, in_specs=placed, out_specs=given, check_vma=False
            )
        return step(*args)

    return run
```
